128 devices in a mesh: ctx: 8 (over y, z_hi), fsdp: 16 (over z_lo, x, core).
Axes of the slice: x: 4, y: 4, z: 4 (z_hi: 2, z_lo: 2; z = z_hi * 2 + z_lo), core: 2. Of those that a mesh axis runs over, the one named last changes fastest.
Arguments:
- tokens: bfloat16 [16, 1024, 2048], P('fsdp', 'ctx'), may hold values from -6 to 6
- cotangent: bfloat16 [16, 1024, 2048], P('fsdp', 'ctx'), may hold values from -6 to 6
- w_qkv: bfloat16 [2048, 6144], P(('ctx', 'fsdp')), may hold values from -0.125 to 0.125
- w_out: bfloat16 [2048, 2048], P(('ctx', 'fsdp')), may hold values from -0.5 to 0.5
- w_router: bfloat16 [2048, 16], P(('ctx', 'fsdp')), may hold values from -0.0625 to 0.0625
- norm_attn: bfloat16 [2048], P(('ctx', 'fsdp')), may hold values from 0.099609375 to 1.8984375
- norm_moe: bfloat16 [2048], P(('ctx', 'fsdp')), may hold values from 0.099609375 to 1.8984375
- query_gain: bfloat16 [2048], P(('ctx', 'fsdp')), may hold values from 0.796875 to 2
- key_gain: bfloat16 [2048], P(('ctx', 'fsdp')), may hold values from 0.796875 to 2
- w_gate_up: bfloat16 [16, 2048, 2048], P('ctx', 'fsdp'), may hold values from -0.125 to 0.125
- w_down: bfloat16 [16, 1024, 2048], P('ctx', None, 'fsdp'), may hold values from -0.5 to 0.5
- routes: int32 [16, 1024, 4], P('fsdp'), may hold values from 0 to 15, all different within a row; in each aligned block of 1024 rows (0 to 1023, 1024 to 2047, ..., all dimensions but the last counted through in order) at most 384 rows name the same one
- block_order: int32 [16, 8], P('fsdp', 'ctx'), may hold values from 0 to 7, each once within a row
Outputs:
- layer_output: bfloat16 [16, 1024, 2048], P('fsdp', 'ctx')
- grad_tokens: bfloat16 [16, 1024, 2048], P('fsdp', 'ctx')
- grad_w_qkv: float32 [2048, 6144], P(('ctx', 'fsdp'))
- grad_w_out: float32 [2048, 2048], P(('ctx', 'fsdp'))
- grad_w_router: float32 [2048, 16], P(('ctx', 'fsdp'))
- grad_norm_attn: float32 [2048], P(('ctx', 'fsdp'))
- grad_norm_moe: float32 [2048], P(('ctx', 'fsdp'))
- grad_query_gain: float32 [2048], P(('ctx', 'fsdp'))
- grad_key_gain: float32 [2048], P(('ctx', 'fsdp'))
- grad_w_gate_up: float32 [16, 2048, 2048], P('ctx', 'fsdp')
- grad_w_down: float32 [16, 1024, 2048], P('ctx', None, 'fsdp')
The draws below stay inside these ranges and needn't reach their ends.
Inputs may be any that keep to these rules, and one draw needn't show every extreme that they name: `routes`: each row names 4 different experts. In each sequence no expert is named by more than 384 rows, and some sequence has an expert named by exactly 384. `block_order`: each sequence's row is a permutation of the block numbers.
All inputs are finite; a program needn't handle non-finite values.
Results may differ from the reference program's by a relative error of at most 0.028.
Values may be sent and summed in bfloat16 or wider, within the bound.
No kernel may reach another device: no remote copies, remote signals or barrier semaphores. Data moves between devices by JAX's collectives and lax.ppermute only.
A program may use at most 384 MiB of HBM per device.

```python
import math
import jax
import jax.numpy as jnp
import numpy as np
from jax import lax

D = 2048
HEADS = 16
HEAD_DIM = 128
FF = 1024
TOP = 4
TOK_DEV = 128
CAP = 384
LEN = 1024
EXPERTS = 16
SEQS = 16
N_CTX = 8


def levels(stream_key, extent, shards, least, high):
    def one(dim, blocks):
        steps = jax.random.uniform(jax.random.fold_in(jax.random.fold_in(stream_key, 6), dim), (blocks,), jnp.float32, least / len(shards), high / len(shards))
        return jnp.repeat(jnp.exp(steps), extent[dim] // blocks).reshape((-1,) + (1,) * (len(extent) - dim - 1))

    loudness = one(*shards[0])
    for cut in shards[1:]:
        loudness = loudness * one(*cut)
    return loudness


def deal_out(stream_key, own, number, rows, count, top, bound, lean):
    sequence = jax.random.permutation(stream_key, count)
    crowded, usual = portions_of(count, rows * top, bound, lean, True), portions_of(count, rows * top, bound, lean, False)
    places = jnp.arange(count)

    def named(lengths, offset_by):
        used = int((lengths > 0).sum())
        fixed = max(1, used // 4)
        shifted = fixed + (places - fixed + offset_by * (used - fixed)) % max(1, count - fixed)
        return jnp.zeros((count,), jnp.int32).at[sequence[jnp.where(places < fixed, places, shifted)]].set(jnp.asarray(lengths, jnp.int32))

    lengths = jnp.where(number % 4 == 0, named(crowded, number // 4), named(usual, number - number // 4 - 1))
    mixed = jax.random.permutation(jax.random.fold_in(own, 3), count)
    donor, sink = mixed[0:count // 2 * 2:2], mixed[1:count // 2 * 2:2]
    margin = jnp.minimum(lengths[donor] - 1, bound - lengths[sink]) // 2
    margin = jnp.where((donor == sequence[0]) | (sink == sequence[0]) | (lengths[sink] == 0), 0, jnp.maximum(margin, 0))
    shifted = jax.random.randint(jax.random.fold_in(own, 4), (count // 2,), 0, 1 << 20) % (margin + 1)
    lengths = lengths.at[donor].add(-shifted).at[sink].add(shifted)
    labels = jnp.searchsorted(jnp.cumsum(lengths), jnp.arange(rows * top), side="right").astype(jnp.int32)
    table = labels.reshape(top, rows).T
    table = table[jax.random.permutation(jax.random.fold_in(own, 1), rows)]
    offset_by = jax.random.randint(jax.random.fold_in(own, 2), (rows, 1), 0, top)
    return jnp.take_along_axis(table, (jnp.arange(top)[None, :] + offset_by) % top, axis=1)


def portions_of(number_of, total, most, skew, full):
    portions = [(1 << 20) // math.isqrt(rank ** skew) + 1 for rank in range(1, number_of + 1)]
    largest = most if full else min(most, max(-(-total // number_of), total * portions[0] // sum(portions)))
    least = 1 if total - largest >= number_of - 1 else 0
    counts, spare = [largest] + [least] * (number_of - 1), total - largest - least * (number_of - 1)
    while spare > 0:
        candidates = [i for i in range(1, number_of) if counts[i] < largest] or [i for i in range(1, number_of) if counts[i] < most]
        mass, budget = sum([portions[i] for i in candidates]), spare
        for i in candidates:
            more = min(most - counts[i], max(1, budget * portions[i] // mass), spare)
            counts[i] = counts[i] + more
            spare = spare - more
    return np.array(counts)


def centred(key, dims, spread, limit, shards=(), held_as=jnp.bfloat16):
    level = levels(key, dims, shards, -0.22, 0.18) if shards else 1.0
    result = jax.random.normal(key, dims, jnp.float32) * spread * level
    return jnp.minimum(jnp.maximum(result, -limit), limit).astype(held_as)


def setup_inputs(seed: int = 0) -> dict:
    key_list = jax.random.split(jax.random.key(seed), 14)
    tokens = centred(key_list[0], (SEQS, LEN, D), 1.0, 6.0, ((0, 16), (1, 8)))
    cotangent = centred(key_list[1], (SEQS, LEN, D), 1.0, 6.0, ((0, 16), (1, 8)))
    w_qkv = centred(key_list[2], (D, 3 * D), D ** -0.5, 0.125, ((0, 128),))
    w_out = centred(key_list[3], (D, D), (D // 16) ** -0.5, 0.5, ((0, 128),))
    w_router = centred(key_list[4], (D, EXPERTS), (4 * D) ** -0.5, 0.0625, ((0, 128),))
    norm_attn = jnp.clip(1.0 + 0.18 * jax.random.normal(key_list[5], (D,), jnp.float32), 0.099609375, 1.8984375).astype(jnp.bfloat16)
    norm_moe = jnp.clip(1.0 + 0.18 * jax.random.normal(key_list[6], (D,), jnp.float32), 0.099609375, 1.8984375).astype(jnp.bfloat16)
    query_gain = jnp.clip(jnp.exp(math.log(2.0) - 0.92020463 * jax.random.uniform(key_list[7], (D,), jnp.float32) ** levels(key_list[7], (D,), ((0, 128),), -0.2, 0.2)), 0.796875, 2.0).astype(jnp.bfloat16)
    key_gain = jnp.clip(jnp.exp(math.log(2.0) - 0.92020463 * jax.random.uniform(key_list[8], (D,), jnp.float32) ** levels(key_list[8], (D,), ((0, 128),), -0.2, 0.2)), 0.796875, 2.0).astype(jnp.bfloat16)
    w_gate_up = centred(key_list[9], (EXPERTS, D, 2 * FF), D ** -0.5, 0.125, ((0, 8), (1, 16)))
    w_down = centred(key_list[10], (EXPERTS, FF, D), (FF // 8) ** -0.5, 0.5, ((0, 8), (2, 16)))
    routes_keys = jax.random.split(jax.random.fold_in(key_list[11], 1), SEQS * LEN // LEN)
    routes_turns = jax.random.permutation(jax.random.fold_in(key_list[11], 3), SEQS * LEN // LEN)
    routes = jax.vmap(lambda own, number: deal_out(jax.random.fold_in(key_list[11], 2), own, number, LEN, EXPERTS, TOP, CAP, 1))(routes_keys, routes_turns).reshape((SEQS, LEN, TOP))
    block_order = jax.vmap(lambda own: jax.random.permutation(own, N_CTX))(jax.random.split(key_list[12], SEQS)).reshape((SEQS, N_CTX)).astype(jnp.int32)
    return {"tokens": tokens, "cotangent": cotangent, "w_qkv": w_qkv, "w_out": w_out, "w_router": w_router, "norm_attn": norm_attn, "norm_moe": norm_moe, "query_gain": query_gain, "key_gain": key_gain, "w_gate_up": w_gate_up, "w_down": w_down, "routes": routes, "block_order": block_order}


epsilon = 1e-06
rope_base = 10000.0
highest = lax.Precision.HIGHEST

@jax.custom_vjp
def low(v):
    return lax.optimization_barrier(v.astype(jnp.bfloat16)).astype(jnp.float32)

@jax.custom_vjp
def low_back(v):
    return v

def low_keep(v):
    return (low(v), None)

def low_pass(kept, grad):
    return (grad,)

def back_keep(v):
    return (v, None)

def back_low(kept, grad):
    return (low(grad),)
low.defvjp(low_keep, low_pass)
low_back.defvjp(back_keep, back_low)

def exact_dot(left_mat, right_mat):
    return jnp.dot(left_mat, right_mat, precision=highest)

def rms_norm(values, norm_gain):
    return values * lax.rsqrt(lax.optimization_barrier(jnp.mean(values * values, axis=-1, keepdims=True)) + epsilon) * norm_gain

def rotate(values, positions):
    half_dim = values.shape[-1] // 2
    frequency = rope_base ** (-2.0 * jnp.arange(half_dim, dtype=jnp.float32) / values.shape[-1])
    angles = positions.astype(jnp.float32)[:, None] * frequency[None, :]
    cosine = jnp.cos(angles)[:, None, :]
    sine_part = jnp.sin(angles)[:, None, :]
    first_half = values[..., :half_dim]
    second = values[..., half_dim:]
    return jnp.concatenate([first_half * cosine - second * sine_part, second * cosine + first_half * sine_part], axis=-1)

def attend_head(head_items):
    queries, key_rows, value_rows = head_items
    scores = low_back(exact_dot(queries, key_rows.T) * HEAD_DIM ** (-0.5))
    weights = jax.nn.softmax(scores, axis=-1)
    return low(low_back(exact_dot(low(weights), value_rows)))

def slot_table(hit_count):
    row_count = hit_count.shape[0]
    slot_rank = (jnp.cumsum(hit_count) - hit_count).astype(jnp.int32)
    places = jnp.where(hit_count > 0, slot_rank, CAP).astype(jnp.int32)
    slot_token = jnp.zeros((CAP + 1,), jnp.int32).at[places].set(jnp.arange(row_count, dtype=jnp.int32))[:CAP]
    live_slot = (jnp.arange(CAP, dtype=jnp.int32) < jnp.sum(hit_count).astype(jnp.int32)).astype(jnp.float32)
    return (slot_token, live_slot)

def expert_apply(normed_two, gate_probs, route_table, expert_index, gate_up_w, down_w):
    chosen = route_table == expert_index
    gate_token = lax.optimization_barrier(jnp.sum(jnp.where(chosen, gate_probs, 0.0), axis=1))
    hit_count = lax.optimization_barrier(jnp.sum(chosen.astype(jnp.int32), axis=1)).astype(jnp.int32)
    slot_token, live_slot = slot_table(hit_count)
    slot_rows = normed_two[slot_token]
    gate_up = low_back(exact_dot(slot_rows, gate_up_w))
    hidden = low(jax.nn.silu(gate_up[:, :FF]) * gate_up[:, FF:])
    expert_out = low_back(exact_dot(hidden, down_w))
    slot_weight = gate_token[slot_token] * live_slot
    return jnp.zeros((LEN, D), jnp.float32).at[slot_token].add(slot_weight[:, None] * expert_out)

def layer(layer_input, weight_list, route_table, positions):
    w_qkv, w_out, w_router, norm_attn, norm_moe, query_gain, key_gain, w_gate_up, w_down = weight_list
    normed_one = low(rms_norm(layer_input, norm_attn))
    qkv_pre = low_back(exact_dot(normed_one, w_qkv))
    queries = rms_norm(qkv_pre[:, :D], query_gain).reshape(LEN, HEADS, HEAD_DIM)
    key_rows = rms_norm(qkv_pre[:, D:2 * D], key_gain).reshape(LEN, HEADS, HEAD_DIM)
    queries = low(rotate(queries, positions))
    key_rows = low(rotate(key_rows, positions))
    value_rows = low(qkv_pre[:, 2 * D:].reshape(LEN, HEADS, HEAD_DIM))
    head_out = lax.map(jax.checkpoint(attend_head), (queries.transpose(1, 0, 2), key_rows.transpose(1, 0, 2), value_rows.transpose(1, 0, 2)))
    attended = head_out.transpose(1, 0, 2).reshape(LEN, D)
    after_attention = layer_input + low_back(exact_dot(attended, w_out))
    normed_two = low(rms_norm(after_attention, norm_moe))
    logits = exact_dot(normed_two, w_router)
    gate_probs = jax.nn.softmax(jnp.take_along_axis(logits, route_table, axis=1), axis=-1)

    def add_expert(running_sum, expert_items):
        expert_index, gate_up_w, down_w = expert_items
        return (running_sum + expert_apply(normed_two, gate_probs, route_table, expert_index, gate_up_w, down_w), None)
    moe_sum, _ = lax.scan(jax.checkpoint(add_expert), jnp.zeros((LEN, D), jnp.float32), (jnp.arange(EXPERTS, dtype=jnp.int32), w_gate_up, w_down))
    return after_attention + moe_sum

def reference(tokens, cotangent, w_qkv, w_out, w_router, norm_attn, norm_moe, query_gain, key_gain, w_gate_up, w_down, routes, block_order):
    weight_list = tuple((arr.astype(jnp.float32) for arr in (w_qkv, w_out, w_router, norm_attn, norm_moe, query_gain, key_gain, w_gate_up, w_down)))

    def one_sequence(grad_totals, seq_items):
        seq_tokens, seq_cot, seq_routes, seq_order = seq_items
        row_ids = jnp.arange(LEN, dtype=jnp.int32)
        positions = (seq_order[row_ids // TOK_DEV] * TOK_DEV + row_ids % TOK_DEV).astype(jnp.int32)

        def forward(layer_input, *weight_args):
            return layer(layer_input, weight_args, seq_routes, positions)
        layer_out, pull_back = jax.vjp(forward, seq_tokens.astype(jnp.float32), *weight_list)
        gradients = pull_back(seq_cot.astype(jnp.float32))
        new_totals = tuple((total_grad + part_grad for total_grad, part_grad in zip(grad_totals, gradients[1:])))
        return (new_totals, (layer_out.astype(jnp.bfloat16), gradients[0].astype(jnp.bfloat16)))
    zero_grads = tuple((jnp.zeros_like(arr) for arr in weight_list))
    grad_totals, (seq_outputs, seq_grads) = lax.scan(one_sequence, zero_grads, (tokens, cotangent, routes, block_order))
    return (seq_outputs, seq_grads) + grad_totals
```

```python
import jax
import jax.numpy as jnp
from jax import lax
from jax.sharding import Mesh, PartitionSpec as P

D = 2048
HALF = 1024
HEAD_DIM = 128
FF = 1024
CAP = 384
ROWS = 128
SCALE = HEAD_DIM**-0.5

epsilon = 1e-06
rope_base = 10000.0


def f32(a):
    return a.astype(jnp.float32)


def bf16(a):
    return a.astype(jnp.bfloat16)


def dot(a, b):
    return jnp.dot(a, b, preferred_element_type=jnp.float32)


def dot_t(a, b):
    return lax.dot_general(a, b, (((1,), (1,)), ((), ())), preferred_element_type=jnp.float32)


def t_dot(a, b):
    return lax.dot_general(a, b, (((0,), (0,)), ((), ())), preferred_element_type=jnp.float32)


def other_core(a):
    return lax.ppermute(a, "c", [(0, 1), (1, 0)])


def from_chip(a, step):
    return lax.ppermute(a, "y", [(i, (i + step) % 4) for i in range(4)])


def y_gather(a):
    return [a] + [from_chip(a, step) for step in (1, 2, 3)]


def y_scatter(parts):
    return [parts[0]] + [from_chip(parts[step], 4 - step) for step in (1, 2, 3)]


def by_distance(a, y):
    place = (y - jnp.arange(4)) % 4
    hit = place[:, None] == jnp.arange(4)[None, :]
    return jnp.sum(jnp.where(hit[None, :, :, None], a[:, None], jnp.zeros((), a.dtype)), axis=2)


def ring_sum(a, y):
    n = a.shape[0]
    a = a + other_core(a)
    a = by_distance(a.reshape(n, 4, 256), y)
    a = a + from_chip(a, 1) + from_chip(a, 2) + from_chip(a, 3)
    return by_distance(a, y).reshape(n, 1024)


def split_halves(a):
    lead = a.shape[:-1]
    pairs = a.reshape(*lead, a.shape[-1] // 256, 2, 128)
    return pairs[..., 0, :].reshape(*lead, -1), pairs[..., 1, :].reshape(*lead, -1)


def join_halves(low, high):
    lead = low.shape[:-1]
    pairs = jnp.stack([low.reshape(*lead, -1, 128), high.reshape(*lead, -1, 128)], axis=-2)
    return pairs.reshape(*lead, -1)


def swap(a, k):
    return lax.ppermute(
        a, ("zh", "c"), [(zh * 2 + c, c * 2 + (zh ^ k)) for zh in range(2) for c in range(2)]
    )


def swap_back(a, k):
    return lax.ppermute(
        a, ("zh", "c"), [(c * 2 + (zh ^ k), zh * 2 + c) for zh in range(2) for c in range(2)]
    )


def to_half(low, high, zh, c):
    got = [swap(jnp.where((zh ^ k) == 0, low, high), k) for k in range(2)]
    return jnp.where(c == 0, got[0], got[1]), jnp.where(c == 0, got[1], got[0])


def from_half(a, zh, c):
    first, second = a[:ROWS], a[ROWS:]
    got = [swap_back(jnp.where((c ^ k) == 0, first, second), k) for k in range(2)]
    low = jnp.where(zh == 0, got[0], got[1])
    high = jnp.where(zh == 0, got[1], got[0])
    return join_halves(low, high)


def turn(values, cosine, sine):
    first, second = values[..., :64], values[..., 64:]
    return jnp.concatenate(
        [first * cosine - second * sine, second * cosine + first * sine], axis=-1
    )


def on_device(
    tokens,
    cotangent,
    w_qkv,
    w_out,
    w_router,
    norm_attn,
    norm_moe,
    query_gain,
    key_gain,
    w_gate_up,
    w_down,
    routes,
    block_order,
):
    y, zh, c = lax.axis_index("y"), lax.axis_index("zh"), lax.axis_index("c")
    plane = ("zh", "zl", "x")
    own_first = c == 0

    low, high = split_halves(tokens[0])
    place = jnp.full((16, HALF), block_order[0, 0], jnp.int32).astype(jnp.bfloat16)
    block_0, block_1 = to_half(
        jnp.concatenate([low, place]), jnp.concatenate([high, place]), zh, c
    )
    packed = jnp.stack(y_gather(jnp.stack([block_0, block_1])))
    x_own = packed[:, :, :ROWS].reshape(1024, HALF)
    positions = f32(packed[:, :, ROWS, 0]).reshape(8, 1) * ROWS + jnp.arange(ROWS, dtype=jnp.float32)
    positions = positions.reshape(1024)
    x_par = other_core(x_own)

    pieces = w_qkv.reshape(16, 3, 8, 256).transpose(2, 0, 1, 3).reshape(8, 16, 768)
    small = jnp.concatenate(
        [norm_attn[:, None], norm_moe[:, None], w_router, query_gain[:, None], key_gain[:, None]],
        axis=1,
    )
    small = jnp.pad(small, ((0, 0), (0, 108)))
    pieces = jnp.concatenate([pieces, jnp.broadcast_to(small, (8, 16, 128))], axis=2)
    pieces = lax.all_to_all(pieces, ("y", "c"), 0, 0, tiled=True).reshape(128, 896)
    out_low, out_high = split_halves(w_out)
    out_par = other_core(jnp.where(own_first, out_high, out_low))
    out_own = jnp.where(own_first, out_low, out_high)
    out_both = jnp.where(
        own_first, jnp.concatenate([out_own, out_par]), jnp.concatenate([out_par, out_own])
    )
    out_both = out_both.reshape(32, 4, 256).transpose(1, 0, 2).reshape(128, 256)
    dense = lax.all_gather(
        jnp.concatenate([pieces, out_both], axis=1), plane, axis=0, tiled=True
    ).reshape(2, 2, 4, 4, 2, 16, 1152)

    down_t = w_down.transpose(0, 2, 1)
    expert_w = [
        lax.all_gather(
            jnp.concatenate([w_gate_up[m], down_t[m]], axis=1), plane, axis=0, tiled=True
        ).reshape(2, HALF, 3072)
        for m in range(2)
    ]

    cot_low, cot_high = split_halves(cotangent[0])
    cot_here = jnp.concatenate(to_half(cot_low, cot_high, zh, c))
    cot_all = jnp.concatenate(y_gather(cot_here))
    route_t = routes[0].T
    route_t = jnp.where(c == zh, route_t, other_core(route_t))
    route_t = by_distance(route_t.reshape(4, 4, 256), y).reshape(4, 1024)

    def rolled(a):
        a = a.transpose(1, 3, 0, 2, 4, 5, 6).reshape(2, HALF, -1)
        return jnp.where(own_first, a, a[::-1])

    qkv_w = rolled(dense[..., :768]).reshape(D, 768)
    small_all = dense[..., 768:788]
    small_rolled = f32(rolled(small_all))
    gain_attn = small_rolled[:, :, 0].reshape(D)
    gain_moe = small_rolled[0, :, 1]
    router_w = bf16(small_rolled[0, :, 2:18])
    small_true = f32(small_all[..., 18:20].transpose(3, 0, 1, 2, 4, 5, 6).reshape(8, 256, 2))
    head_block = y * 2 + c
    mine = lax.dynamic_index_in_dim(small_true, head_block, 0, keepdims=False)
    gain_query, gain_key = mine[:, 0], mine[:, 1]
    out_w = (
        dense[..., 896:1152].reshape(2, 2, 4, 4, 2, 16, 256)
        if False
        else dense.reshape(16, 128, 1152)[:, :, 896:]
        .reshape(16, 4, 32, 256)
        .transpose(0, 2, 1, 3)
        .reshape(2, 256, HALF)
    )
    out_w = jnp.where(own_first, out_w, out_w[::-1]).reshape(512, HALF)

    x_all = f32(jnp.concatenate([x_own, x_par], axis=1))
    rstd_one = lax.rsqrt(jnp.mean(x_all * x_all, axis=1, keepdims=True) + epsilon)
    x_hat = x_all * rstd_one
    normed_one = bf16(x_hat * gain_attn)
    qkv = dot(normed_one, qkv_w)
    query_pre, key_pre = qkv[:, :256], qkv[:, 256:512]
    squares = jnp.stack([jnp.sum(query_pre * query_pre, axis=1), jnp.sum(key_pre * key_pre, axis=1)])
    rstd = lax.rsqrt(ring_sum(squares, y) / D + epsilon)
    rstd_q, rstd_k = rstd[0][:, None], rstd[1][:, None]
    frequency = rope_base ** (-2.0 * jnp.arange(64, dtype=jnp.float32) / HEAD_DIM)
    angles = positions[:, None] * frequency[None, :]
    cosine, sine = jnp.cos(angles)[:, None, :], jnp.sin(angles)[:, None, :]
    query = bf16(turn((query_pre * rstd_q * gain_query).reshape(1024, 2, 128), cosine, sine))
    key = bf16(turn((key_pre * rstd_k * gain_key).reshape(1024, 2, 128), cosine, sine))
    value = bf16(qkv[:, 512:]).reshape(1024, 2, 128)
    scores = jnp.einsum("thd,shd->hts", query, key, preferred_element_type=jnp.float32) * SCALE
    row_max = jnp.max(scores, axis=-1, keepdims=True)
    exp_scores = jnp.exp(scores - row_max)
    probs = exp_scores / jnp.sum(exp_scores, axis=-1, keepdims=True)
    probs_low = bf16(probs)
    attended = jnp.einsum("hts,shd->thd", probs_low, value, preferred_element_type=jnp.float32)
    attended = bf16(attended.reshape(1024, 256))
    attended = jnp.concatenate([attended, other_core(attended)], axis=1)
    out_part = dot(attended, out_w).reshape(4, 256, HALF)
    got = y_scatter([out_part[0]] + [bf16(out_part[s]) for s in (1, 2, 3)])
    x_here = f32(x_own[:256])
    after = x_here + sum(f32(g) for g in got)

    square = jnp.sum(after * after, axis=1)
    rstd_two = lax.rsqrt((square + other_core(square)) / D + epsilon)[:, None]
    after_hat = after * rstd_two
    normed_two = bf16(after_hat * gain_moe)
    normed_all = jnp.concatenate(y_gather(normed_two))
    logits = lax.dot_general(
        router_w, normed_all, (((0,), (1,)), ((), ())), preferred_element_type=jnp.float32
    )
    logits = logits + other_core(logits)
    picked = route_t[:, None, :] == jnp.arange(16, dtype=jnp.int32)[None, :, None]
    gates = jax.nn.softmax(jnp.sum(jnp.where(picked, logits[None], 0.0), axis=1), axis=0)

    moe_sum = jnp.zeros((1024, HALF), jnp.float32)
    d_normed = jnp.zeros((1024, HALF), jnp.float32)
    d_gates = jnp.zeros((4, 1024), jnp.float32)
    slots = jnp.arange(CAP, dtype=jnp.int32)
    expert_grads = []
    for m in range(2):
        grads = []
        for h in range(2):
            chosen = route_t == y * 4 + h * 2 + m
            hit = jnp.sum(chosen.astype(jnp.int32), axis=0)
            rank = jnp.cumsum(hit) - hit
            seat = jnp.where(hit > 0, rank, CAP)
            taken = slots[:, None] == seat[None, :]
            pick = taken.astype(jnp.bfloat16)
            gate_token = jnp.sum(jnp.where(chosen, gates, 0.0), axis=0)
            slot_weight = jnp.sum(jnp.where(taken, gate_token[None, :], 0.0), axis=1)[:, None]
            gate_up_w, down_w = expert_w[m][h, :, : 2 * FF], expert_w[m][h, :, 2 * FF :]
            slot_rows = bf16(dot(pick, normed_all))
            cot_rows = dot(pick, cot_all)
            d_out = bf16(slot_weight * cot_rows)
            part = jnp.concatenate([dot(slot_rows, gate_up_w), dot(d_out, down_w)], axis=1)
            part = part + f32(other_core(bf16(part)))
            gate, up, d_hidden = part[:, :FF], part[:, FF : 2 * FF], part[:, 2 * FF :]
            sig = jax.nn.sigmoid(gate)
            hidden = bf16(gate * sig * up)
            expert_out = dot_t(hidden, down_w)
            d_weight = jnp.sum(expert_out * cot_rows, axis=1)
            d_token = jnp.sum(jnp.where(taken, d_weight[:, None], 0.0), axis=0)
            d_gates = d_gates + jnp.where(chosen, d_token[None], 0.0)
            moe_sum = moe_sum + t_dot(pick, bf16(slot_weight * expert_out))
            d_gate = d_hidden * up * sig * (1.0 + gate * (1.0 - sig))
            d_gate_up = bf16(jnp.concatenate([d_gate, d_hidden * gate * sig], axis=1))
            d_normed = d_normed + t_dot(pick, bf16(dot_t(d_gate_up, gate_up_w)))
            grads.append(
                jnp.concatenate(
                    [bf16(t_dot(slot_rows, d_gate_up)), bf16(t_dot(d_out, hidden))], axis=1
                )
            )
        expert_grads.append(
            lax.psum_scatter(jnp.concatenate(grads), plane, scatter_dimension=0, tiled=True)
        )

    def ring_scatter(a):
        a = bf16(a).reshape(4, 256, HALF)
        return sum(f32(g) for g in y_scatter([a[s] for s in range(4)]))

    layer_output = bf16(after + ring_scatter(moe_sum))
    d_normed_here = ring_scatter(d_normed)
    d_gates = d_gates.reshape(4, 4, 256)
    d_gates = sum(y_scatter([d_gates[:, s] for s in range(4)]))
    d_gates = d_gates + other_core(d_gates)

    gates_here, picked_here = gates[:, :256], picked[:, :, :256]
    d_routed = gates_here * (d_gates - jnp.sum(gates_here * d_gates, axis=0, keepdims=True))
    d_logits = jnp.sum(jnp.where(picked_here, d_routed[:, None, :], 0.0), axis=0)
    grad_router = lax.dot_general(
        f32(normed_two), d_logits, (((0,), (1,)), ((), ())), preferred_element_type=jnp.float32
    )
    d_normed_here = d_normed_here + lax.dot_general(
        d_logits, f32(router_w), (((0,), (1,)), ((), ())), preferred_element_type=jnp.float32
    )
    grad_norm_moe = jnp.sum(d_normed_here * after_hat, axis=0)
    d_scaled = d_normed_here * gain_moe
    along = jnp.sum(d_scaled * after_hat, axis=1)
    along = (along + other_core(along))[:, None] / D
    d_after = f32(cot_here) + rstd_two * (d_scaled - after_hat * along)

    d_attn = jnp.concatenate(y_gather(bf16(d_after)))
    grad_out = t_dot(attended, d_attn)
    d_att = dot_t(d_attn, out_w)
    d_att = bf16(d_att[:, :256] + other_core(d_att[:, 256:])).reshape(1024, 2, 128)
    d_probs = jnp.einsum("thd,shd->hts", d_att, value, preferred_element_type=jnp.float32)
    d_scores = bf16(probs * (d_probs - jnp.sum(probs * d_probs, axis=-1, keepdims=True)))
    d_value = jnp.einsum("hts,thd->shd", probs_low, d_att, preferred_element_type=jnp.float32)
    d_key = jnp.einsum("hts,thd->shd", d_scores, query, preferred_element_type=jnp.float32)
    d_query = jnp.einsum("hts,shd->thd", d_scores, key, preferred_element_type=jnp.float32)
    d_query = turn(d_query * SCALE, cosine, -sine).reshape(1024, 256)
    d_key = turn(d_key * SCALE, cosine, -sine).reshape(1024, 256)
    query_hat, key_hat = query_pre * rstd_q, key_pre * rstd_k
    grad_query_gain = jnp.sum(d_query * query_hat, axis=0)
    grad_key_gain = jnp.sum(d_key * key_hat, axis=0)
    d_query, d_key = d_query * gain_query, d_key * gain_key
    along = jnp.stack([jnp.sum(d_query * query_hat, axis=1), jnp.sum(d_key * key_hat, axis=1)])
    along = ring_sum(along, y)[:, :, None] / D
    d_query = rstd_q * (d_query - query_hat * along[0])
    d_key = rstd_k * (d_key - key_hat * along[1])
    d_qkv = jnp.concatenate([bf16(d_query), bf16(d_key), bf16(d_value.reshape(1024, 256))], axis=1)
    grad_qkv = t_dot(normed_one, d_qkv)
    d_normed_one = dot_t(d_qkv, qkv_w)
    grad_norm_attn = jnp.sum(d_normed_one * x_hat, axis=0)
    d_normed_one = d_normed_one[:, :HALF] + f32(other_core(bf16(d_normed_one[:, HALF:])))
    d_normed_one = ring_scatter(d_normed_one) * gain_attn[:HALF]
    hat_here = x_hat[:256, :HALF]
    along = jnp.sum(d_normed_one * hat_here, axis=1)
    along = (along + other_core(along))[:, None] / D
    grad_tokens = bf16(d_after + rstd_one[:256] * (d_normed_one - hat_here * along))

    extras = jnp.concatenate(
        [
            grad_norm_attn[:, None],
            jnp.pad(
                jnp.concatenate([grad_norm_moe[:, None], grad_router], axis=1), ((0, HALF), (0, 0))
            ),
        ],
        axis=1,
    )
    both = jnp.concatenate([grad_qkv, extras], axis=1).reshape(2, HALF, 786)
    both = jnp.where(own_first, both, both[::-1]).reshape(2, 4, 2, 4, 2, 16, 786)
    both = both.transpose(2, 0, 3, 1, 4, 5, 6)
    gains = jnp.stack([grad_query_gain, grad_key_gain], axis=1)
    at_home = jnp.arange(8)[:, None, None] == head_block
    gains = jnp.where(at_home, gains[None], 0.0).reshape(4, 2, 2, 4, 2, 16, 2)
    gains = gains.transpose(1, 2, 3, 0, 4, 5, 6)
    both = jnp.concatenate([both, gains], axis=-1)
    both = jnp.pad(both, ((0, 0),) * 6 + ((0, 108),)).reshape(D, 896)
    both = lax.psum_scatter(bf16(both), plane, scatter_dimension=0, tiled=True)
    both = lax.all_to_all(both.reshape(8, 16, 896), ("y", "c"), 0, 0, tiled=True)
    both = f32(both)
    grad_w_qkv = both[:, :, :768].reshape(8, 16, 3, 256).transpose(1, 2, 0, 3).reshape(16, 3 * D)
    smalls = jnp.sum(both[:, :, 768:788], axis=0)

    grad_out = grad_out.reshape(2, 256, HALF)
    grad_out = jnp.where(own_first, grad_out, grad_out[::-1]).reshape(512, HALF)
    grad_out = lax.psum_scatter(grad_out, plane, scatter_dimension=0, tiled=True)
    out_own = jnp.where(own_first, grad_out[:16], grad_out[16:])
    out_par = other_core(jnp.where(own_first, grad_out[16:], grad_out[:16]))
    grad_w_out = jnp.where(own_first, join_halves(out_own, out_par), join_halves(out_par, out_own))

    expert_grads = [f32(g) for g in expert_grads]
    grad_gate_up = jnp.stack([g[:, : 2 * FF] for g in expert_grads])
    grad_down = jnp.stack([g[:, 2 * FF :].T for g in expert_grads])
    return (
        from_half(layer_output, zh, c)[None],
        from_half(grad_tokens, zh, c)[None],
        grad_w_qkv,
        grad_w_out,
        smalls[:, 2:18],
        smalls[:, 0],
        smalls[:, 1],
        smalls[:, 18],
        smalls[:, 19],
        grad_gate_up,
        grad_down,
    )


def solution(mesh):
    fine = Mesh(mesh.devices.reshape(4, 2, 2, 4, 2), ("y", "zh", "zl", "x", "c"))
    ctx, fsdp = ("y", "zh"), ("zl", "x", "c")
    rows, blocks, line = P(ctx + fsdp, None), P(fsdp, ctx, None), P(ctx + fsdp)
    gate_up, down = P(ctx, fsdp, None), P(ctx, None, fsdp)
    return jax.shard_map(
        on_device,
        mesh=fine,
        in_specs=(blocks, blocks, rows, rows, rows, line, line, line, line, gate_up, down)
        + (P(fsdp, None, None), P(fsdp, ctx)),
        out_specs=(blocks, blocks, rows, rows, rows, line, line, line, line, gate_up, down),
        check_vma=False,
    )
```

```python
import jax
import jax.numpy as jnp
import numpy as np
from jax import lax
from jax.sharding import Mesh, PartitionSpec as P

D = 2048
HALF = 1024
HEAD_DIM = 128
FF = 1024
CAP = 384
ROWS = 128
SCALE = HEAD_DIM**-0.5

epsilon = 1e-06
rope_base = 10000.0


def f32(a):
    return a.astype(jnp.float32)


def bf16(a):
    return a.astype(jnp.bfloat16)


def dot(a, b):
    return jnp.dot(a, b, preferred_element_type=jnp.float32)


def dot_t(a, b):
    return lax.dot_general(a, b, (((1,), (1,)), ((), ())), preferred_element_type=jnp.float32)


def t_dot(a, b):
    return lax.dot_general(a, b, (((0,), (0,)), ((), ())), preferred_element_type=jnp.float32)


def other_core(a):
    return lax.ppermute(a, "c", [(0, 1), (1, 0)])


def from_chip(a, step):
    return lax.ppermute(a, "y", [(i, (i + step) % 4) for i in range(4)])


def y_gather(a):
    return [a] + [from_chip(a, step) for step in (1, 2, 3)]


def y_scatter(parts):
    return [parts[0]] + [from_chip(parts[step], 4 - step) for step in (1, 2, 3)]


def by_distance(a, y):
    place = (y - jnp.arange(4)) % 4
    hit = place[:, None] == jnp.arange(4)[None, :]
    return jnp.sum(jnp.where(hit[None, :, :, None], a[:, None], jnp.zeros((), a.dtype)), axis=2)


def chosen(a, place):
    hit = place[:, None] == jnp.arange(4)[None, :]
    hit = hit.reshape(4, 4, *[1] * (a.ndim - 1))
    return jnp.sum(jnp.where(hit, a[None], jnp.zeros((), a.dtype)), axis=1)


def trade(pieces, y, c):
    pairs = pieces.reshape(4, 2, *pieces.shape[1:])
    mine = jnp.where(c == 0, pairs[:, 0], pairs[:, 1])
    theirs = jnp.where(c == 0, pairs[:, 1], pairs[:, 0])
    got = other_core(theirs)
    both = jnp.where(c == 0, jnp.stack([mine, got], 1), jnp.stack([got, mine], 1))
    both = chosen(both, (y + jnp.arange(4)) % 4)
    got = jnp.stack([both[0]] + [from_chip(both[step], step) for step in (1, 2, 3)])
    return chosen(got, (y - jnp.arange(4)) % 4).reshape(pieces.shape)


def ring_sum(a, y):
    n = a.shape[0]
    a = a + other_core(a)
    a = by_distance(a.reshape(n, 4, 256), y)
    a = a + from_chip(a, 1) + from_chip(a, 2) + from_chip(a, 3)
    return by_distance(a, y).reshape(n, 1024)


def angle_tables():
    frequency = rope_base ** (-2.0 * np.arange(64) / HEAD_DIM)
    blocks = np.arange(8)[:, None] * ROWS * frequency[None]
    rows = np.arange(ROWS)[:, None] * frequency[None]
    tables = (np.cos(blocks), np.sin(blocks), np.cos(rows), np.sin(rows))
    return [jnp.asarray(table, jnp.float32) for table in tables]


def split_halves(a):
    blocks = [a[..., k * 128 : k * 128 + 128] for k in range(a.shape[-1] // 128)]
    return jnp.concatenate(blocks[0::2], axis=-1), jnp.concatenate(blocks[1::2], axis=-1)


def join_halves(low, high):
    blocks = []
    for k in range(low.shape[-1] // 128):
        blocks += [low[..., k * 128 : k * 128 + 128], high[..., k * 128 : k * 128 + 128]]
    return jnp.concatenate(blocks, axis=-1)


def other_layer(a):
    return lax.ppermute(a, "zh", [(0, 1), (1, 0)])


def to_half(low, high, zh, c):
    mine = jnp.where(c == 0, low, high)
    got = other_core(jnp.where(c == 0, high, low))
    keep = jnp.where(zh == c, mine, got)
    got = other_layer(jnp.where(zh == c, got, mine))
    return jnp.where(zh == 0, keep, got), jnp.where(zh == 0, got, keep)


def from_half(a, zh, c):
    first, second = a[:ROWS], a[ROWS:]
    mine = jnp.where(zh == 0, first, second)
    got = other_layer(jnp.where(zh == 0, second, first))
    keep = jnp.where(zh == c, mine, got)
    got = other_core(jnp.where(zh == c, got, mine))
    return join_halves(jnp.where(c == 0, keep, got), jnp.where(c == 0, got, keep))


def turn(values, cosine, sine):
    out = []
    for at in (0, 128):
        first, second = values[:, at : at + 64], values[:, at + 64 : at + 128]
        out += [first * cosine - second * sine, second * cosine + first * sine]
    return jnp.concatenate(out, axis=1)


def heads_of(a):
    return a.reshape(1024, 2, 128)


def attend(query, key, value):
    scores = jnp.einsum(
        "thd,shd->hts", heads_of(query), heads_of(key), preferred_element_type=jnp.float32
    )
    scores = scores * SCALE
    weights = jnp.exp(scores - jnp.max(scores, axis=-1, keepdims=True))
    probs = weights / jnp.sum(weights, axis=-1, keepdims=True)
    attended = jnp.einsum(
        "hts,shd->thd", bf16(probs), heads_of(value), preferred_element_type=jnp.float32
    )
    return bf16(attended.reshape(1024, 256)), probs


def attend_back(d_att, query, key, value, probs):
    d_att, query, key, value = (heads_of(a) for a in (d_att, query, key, value))
    d_probs = jnp.einsum("thd,shd->hts", d_att, value, preferred_element_type=jnp.float32)
    d_scores = bf16(probs * (d_probs - jnp.sum(probs * d_probs, axis=-1, keepdims=True)))
    d_value = jnp.einsum("hts,thd->shd", bf16(probs), d_att, preferred_element_type=jnp.float32)
    d_key = jnp.einsum("hts,thd->shd", d_scores, query, preferred_element_type=jnp.float32)
    d_query = jnp.einsum("hts,shd->thd", d_scores, key, preferred_element_type=jnp.float32)
    return tuple(a.reshape(1024, 256) for a in (d_query * SCALE, d_key * SCALE, d_value))


def per_expert(pattern, a, b):
    return jnp.einsum(pattern, a, b, preferred_element_type=jnp.float32)


def open_experts(seat, gate, normed, cot, weights):
    taken = jnp.arange(CAP, dtype=jnp.int32)[None, :, None] == seat
    pick = taken.astype(jnp.bfloat16)
    weight = jnp.sum(jnp.where(taken, gate, 0.0), axis=2)[:, :, None]
    rows = bf16(per_expert("hst,td->hsd", pick, normed))
    cot_rows = per_expert("hst,td->hsd", pick, cot)
    d_out = bf16(weight * cot_rows)
    part = jnp.concatenate(
        [
            bf16(per_expert("hsd,hdf->hsf", rows, weights[:, :, : 2 * FF])),
            bf16(per_expert("hsd,hdf->hsf", d_out, weights[:, :, 2 * FF :])),
        ],
        axis=2,
    )
    return part, rows, d_out, bf16(cot_rows), pick, taken, weight


def close_experts(own, received, state, weights, before):
    rows, d_out, cot_rows, pick, taken, weight = state
    part = f32(own) + f32(received)
    gate, up, d_hidden = part[:, :, :FF], part[:, :, FF : 2 * FF], part[:, :, 2 * FF :]
    sig = jax.nn.sigmoid(gate)
    hidden = bf16(gate * sig * up)
    out = per_expert("hsf,hdf->hsd", hidden, weights[:, :, 2 * FF :])
    d_weight = jnp.sum(out * f32(cot_rows), axis=2)
    d_token = jnp.sum(jnp.where(taken, d_weight[:, :, None], 0.0), axis=1)
    d_gate = bf16(d_hidden * up * sig * (1.0 + gate * (1.0 - sig)))
    d_gate_up = jnp.concatenate([d_gate, bf16(d_hidden * gate * sig)], axis=2)
    d_rows = bf16(per_expert("hsf,hdf->hsd", d_gate_up, weights[:, :, : 2 * FF]))
    both = jnp.concatenate([bf16(weight * out), d_rows], axis=2)
    pick, both = pick.reshape(2 * CAP, 1024), both.reshape(2 * CAP, 2 * HALF)
    found = t_dot(pick, both)
    if before is not None:
        found = found + before
    return found, (rows, d_out, d_gate_up, hidden), d_token


def expert_products(rows, d_out, d_gate_up, hidden):
    left = jnp.concatenate([rows, d_out], axis=1)
    right = jnp.concatenate(
        [
            jnp.pad(d_gate_up, ((0, 0), (0, 0), (0, FF))),
            jnp.pad(hidden, ((0, 0), (0, 0), (2 * FF, 0))),
        ],
        axis=1,
    )
    return bf16(per_expert("hsd,hsf->hdf", left, right)).reshape(D, 3 * FF)


def on_device(
    tokens,
    cotangent,
    w_qkv,
    w_out,
    w_router,
    norm_attn,
    norm_moe,
    query_gain,
    key_gain,
    w_gate_up,
    w_down,
    routes,
    block_order,
):
    y, zh, c = lax.axis_index("y"), lax.axis_index("zh"), lax.axis_index("c")
    plane = ("zh", "zl", "x")
    own_first = c == 0

    low, high = split_halves(tokens[0])
    low, high, w_qkv = lax.optimization_barrier((low, high, w_qkv))
    x_blocks = jnp.concatenate(to_half(low, high, zh, c))
    x_blocks, block_order, w_gate_up, cotangent, routes = lax.optimization_barrier(
        (x_blocks, block_order, w_gate_up, cotangent, routes)
    )
    x_own = y_gather(x_blocks)
    x_par = [other_core(part) for part in x_own]
    place = jnp.full((8, 128), block_order[0, 0], jnp.int32).astype(jnp.float32)
    places = y_gather(jnp.stack(to_half(place, place, zh, c)))
    places = jnp.stack(places)[:, :, 0, 0].reshape(8)

    pieces = w_qkv.reshape(16, 3, 8, 256).transpose(2, 0, 1, 3).reshape(8, 16, 768)
    small = jnp.concatenate(
        [norm_attn[:, None], norm_moe[:, None], w_router, query_gain[:, None], key_gain[:, None]],
        axis=1,
    )
    small = jnp.pad(small, ((0, 0), (0, 108)))
    pieces = jnp.concatenate([pieces, jnp.broadcast_to(small, (8, 16, 128))], axis=2)
    pieces = trade(pieces, y, c).reshape(128, 896)
    out_low, out_high = split_halves(w_out)
    out_par = other_core(jnp.where(own_first, out_high, out_low))
    out_own = jnp.where(own_first, out_low, out_high)
    out_both = jnp.where(
        own_first, jnp.concatenate([out_own, out_par]), jnp.concatenate([out_par, out_own])
    )
    out_both = out_both.reshape(32, 4, 256).transpose(1, 0, 2).reshape(128, 256)
    dense = jnp.concatenate([pieces, out_both], axis=1)
    dense, w_gate_up = lax.optimization_barrier((dense, w_gate_up))
    dense = lax.all_gather(dense, plane, axis=0, tiled=True).reshape(2, 2, 4, 4, 2, 16, 1152)

    down_t = w_down.transpose(0, 2, 1)
    expert_w = [
        lax.all_gather(
            jnp.concatenate([w_gate_up[m], down_t[m]], axis=1), plane, axis=0, tiled=True
        ).reshape(2, HALF, 3 * FF)
        for m in range(2)
    ]

    cot_low, cot_high = split_halves(cotangent[0])
    cot_here = jnp.concatenate(to_half(cot_low, cot_high, zh, c))
    cot_sent, x_own = lax.optimization_barrier((cot_here, x_own))
    cot_parts = y_gather(cot_sent)
    route_t = routes[0].T
    route_t = jnp.where(c == zh, route_t, other_core(route_t))
    route_t = by_distance(route_t.reshape(4, 4, 256), y).reshape(4, 1024)

    def rolled(a):
        a = a.transpose(1, 3, 0, 2, 4, 5, 6).reshape(2, HALF, -1)
        return jnp.where(own_first, a, a[::-1])

    qkv_w = rolled(dense[..., :768]).reshape(D, 768)
    small_all = dense[..., 768:788]
    small_rolled = f32(rolled(small_all))
    gain_attn = small_rolled[:, :, 0]
    gain_moe = small_rolled[0, :, 1]
    router_w = bf16(small_rolled[0, :, 2:18])
    small_true = f32(small_all[..., 18:20].transpose(3, 0, 1, 2, 4, 5, 6).reshape(8, 256, 2))
    head_block = y * 2 + c
    mine = lax.dynamic_index_in_dim(small_true, head_block, 0, keepdims=False)
    gain_query, gain_key = mine[:, 0], mine[:, 1]
    out_w = dense.reshape(16, 128, 1152)[:, :, 896:].reshape(16, 4, 32, 256)
    out_w = out_w.transpose(0, 2, 1, 3).reshape(2, 256, HALF)
    out_w = jnp.where(own_first, out_w, out_w[::-1]).reshape(512, HALF)

    x_own_all, x_par_all = f32(jnp.concatenate(x_own)), f32(jnp.concatenate(x_par))
    square = jnp.sum(x_own_all * x_own_all, axis=1) + jnp.sum(x_par_all * x_par_all, axis=1)
    rstd_one = lax.rsqrt(square / D + epsilon)[:, None]
    normed_one = jnp.concatenate(
        [bf16(x_own_all * rstd_one * gain_attn[0]), bf16(x_par_all * rstd_one * gain_attn[1])],
        axis=1,
    )
    qkv = dot(normed_one, qkv_w)
    squares = jnp.stack(
        [
            jnp.sum(qkv[:, :256] * qkv[:, :256], axis=1),
            jnp.sum(qkv[:, 256:512] * qkv[:, 256:512], axis=1),
        ]
    )
    rstd = lax.rsqrt(ring_sum(squares, y) / D + epsilon)
    rstd_q, rstd_k = rstd[0][:, None], rstd[1][:, None]
    here = places[:, None, None] == jnp.arange(8, dtype=jnp.float32)[None, :, None]
    block_cos, block_sin, row_cos, row_sin = angle_tables()
    block_cos = jnp.sum(jnp.where(here, block_cos, 0.0), axis=1)[:, None]
    block_sin = jnp.sum(jnp.where(here, block_sin, 0.0), axis=1)[:, None]
    cosine = block_cos * row_cos - block_sin * row_sin
    sine = block_sin * row_cos + block_cos * row_sin
    cosine, sine = cosine.reshape(1024, 64), sine.reshape(1024, 64)
    qkv, out_w, cosine, sine = lax.optimization_barrier((qkv, out_w, cosine, sine))
    query_hat, key_hat = qkv[:, :256] * rstd_q, qkv[:, 256:512] * rstd_k
    heads = (
        bf16(turn(query_hat * gain_query, cosine, sine)),
        bf16(turn(key_hat * gain_key, cosine, sine)),
        bf16(qkv[:, 512:]),
    )
    attended, probs = attend(*heads)
    attended, cot_parts = lax.optimization_barrier((attended, cot_parts))
    cot_all = jnp.concatenate(cot_parts)
    attended = jnp.concatenate([attended, other_core(attended)], axis=1)
    out_part = dot(attended, out_w).reshape(4, 256, HALF)
    got = y_scatter([out_part[0]] + [bf16(out_part[s]) for s in (1, 2, 3)])
    x_here = f32(x_own[0])
    after = x_here + sum(f32(g) for g in got)

    square = jnp.sum(after * after, axis=1)
    rstd_two = lax.rsqrt((square + other_core(square)) / D + epsilon)[:, None]
    after_hat = after * rstd_two
    normed_two = bf16(after_hat * gain_moe)
    normed_all = jnp.concatenate(y_gather(normed_two))
    logits = lax.dot_general(
        router_w, normed_all, (((0,), (1,)), ((), ())), preferred_element_type=jnp.float32
    )
    logits = logits + other_core(logits)
    picked = route_t[:, None, :] == jnp.arange(16, dtype=jnp.int32)[None, :, None]
    gates = jax.nn.softmax(jnp.sum(jnp.where(picked, logits[None], 0.0), axis=1), axis=0)

    found, d_gates, saved = None, jnp.zeros((4, 1024), jnp.float32), []
    for m in range(2):
        chosen_here = route_t[None] == y * 4 + jnp.arange(2, dtype=jnp.int32)[:, None, None] * 2 + m
        hit = jnp.sum(chosen_here.astype(jnp.int32), axis=1)
        rank = jnp.cumsum(hit, axis=1) - hit
        seat = jnp.where(hit > 0, rank, CAP)[:, None]
        gate_token = jnp.sum(jnp.where(chosen_here, gates[None], 0.0), axis=1)[:, None]
        part, *state = open_experts(seat, gate_token, normed_all, cot_all, expert_w[m])
        found, kept, d_token = close_experts(part, other_core(part), state, expert_w[m], found)
        saved.append(kept)
        d_gates = d_gates + jnp.sum(jnp.where(chosen_here, d_token[:, None], 0.0), axis=0)
    first_grads = expert_products(*saved[0])
    found, first_grads = lax.optimization_barrier((found, first_grads))
    expert_grads = [lax.psum_scatter(first_grads, plane, scatter_dimension=0, tiled=True)]
    moe_sum, d_normed = bf16(found[:, :HALF]), bf16(found[:, HALF:])

    def ring_scatter(a):
        a = a.reshape(4, 256, HALF)
        return sum(f32(g) for g in y_scatter([a[s] for s in range(4)]))

    d_normed_here = ring_scatter(d_normed)
    d_normed_here, kept = lax.optimization_barrier((d_normed_here, saved[1]))
    second_grads = expert_products(*kept)
    d_gates = d_gates.reshape(4, 4, 256)
    d_gates = sum(y_scatter([d_gates[:, s] for s in range(4)]))
    d_gates = d_gates + other_core(d_gates)

    gates_here, picked_here = gates[:, :256], picked[:, :, :256]
    d_routed = gates_here * (d_gates - jnp.sum(gates_here * d_gates, axis=0, keepdims=True))
    d_logits = jnp.sum(jnp.where(picked_here, d_routed[:, None, :], 0.0), axis=0)
    grad_router = lax.dot_general(
        f32(normed_two), d_logits, (((0,), (1,)), ((), ())), preferred_element_type=jnp.float32
    )
    d_through = lax.dot_general(
        d_logits, f32(router_w), (((0,), (1,)), ((), ())), preferred_element_type=jnp.float32
    )
    d_normed_here = d_normed_here + d_through
    grad_norm_moe = jnp.sum(d_normed_here * after_hat, axis=0)
    d_scaled = d_normed_here * gain_moe
    along = jnp.sum(d_scaled * after_hat, axis=1)
    along = (along + other_core(along))[:, None] / D
    d_after = f32(cot_here) + rstd_two * (d_scaled - after_hat * along)

    d_attn = jnp.concatenate(y_gather(bf16(d_after)))
    moe_sum, d_attn = lax.optimization_barrier((moe_sum, d_attn))
    moe_here = ring_scatter(moe_sum)
    d_att = dot_t(d_attn, out_w)
    d_att = bf16(d_att[:, :256] + other_core(d_att[:, 256:]))
    d_att, expert_grads[0], second_grads = lax.optimization_barrier(
        (d_att, expert_grads[0], second_grads)
    )
    expert_grads.append(lax.psum_scatter(second_grads, plane, scatter_dimension=0, tiled=True))
    d_query, d_key, d_value = attend_back(d_att, *heads, probs)
    d_query, d_key = turn(d_query, cosine, -sine), turn(d_key, cosine, -sine)
    d_query, d_attn = lax.optimization_barrier((d_query, d_attn))
    grad_out = t_dot(attended, d_attn)
    grad_query_gain = jnp.sum(d_query * query_hat, axis=0)
    grad_key_gain = jnp.sum(d_key * key_hat, axis=0)
    along = jnp.stack(
        [
            jnp.sum(d_query * gain_query * query_hat, axis=1),
            jnp.sum(d_key * gain_key * key_hat, axis=1),
        ]
    )
    along = ring_sum(along, y)[:, :, None] / D
    along, moe_here = lax.optimization_barrier((along, moe_here))
    d_query = rstd_q * (d_query * gain_query - query_hat * along[0])
    d_key = rstd_k * (d_key * gain_key - key_hat * along[1])
    d_qkv = jnp.concatenate([bf16(d_query), bf16(d_key), bf16(d_value)], axis=1)
    d_par = dot_t(d_qkv, qkv_w[HALF:])
    d_own = dot_t(d_qkv, qkv_w[:HALF])
    grad_norm_attn = jnp.concatenate(
        [
            jnp.sum(d_own * (x_own_all * rstd_one), axis=0),
            jnp.sum(d_par * (x_par_all * rstd_one), axis=0),
        ]
    )
    d_par = bf16(d_par)
    received = other_core(d_par)
    received, d_qkv = lax.optimization_barrier((received, d_qkv))
    d_sent = bf16(d_own + f32(received))
    got = y_scatter([d_sent[s * 256 : s * 256 + 256] for s in range(4)])
    grad_qkv = bf16(t_dot(normed_one, d_qkv))
    got, moe_here = lax.optimization_barrier((got, moe_here))
    layer_output = from_half(bf16(after + moe_here), zh, c)[None]
    d_normed_one = sum(f32(g) for g in got) * gain_attn[0]
    hat_here = x_here * rstd_one[:256]
    along = jnp.sum(d_normed_one * hat_here, axis=1)
    along = (along + other_core(along))[:, None] / D
    grad_tokens = bf16(d_after + rstd_one[:256] * (d_normed_one - hat_here * along))

    wide = jnp.concatenate([grad_norm_moe[:, None], grad_router], axis=1)
    wide = jnp.pad(wide, ((0, HALF), (0, 0)))
    extras = jnp.concatenate([grad_norm_attn[:, None], wide], axis=1).reshape(2, HALF, 18)
    extras = jnp.where(own_first, extras, extras[::-1]).reshape(2, 4, 2, 4, 2, 16, 18)
    gains = jnp.stack([grad_query_gain, grad_key_gain], axis=1)
    at_home = jnp.arange(8)[:, None, None] == head_block
    gains = jnp.where(at_home, gains[None], 0.0).reshape(4, 2, 2, 4, 2, 16, 2)
    extras = jnp.concatenate(
        [extras.transpose(2, 0, 3, 1, 4, 5, 6), gains.transpose(1, 2, 3, 0, 4, 5, 6)], axis=-1
    )
    coarse = bf16(extras)
    extras = jnp.concatenate([coarse, bf16(extras - f32(coarse))], axis=-1)
    extras = jnp.pad(extras, ((0, 0),) * 6 + ((0, 88),))
    both = grad_qkv.reshape(2, HALF, 768)
    both = jnp.where(own_first, both, both[::-1]).reshape(2, 4, 2, 4, 2, 16, 768)
    both = both.transpose(2, 0, 3, 1, 4, 5, 6)
    both = jnp.concatenate([both, extras], axis=-1).reshape(16, 128, 896)
    grad_out = bf16(grad_out).reshape(2, 256, HALF)
    grad_out = jnp.where(own_first, grad_out, grad_out[::-1]).reshape(16, 32, 4, 256)
    grad_out = grad_out.transpose(0, 2, 1, 3).reshape(16, 128, 256)
    both = jnp.concatenate([both, grad_out], axis=2).reshape(D, 1152)
    both, expert_grads, got = lax.optimization_barrier((both, expert_grads, got))
    both = lax.psum_scatter(both, plane, scatter_dimension=0, tiled=True)
    grad_out = both[:, 896:].reshape(4, 32, 256).transpose(1, 0, 2).reshape(32, HALF)
    both = f32(trade(both[:, :896].reshape(8, 16, 896), y, c))
    grad_w_qkv = both[:, :, :768].reshape(8, 16, 3, 256).transpose(1, 2, 0, 3).reshape(16, 3 * D)
    smalls = jnp.sum(both[:, :, 768:788] + both[:, :, 788:808], axis=0)

    out_own = jnp.where(own_first, grad_out[:16], grad_out[16:])
    out_par = other_core(jnp.where(own_first, grad_out[16:], grad_out[:16]))
    grad_w_out = jnp.where(own_first, join_halves(out_own, out_par), join_halves(out_par, out_own))
    grad_w_out = f32(grad_w_out)

    expert_grads = [f32(g) for g in expert_grads]
    grad_gate_up = jnp.stack([g[:, : 2 * FF] for g in expert_grads])
    grad_down = jnp.stack([g[:, 2 * FF :].T for g in expert_grads])
    return (
        layer_output,
        from_half(grad_tokens, zh, c)[None],
        grad_w_qkv,
        grad_w_out,
        smalls[:, 2:18],
        smalls[:, 0],
        smalls[:, 1],
        smalls[:, 18],
        smalls[:, 19],
        grad_gate_up,
        grad_down,
    )


def solution(mesh):
    fine = Mesh(mesh.devices.reshape(4, 2, 2, 4, 2), ("y", "zh", "zl", "x", "c"))
    ctx, fsdp = ("y", "zh"), ("zl", "x", "c")
    rows, blocks, line = P(ctx + fsdp, None), P(fsdp, ctx, None), P(ctx + fsdp)
    gate_up, down = P(ctx, fsdp, None), P(ctx, None, fsdp)
    return jax.shard_map(
        on_device,
        mesh=fine,
        in_specs=(blocks, blocks, rows, rows, rows, line, line, line, line, gate_up, down)
        + (P(fsdp, None, None), P(fsdp, ctx)),
        out_specs=(blocks, blocks, rows, rows, rows, line, line, line, line, gate_up, down),
        check_vma=False,
    )
```

```python
import jax
import jax.numpy as jnp
import numpy as np
from jax import lax
from jax.experimental import pallas as pl
from jax.experimental.pallas import tpu as pltpu
from jax.sharding import Mesh, PartitionSpec as P

D = 2048
HALF = 1024
HEAD_DIM = 128
FF = 1024
CAP = 384
ROWS = 128
SCALE = HEAD_DIM**-0.5

epsilon = 1e-06
rope_base = 10000.0


def f32(a):
    return a.astype(jnp.float32)


def bf16(a):
    return a.astype(jnp.bfloat16)


def dot(a, b):
    return jnp.dot(a, b, preferred_element_type=jnp.float32)


def dot_t(a, b):
    return lax.dot_general(a, b, (((1,), (1,)), ((), ())), preferred_element_type=jnp.float32)


def t_dot(a, b):
    return lax.dot_general(a, b, (((0,), (0,)), ((), ())), preferred_element_type=jnp.float32)


def other_core(a):
    return lax.ppermute(a, "c", [(0, 1), (1, 0)])


def from_chip(a, step):
    return lax.ppermute(a, "y", [(i, (i + step) % 4) for i in range(4)])


def y_gather(a):
    return [a] + [from_chip(a, step) for step in (1, 2, 3)]


def y_scatter(parts):
    return [parts[0]] + [from_chip(parts[step], 4 - step) for step in (1, 2, 3)]


def by_distance(a, y):
    place = (y - jnp.arange(4)) % 4
    hit = place[:, None] == jnp.arange(4)[None, :]
    return jnp.sum(jnp.where(hit[None, :, :, None], a[:, None], jnp.zeros((), a.dtype)), axis=2)


def chosen(a, place):
    hit = place[:, None] == jnp.arange(4)[None, :]
    hit = hit.reshape(4, 4, *[1] * (a.ndim - 1))
    return jnp.sum(jnp.where(hit, a[None], jnp.zeros((), a.dtype)), axis=1)


def trade(pieces, y, c):
    pairs = pieces.reshape(4, 2, *pieces.shape[1:])
    mine = jnp.where(c == 0, pairs[:, 0], pairs[:, 1])
    theirs = jnp.where(c == 0, pairs[:, 1], pairs[:, 0])
    got = other_core(theirs)
    both = jnp.where(c == 0, jnp.stack([mine, got], 1), jnp.stack([got, mine], 1))
    both = chosen(both, (y + jnp.arange(4)) % 4)
    got = jnp.stack([both[0]] + [from_chip(both[step], step) for step in (1, 2, 3)])
    return chosen(got, (y - jnp.arange(4)) % 4).reshape(pieces.shape)


def ring_sum(a, y):
    n = a.shape[0]
    a = a + other_core(a)
    a = by_distance(a.reshape(n, 4, 256), y)
    a = a + from_chip(a, 1) + from_chip(a, 2) + from_chip(a, 3)
    return by_distance(a, y).reshape(n, 1024)


def angle_tables():
    frequency = rope_base ** (-2.0 * np.arange(64) / HEAD_DIM)
    blocks = np.arange(8)[:, None] * ROWS * frequency[None]
    rows = np.arange(ROWS)[:, None] * frequency[None]
    tables = (np.cos(blocks), np.sin(blocks), np.cos(rows), np.sin(rows))
    return [jnp.asarray(table, jnp.float32) for table in tables]


def split_halves(a):
    blocks = [a[..., k * 128 : k * 128 + 128] for k in range(a.shape[-1] // 128)]
    return jnp.concatenate(blocks[0::2], axis=-1), jnp.concatenate(blocks[1::2], axis=-1)


def join_halves(low, high):
    blocks = []
    for k in range(low.shape[-1] // 128):
        blocks += [low[..., k * 128 : k * 128 + 128], high[..., k * 128 : k * 128 + 128]]
    return jnp.concatenate(blocks, axis=-1)


def other_layer(a):
    return lax.ppermute(a, "zh", [(0, 1), (1, 0)])


def to_half(low, high, zh, c):
    mine = jnp.where(c == 0, low, high)
    got = other_core(jnp.where(c == 0, high, low))
    keep = jnp.where(zh == c, mine, got)
    got = other_layer(jnp.where(zh == c, got, mine))
    return jnp.where(zh == 0, keep, got), jnp.where(zh == 0, got, keep)


def from_half(a, zh, c):
    first, second = a[:ROWS], a[ROWS:]
    mine = jnp.where(zh == 0, first, second)
    got = other_layer(jnp.where(zh == 0, second, first))
    keep = jnp.where(zh == c, mine, got)
    got = other_core(jnp.where(zh == c, got, mine))
    return join_halves(jnp.where(c == 0, keep, got), jnp.where(c == 0, got, keep))


def roped(values, cosine, sine):
    return values * cosine + pltpu.roll(values, 64, 1) * sine


def project_kernel(*refs):
    own, par = refs[:4], refs[4:8]
    gain, weights, qkv, tokens, rstd, squares = refs[8:]
    for s in range(4):

        @pl.when(pl.program_id(0) == s)
        def _():
            first, second = own[s][...].astype(jnp.float32), par[s][...].astype(jnp.float32)
            tokens[:, pl.ds(0, HALF)] = own[s][...]
            tokens[:, pl.ds(HALF, HALF)] = par[s][...]
            total = jnp.sum(first * first, axis=1, keepdims=True)
            total = total + jnp.sum(second * second, axis=1, keepdims=True)
            scale = lax.rsqrt(total * (1.0 / D) + epsilon)
            rstd[...] = scale
            first = (first * scale * gain[pl.ds(0, 1), :]).astype(jnp.bfloat16)
            second = (second * scale * gain[pl.ds(1, 1), :]).astype(jnp.bfloat16)
            out = dot(first, weights[pl.ds(0, HALF), :])
            out = out + dot(second, weights[pl.ds(HALF, HALF), :])
            qkv[...] = out
            ones = jnp.ones((8, 256), jnp.bfloat16)
            for k in range(2):
                part = out[:, k * 256 : k * 256 + 256]
                part = part * part
                coarse = part.astype(jnp.bfloat16)
                fine = (part - coarse.astype(jnp.float32)).astype(jnp.bfloat16)
                squares[pl.ds(k * 8, 8), :] = dot_t(ones, coarse) + dot_t(ones, fine)


def project(own, par, gain, weights):
    whole = pl.BlockSpec((256, HALF), lambda s: (0, 0))
    rows = lambda n: pl.BlockSpec((256, n), lambda s: (s, 0))
    return pl.pallas_call(
        project_kernel,
        grid=(4,),
        in_specs=[whole] * 8
        + [pl.BlockSpec((2, HALF), lambda s: (0, 0)), pl.BlockSpec((D, 768), lambda s: (0, 0))],
        out_specs=[
            rows(768),
            rows(D),
            rows(1),
            pl.BlockSpec((16, 256), lambda s: (0, s)),
        ],
        out_shape=[
            jax.ShapeDtypeStruct((1024, 768), jnp.float32),
            jax.ShapeDtypeStruct((1024, D), jnp.bfloat16),
            jax.ShapeDtypeStruct((1024, 1), jnp.float32),
            jax.ShapeDtypeStruct((16, 1024), jnp.float32),
        ],
        compiler_params=pltpu.CompilerParams(vmem_limit_bytes=VMEM_LIMIT),
        cost_estimate=pl.CostEstimate(
            flops=2 * 1024 * D * 768, bytes_accessed=20 << 20, transcendentals=0
        ),
    )(*own, *par, gain, weights)


def spread_kernel(
    d_q, d_k, d_v, q_pre, k_pre, rstd_q, rstd_k, along_q, along_k, gain_q, gain_k, tokens, rstd,
    weights, d_qkv, d_par, d_own, d_gain,
):
    @pl.when(pl.program_id(0) == 0)
    def _():
        d_gain[...] = jnp.zeros_like(d_gain)

    sides = (
        (d_q, q_pre, rstd_q, along_q, gain_q),
        (d_k, k_pre, rstd_k, along_k, gain_k),
    )
    for k, (grad, pre, scale, along, gain) in enumerate(sides):
        hat = pre[...] * scale[...]
        part = scale[...] * (grad[...] * gain[...] - hat * along[...])
        d_qkv[:, pl.ds(k * 256, 256)] = part.astype(jnp.bfloat16)
    d_qkv[:, pl.ds(512, 256)] = d_v[0]
    low = d_qkv[...]
    for k, out in ((1, d_par), (0, d_own)):
        at = pl.ds(k * HALF, HALF)
        part = dot_t(low, weights[at, :])
        out[...] = part.astype(out.dtype)
        hat = tokens[:, at].astype(jnp.float32) * rstd[...]
        d_gain[:, at] += jnp.sum(part * hat, axis=0, keepdims=True)


def spread(d_q, d_k, d_v, qkv, rstd_q, rstd_k, along_q, along_k, gain_q, gain_k, tokens, rstd, w):
    rows = lambda n, k=0: pl.BlockSpec((256, n), lambda s: (s, k))
    line = pl.BlockSpec((1, 256), lambda s: (0, 0))
    return pl.pallas_call(
        spread_kernel,
        grid=(4,),
        in_specs=[
            rows(256),
            rows(256),
            pl.BlockSpec((1, 256, 256), lambda s: (s, 0, 0)),
            rows(256),
            rows(256, 1),
            rows(1),
            rows(1),
            rows(1),
            rows(1),
            line,
            line,
            rows(D),
            rows(1),
            pl.BlockSpec((D, 768), lambda s: (0, 0)),
        ],
        out_specs=[rows(768), rows(HALF), rows(HALF), pl.BlockSpec((1, D), lambda s: (0, 0))],
        out_shape=[
            jax.ShapeDtypeStruct((1024, 768), jnp.bfloat16),
            jax.ShapeDtypeStruct((1024, HALF), jnp.bfloat16),
            jax.ShapeDtypeStruct((1024, HALF), jnp.float32),
            jax.ShapeDtypeStruct((1, D), jnp.float32),
        ],
        compiler_params=pltpu.CompilerParams(vmem_limit_bytes=VMEM_LIMIT),
        cost_estimate=pl.CostEstimate(
            flops=2 * 1024 * D * 768, bytes_accessed=20 << 20, transcendentals=0
        ),
    )(
        d_q, d_k, d_v, qkv, qkv, rstd_q, rstd_k, along_q, along_k,
        gain_q[None], gain_k[None], tokens, rstd, w,
    )


def whole_spec(*shape):
    return pl.BlockSpec(shape, lambda *_: (0,) * len(shape))


def params(flops, data):
    return dict(
        compiler_params=pltpu.CompilerParams(vmem_limit_bytes=VMEM_LIMIT),
        cost_estimate=pl.CostEstimate(flops=flops, bytes_accessed=data, transcendentals=0),
    )


def output_kernel(attended, weights, parts, own):
    out = dot(attended[...], weights[...])
    parts[0] = out.astype(jnp.bfloat16)

    @pl.when(pl.program_id(0) == 0)
    def _():
        own[...] = out


def output_product(attended, weights):
    return pl.pallas_call(
        output_kernel,
        grid=(4,),
        in_specs=[pl.BlockSpec((256, 512), lambda s: (s, 0)), whole_spec(512, HALF)],
        out_specs=[pl.BlockSpec((1, 256, HALF), lambda s: (s, 0, 0)), whole_spec(256, HALF)],
        out_shape=[
            jax.ShapeDtypeStruct((4, 256, HALF), jnp.bfloat16),
            jax.ShapeDtypeStruct((256, HALF), jnp.float32),
        ],
        **params(1 << 30, 5 << 20),
    )(attended, weights)


def residual_kernel(tokens, own, first, second, third, after, square):
    total = tokens[...].astype(jnp.float32) + own[...]
    for part in (first, second, third):
        total = total + part[...].astype(jnp.float32)
    after[...] = total
    square[...] = jnp.sum(total * total, axis=1, keepdims=True)


def residual(tokens, own, got):
    rows = whole_spec(256, HALF)
    return pl.pallas_call(
        residual_kernel,
        grid=(1,),
        in_specs=[rows] * 5,
        out_specs=[rows, whole_spec(256, 1)],
        out_shape=[
            jax.ShapeDtypeStruct((256, HALF), jnp.float32),
            jax.ShapeDtypeStruct((256, 1), jnp.float32),
        ],
        **params(1 << 20, 5 << 20),
    )(tokens, own, *got)


def logits_kernel(router_t, normed, out):
    out[...] = dot_t(router_t[...], normed[...])


def logits_of(router_t, normed):
    return pl.pallas_call(
        logits_kernel,
        grid=(1,),
        in_specs=[whole_spec(16, HALF), whole_spec(1024, HALF)],
        out_specs=whole_spec(16, 1024),
        out_shape=jax.ShapeDtypeStruct((16, 1024), jnp.float32),
        **params(1 << 25, 2 << 20),
    )(router_t, normed)


def route_back_kernel(
    normed, d_logits, router_t, after, rstd, gain, *refs
):
    got, (grad, d_normed, d_gain, along) = refs[:4], refs[4:]
    coarse = d_logits[...].astype(jnp.bfloat16)
    fine = (d_logits[...] - coarse.astype(jnp.float32)).astype(jnp.bfloat16)
    grad[...] = dot(coarse, normed[...]) + dot(fine, normed[...])
    total = got[0][...].astype(jnp.float32)
    for part in got[1:]:
        total = total + part[...].astype(jnp.float32)
    total = total + (t_dot(coarse, router_t[...]) + t_dot(fine, router_t[...]))
    d_normed[...] = total
    hat = after[...] * rstd[...]
    d_gain[...] = jnp.sum(total * hat, axis=0, keepdims=True)
    along[...] = jnp.sum(total * gain[...] * hat, axis=1, keepdims=True)


def route_back(normed, d_logits, router_t, after, rstd, gain, got):
    rows = whole_spec(256, HALF)
    return pl.pallas_call(
        route_back_kernel,
        grid=(1,),
        in_specs=[
            rows,
            whole_spec(16, 256),
            whole_spec(16, HALF),
            rows,
            whole_spec(256, 1),
            whole_spec(1, HALF),
            rows,
            rows,
            rows,
            rows,
        ],
        out_specs=[whole_spec(16, HALF), rows, whole_spec(1, HALF), whole_spec(256, 1)],
        out_shape=[
            jax.ShapeDtypeStruct((16, HALF), jnp.float32),
            jax.ShapeDtypeStruct((256, HALF), jnp.float32),
            jax.ShapeDtypeStruct((1, HALF), jnp.float32),
            jax.ShapeDtypeStruct((256, 1), jnp.float32),
        ],
        **params(1 << 25, 6 << 20),
    )(normed, d_logits, router_t, after, rstd, gain, *got)


def back_kernel(tokens, rstd, gain, first, second, third, fourth, d_normed, along):
    total = first[...].astype(jnp.float32)
    for part in (second, third, fourth):
        total = total + part[...].astype(jnp.float32)
    total = total * gain[...]
    d_normed[...] = total
    hat = tokens[...].astype(jnp.float32) * rstd[...]
    along[...] = jnp.sum(total * hat, axis=1, keepdims=True)


def back_sums(tokens, rstd, gain, got):
    rows = whole_spec(256, HALF)
    return pl.pallas_call(
        back_kernel,
        grid=(1,),
        in_specs=[rows, whole_spec(256, 1), whole_spec(1, HALF)] + [rows] * 4,
        out_specs=[rows, whole_spec(256, 1)],
        out_shape=[
            jax.ShapeDtypeStruct((256, HALF), jnp.float32),
            jax.ShapeDtypeStruct((256, 1), jnp.float32),
        ],
        **params(1 << 20, 5 << 20),
    )(tokens, rstd, gain, *got)


def out_grad_kernel(attended, d_attn, out, total):
    @pl.when(pl.program_id(0) == 0)
    def _():
        total[...] = jnp.zeros_like(total)

    total[...] += t_dot(attended[...], d_attn[...])

    @pl.when(pl.program_id(0) == 3)
    def _():
        out[...] = total[...].astype(jnp.bfloat16)


def out_grad(attended, d_attn):
    rows = lambda n: pl.BlockSpec((256, n), lambda s: (s, 0))
    return pl.pallas_call(
        out_grad_kernel,
        grid=(4,),
        in_specs=[rows(512), rows(HALF)],
        out_specs=whole_spec(512, HALF),
        out_shape=jax.ShapeDtypeStruct((512, HALF), jnp.bfloat16),
        scratch_shapes=[pltpu.VMEM((512, HALF), jnp.float32)],
        **params(1 << 30, 5 << 20),
    )(attended, d_attn)


def heads_kernel(d_attn, weights, own, par):
    own[...] = dot_t(d_attn[...], weights[pl.ds(0, 256), :])
    par[...] = dot_t(d_attn[...], weights[pl.ds(256, 256), :])


def heads_product(d_attn, weights):
    rows = lambda n: pl.BlockSpec((256, n), lambda s: (s, 0))
    return pl.pallas_call(
        heads_kernel,
        grid=(4,),
        in_specs=[rows(HALF), whole_spec(512, HALF)],
        out_specs=[rows(256), rows(256)],
        out_shape=[jax.ShapeDtypeStruct((1024, 256), jnp.float32)] * 2,
        **params(1 << 30, 5 << 20),
    )(d_attn, weights)


def along_kernel(
    d_q, d_k, q_pre, k_pre, rstd_q, rstd_k, gain_q, gain_k, along, d_gain_q, d_gain_k
):
    @pl.when(pl.program_id(0) == 0)
    def _():
        d_gain_q[...] = jnp.zeros_like(d_gain_q)
        d_gain_k[...] = jnp.zeros_like(d_gain_k)

    ones = jnp.ones((8, 256), jnp.bfloat16)
    sides = ((d_q, q_pre, rstd_q, gain_q, d_gain_q), (d_k, k_pre, rstd_k, gain_k, d_gain_k))
    for k, (grad, pre, scale, gain, d_gain) in enumerate(sides):
        part = grad[...] * (pre[...] * scale[...])
        d_gain[...] += jnp.sum(part, axis=0, keepdims=True)
        part = part * gain[...]
        coarse = part.astype(jnp.bfloat16)
        part = part - coarse.astype(jnp.float32)
        fine = part.astype(jnp.bfloat16)
        along[pl.ds(k * 8, 8), :] = dot_t(ones, coarse) + dot_t(ones, fine)


def along_sums(d_q, d_k, qkv, rstd_q, rstd_k, gain_q, gain_k):
    rows = lambda n, k=0: pl.BlockSpec((256, n), lambda s: (s, k))
    line = whole_spec(1, 256)
    return pl.pallas_call(
        along_kernel,
        grid=(4,),
        in_specs=[rows(256), rows(256), rows(256), rows(256, 1), rows(1), rows(1), line, line],
        out_specs=[pl.BlockSpec((16, 256), lambda s: (0, s)), line, line],
        out_shape=[
            jax.ShapeDtypeStruct((16, 1024), jnp.float32),
            jax.ShapeDtypeStruct((1, 256), jnp.float32),
            jax.ShapeDtypeStruct((1, 256), jnp.float32),
        ],
        **params(1 << 22, 5 << 20),
    )(d_q, d_k, qkv, qkv, rstd_q, rstd_k, gain_q[None], gain_k[None])


def outer_kernel(tokens, rstd, gain, d_qkv, out, total):
    @pl.when(pl.program_id(0) == 0)
    def _():
        total[...] = jnp.zeros_like(total)

    low = d_qkv[...]
    for k in range(4):
        at = pl.ds(k * 512, 512)
        normed = tokens[:, at].astype(jnp.float32) * rstd[...] * gain[:, at]
        total[at, :] += dot(jnp.transpose(normed).astype(jnp.bfloat16), low)

    @pl.when(pl.program_id(0) == 3)
    def _():
        out[...] = total[...].astype(jnp.bfloat16)


def outer(tokens, rstd, gain, d_qkv):
    rows = lambda n: pl.BlockSpec((256, n), lambda s: (s, 0))
    return pl.pallas_call(
        outer_kernel,
        grid=(4,),
        in_specs=[rows(D), rows(1), pl.BlockSpec((1, D), lambda s: (0, 0)), rows(768)],
        out_specs=pl.BlockSpec((D, 768), lambda s: (0, 0)),
        out_shape=jax.ShapeDtypeStruct((D, 768), jnp.bfloat16),
        scratch_shapes=[pltpu.VMEM((D, 768), jnp.float32)],
        compiler_params=pltpu.CompilerParams(vmem_limit_bytes=VMEM_LIMIT),
        cost_estimate=pl.CostEstimate(
            flops=2 * 1024 * D * 768, bytes_accessed=16 << 20, transcendentals=0
        ),
    )(tokens, rstd, gain, d_qkv)


def attend_kernel(
    q_pre, k_pre, v_pre, rstd_q, rstd_k, gain_q, gain_k, cosine, sine,
    attended, q_out, k_out, v_out, total, v_t,
):
    i = pl.program_id(1)

    @pl.when(i == 0)
    def _():
        cos, sin = cosine[...], sine[...]
        q_out[0] = roped(q_pre[...] * rstd_q[...] * gain_q[0], cos, sin).astype(jnp.bfloat16)
        k_out[0] = roped(k_pre[...] * rstd_k[...] * gain_k[0], cos, sin).astype(jnp.bfloat16)
        v_out[0] = v_pre[...].astype(jnp.bfloat16)
        v_t[...] = jnp.transpose(v_pre[...]).astype(jnp.bfloat16)

    query = q_out[0, pl.ds(pl.multiple_of(i * SPAN, SPAN), SPAN), :]
    scores = dot_t(k_out[0], query) * SCALE
    most = jnp.max(scores, axis=0, keepdims=True)
    weights = jnp.exp(scores - most)
    mass = jnp.sum(weights, axis=0, keepdims=True)
    total[0] = most + jnp.log(mass)
    probs = (weights / mass).astype(jnp.bfloat16)
    attended[0] = jnp.transpose(dot(v_t[...], probs)).astype(jnp.bfloat16)


SPAN = 256


def attend(qkv, rstd_q, rstd_k, gain_q, gain_k, cosine, sine):
    column = pl.BlockSpec((1024, 1), lambda h, i: (0, 0))
    gain = pl.BlockSpec((1, 1, 128), lambda h, i: (h, 0, 0))
    table = pl.BlockSpec((1024, 128), lambda h, i: (0, 0))
    head = pl.BlockSpec((1, 1024, 128), lambda h, i: (h, 0, 0))
    head_shape = jax.ShapeDtypeStruct((2, 1024, 128), jnp.bfloat16)
    return pl.pallas_call(
        attend_kernel,
        grid=(2, 1024 // SPAN),
        in_specs=[
            pl.BlockSpec((1024, 128), lambda h, i: (0, h)),
            pl.BlockSpec((1024, 128), lambda h, i: (0, 2 + h)),
            pl.BlockSpec((1024, 128), lambda h, i: (0, 4 + h)),
            column,
            column,
            gain,
            gain,
            table,
            table,
        ],
        out_specs=[
            pl.BlockSpec((1, SPAN, 128), lambda h, i: (i, 0, h)),
            head,
            head,
            head,
            pl.BlockSpec((1, 1, SPAN), lambda h, i: (h, 0, i)),
        ],
        out_shape=[
            jax.ShapeDtypeStruct((1024 // SPAN, SPAN, 256), jnp.bfloat16),
            head_shape,
            head_shape,
            head_shape,
            jax.ShapeDtypeStruct((2, 1, 1024), jnp.float32),
        ],
        scratch_shapes=[pltpu.VMEM((128, 1024), jnp.bfloat16)],
        compiler_params=pltpu.CompilerParams(vmem_limit_bytes=VMEM_LIMIT),
        cost_estimate=pl.CostEstimate(
            flops=2 * 4 * 1024 * 1024 * 128, bytes_accessed=8 << 20, transcendentals=2 << 20
        ),
    )(
        qkv,
        qkv,
        qkv,
        rstd_q,
        rstd_k,
        gain_q.reshape(2, 1, 128),
        gain_k.reshape(2, 1, 128),
        cosine,
        sine,
    )


def attend_back_kernel(
    d_att, q, k, v, total, cosine, sine, d_q, d_k, d_v, k_t, k_acc, v_acc
):
    i = pl.program_id(1)

    @pl.when(i == 0)
    def _():
        k_t[...] = jnp.transpose(k[0].astype(jnp.float32)).astype(jnp.bfloat16)
        k_acc[...] = jnp.zeros_like(k_acc)
        v_acc[...] = jnp.zeros_like(v_acc)

    at = pl.ds(pl.multiple_of(i * SPAN, SPAN), SPAN)
    query = q[0, at, :]
    probs = jnp.exp(dot_t(k[0], query) * SCALE - total[0])
    d_probs = dot_t(v[0], d_att[...])
    spread = jnp.sum(probs * d_probs, axis=0, keepdims=True)
    d_scores = (probs * (d_probs - spread)).astype(jnp.bfloat16)
    v_acc[...] += dot(probs.astype(jnp.bfloat16), d_att[...])
    k_acc[...] += dot(d_scores, query)
    d_query = jnp.transpose(dot(k_t[...], d_scores)) * SCALE
    d_q[...] = roped(d_query, cosine[at, :], -sine[at, :])

    @pl.when(i == pl.num_programs(1) - 1)
    def _():
        d_k[...] = roped(k_acc[...] * SCALE, cosine[...], -sine[...])
        d_v[...] = v_acc[...].reshape(4, 256, 128).astype(jnp.bfloat16)


def attend_back(d_att, q, k, v, total, cosine, sine):
    table = pl.BlockSpec((1024, 128), lambda h, i: (0, 0))
    head = pl.BlockSpec((1, 1024, 128), lambda h, i: (h, 0, 0))
    columns = pl.BlockSpec((1024, 128), lambda h, i: (0, h))
    tile = pl.BlockSpec((SPAN, 128), lambda h, i: (i, h))
    return pl.pallas_call(
        attend_back_kernel,
        grid=(2, 1024 // SPAN),
        in_specs=[
            tile,
            head,
            head,
            head,
            pl.BlockSpec((1, 1, SPAN), lambda h, i: (h, 0, i)),
            table,
            table,
        ],
        out_specs=[tile, columns, pl.BlockSpec((4, 256, 128), lambda h, i: (0, 0, h))],
        out_shape=[
            jax.ShapeDtypeStruct((1024, 256), jnp.float32),
            jax.ShapeDtypeStruct((1024, 256), jnp.float32),
            jax.ShapeDtypeStruct((4, 256, 256), jnp.bfloat16),
        ],
        scratch_shapes=[
            pltpu.VMEM((128, 1024), jnp.bfloat16),
            pltpu.VMEM((1024, 128), jnp.float32),
            pltpu.VMEM((1024, 128), jnp.float32),
        ],
        compiler_params=pltpu.CompilerParams(vmem_limit_bytes=VMEM_LIMIT),
        cost_estimate=pl.CostEstimate(
            flops=2 * 10 * 1024 * 1024 * 128, bytes_accessed=8 << 20, transcendentals=2 << 20
        ),
    )(d_att, q, k, v, total, cosine, sine)


CHUNKS = 2
PART = FF // CHUNKS
WIDE = 3 * PART
VMEM_LIMIT = 58 * 1024 * 1024


def pack_kernel(gate_up, down, out):
    down_t = jnp.transpose(down[0].astype(jnp.float32)).astype(jnp.bfloat16)
    for f in range(CHUNKS):
        out[0, :, pl.ds(f * WIDE, PART)] = gate_up[0, :, pl.ds(f * PART, PART)]
        out[0, :, pl.ds(f * WIDE + PART, PART)] = gate_up[0, :, pl.ds(FF + f * PART, PART)]
        out[0, :, pl.ds(f * WIDE + 2 * PART, PART)] = down_t[:, f * PART : (f + 1) * PART]


def pack_experts(gate_up, down):
    return pl.pallas_call(
        pack_kernel,
        grid=(2,),
        in_specs=[
            pl.BlockSpec((1, 128, 2 * FF), lambda m: (m, 0, 0)),
            pl.BlockSpec((1, FF, 128), lambda m: (m, 0, 0)),
        ],
        out_specs=pl.BlockSpec((1, 128, 3 * FF), lambda m: (m, 0, 0)),
        out_shape=jax.ShapeDtypeStruct((2, 128, 3 * FF), jnp.bfloat16),
        compiler_params=pltpu.CompilerParams(vmem_limit_bytes=VMEM_LIMIT),
        cost_estimate=pl.CostEstimate(flops=0, bytes_accessed=4 << 20, transcendentals=0),
    )(gate_up, down)


def unpack_kernel(first, second, gate_up, down):
    for m, part in enumerate((first, second)):

        @pl.when(pl.program_id(0) == m)
        def _():
            for f in range(CHUNKS):
                at = f * WIDE
                gate_up[0, :, pl.ds(f * PART, PART)] = part[:, pl.ds(at, PART)].astype(jnp.float32)
                up = part[:, pl.ds(at + PART, PART)].astype(jnp.float32)
                gate_up[0, :, pl.ds(FF + f * PART, PART)] = up
                down_t = part[:, pl.ds(at + 2 * PART, PART)].astype(jnp.float32)
                down[0, pl.ds(f * PART, PART), :] = jnp.transpose(down_t)


def unpack_experts(first, second):
    whole = pl.BlockSpec((128, 3 * FF), lambda m: (0, 0))
    return pl.pallas_call(
        unpack_kernel,
        grid=(2,),
        in_specs=[whole, whole],
        out_specs=[
            pl.BlockSpec((1, 128, 2 * FF), lambda m: (m, 0, 0)),
            pl.BlockSpec((1, FF, 128), lambda m: (m, 0, 0)),
        ],
        out_shape=[
            jax.ShapeDtypeStruct((2, 128, 2 * FF), jnp.float32),
            jax.ShapeDtypeStruct((2, FF, 128), jnp.float32),
        ],
        compiler_params=pltpu.CompilerParams(vmem_limit_bytes=VMEM_LIMIT),
        cost_estimate=pl.CostEstimate(flops=0, bytes_accessed=4 << 20, transcendentals=0),
    )(first, second)


def turned(a):
    return jnp.transpose(a.astype(jnp.float32)).astype(jnp.bfloat16)


def open_kernel(
    seat, gate, normed, cot, weights,
    part, rows_t, d_out_t, cot_rows, pick_t, weight, rows, d_out,
):
    @pl.when(pl.program_id(1) == 0)
    def _():
        taken = lax.broadcasted_iota(jnp.int32, (CAP, 1024), 0) == seat[0]
        slot_weight = jnp.sum(jnp.where(taken, gate[0], 0.0), axis=1, keepdims=True)
        weight[0] = slot_weight
        pick = jnp.where(taken, 1.0, 0.0)
        pick_t[0] = turned(pick)
        pick = pick.astype(jnp.bfloat16)
        for at in range(0, HALF, 512):
            spot = pl.ds(at, 512)
            found = dot(pick, normed[:, spot])
            rows[:, spot] = found.astype(jnp.bfloat16)
            rows_t[0, spot, :] = turned(found)
            picked = dot(pick, cot[:, spot])
            cot_rows[0, :, spot] = picked.astype(jnp.bfloat16)
            picked = picked * slot_weight
            d_out[:, spot] = picked.astype(jnp.bfloat16)
            d_out_t[0, spot, :] = turned(picked)

    for k, left in enumerate((rows, rows, d_out)):
        at = pl.ds(k * PART, PART)
        part[0, :, at] = dot(left[...], weights[0, :, at]).astype(jnp.bfloat16)


def open_experts(seat, gate, normed, cot, weights):
    whole = pl.BlockSpec((1024, HALF), lambda h, f: (0, 0))
    line = pl.BlockSpec((1, 1, 1024), lambda h, f: (h, 0, 0))
    slot = pl.BlockSpec((1, CAP, HALF), lambda h, f: (h, 0, 0))
    slot_t = pl.BlockSpec((1, HALF, CAP), lambda h, f: (h, 0, 0))
    shape_t = jax.ShapeDtypeStruct((2, HALF, CAP), jnp.bfloat16)
    return pl.pallas_call(
        open_kernel,
        grid=(2, CHUNKS),
        in_specs=[
            line,
            line,
            whole,
            whole,
            pl.BlockSpec((1, HALF, WIDE), lambda h, f: (h, 0, f)),
        ],
        out_specs=[
            pl.BlockSpec((1, CAP, WIDE), lambda h, f: (h, 0, f)),
            slot_t,
            slot_t,
            slot,
            slot_t,
            pl.BlockSpec((1, CAP, 1), lambda h, f: (h, 0, 0)),
        ],
        out_shape=[
            jax.ShapeDtypeStruct((2, CAP, 3 * FF), jnp.bfloat16),
            shape_t,
            shape_t,
            jax.ShapeDtypeStruct((2, CAP, HALF), jnp.bfloat16),
            shape_t,
            jax.ShapeDtypeStruct((2, CAP, 1), jnp.float32),
        ],
        scratch_shapes=[pltpu.VMEM((CAP, HALF), jnp.bfloat16)] * 2,
        compiler_params=pltpu.CompilerParams(vmem_limit_bytes=VMEM_LIMIT),
        cost_estimate=pl.CostEstimate(
            flops=2 * 2 * CAP * 1024 * 5120, bytes_accessed=30 << 20, transcendentals=0
        ),
    )(seat, gate, normed, cot, weights)


def close_kernel(
    first, seat, own, received, rows_t, d_out_t, cot_rows, pick_t, weight, weights, *refs
):
    if first:
        moe, d_normed, grads, d_token, moe_acc, d_acc, out_acc, row_acc = refs
    else:
        moe_in, d_in, moe, d_normed, grads, d_token, moe_acc, d_acc, out_acc, row_acc = refs
    h, f = pl.program_id(0), pl.program_id(1)

    @pl.when((h == 0) & (f == 0))
    def _():
        if first:
            moe_acc[...] = jnp.zeros_like(moe_acc)
            d_acc[...] = jnp.zeros_like(d_acc)
        else:
            for s in range(4):
                moe_acc[pl.ds(s * 256, 256), :] = moe_in[s].astype(jnp.float32)
                d_acc[pl.ds(s * 256, 256), :] = d_in[s].astype(jnp.float32)

    @pl.when(f == 0)
    def _():
        out_acc[...] = jnp.zeros_like(out_acc)
        row_acc[...] = jnp.zeros_like(row_acc)

    def both(k):
        at = pl.ds(k * PART, PART)
        return own[0, :, at].astype(jnp.float32) + received[0, :, at].astype(jnp.float32)

    gate, up, d_hidden = both(0), both(1), both(2)
    sig = jax.nn.sigmoid(gate)
    scaled = gate * sig
    hidden = (scaled * up).astype(jnp.bfloat16)
    d_gate = (d_hidden * up * sig * (1.0 + gate * (1.0 - sig))).astype(jnp.bfloat16)
    d_up = (d_hidden * scaled).astype(jnp.bfloat16)
    out_acc[...] += dot_t(hidden, weights[0, :, pl.ds(2 * PART, PART)])
    row_acc[...] += dot_t(d_gate, weights[0, :, pl.ds(0, PART)])
    row_acc[...] += dot_t(d_up, weights[0, :, pl.ds(PART, PART)])
    grads[0, :, pl.ds(0, PART)] = dot(rows_t[0], d_gate).astype(jnp.bfloat16)
    grads[0, :, pl.ds(PART, PART)] = dot(rows_t[0], d_up).astype(jnp.bfloat16)
    grads[0, :, pl.ds(2 * PART, PART)] = dot(d_out_t[0], hidden).astype(jnp.bfloat16)

    @pl.when(f == CHUNKS - 1)
    def _():
        d_weight = jnp.sum(out_acc[...] * cot_rows[0].astype(jnp.float32), axis=1, keepdims=True)
        taken = lax.broadcasted_iota(jnp.int32, (CAP, 1024), 0) == seat[0]
        d_token[0] = jnp.sum(jnp.where(taken, d_weight, 0.0), axis=0, keepdims=True)
        weighted = (weight[0] * out_acc[...]).astype(jnp.bfloat16)
        d_rows = row_acc[...].astype(jnp.bfloat16)
        for at in range(0, HALF, 512):
            spot = pl.ds(at, 512)
            moe_acc[:, spot] += dot(pick_t[0], weighted[:, at : at + 512])
            d_acc[:, spot] += dot(pick_t[0], d_rows[:, at : at + 512])

    @pl.when((h == 1) & (f == CHUNKS - 1))
    def _():
        for s in range(4):
            moe[s] = moe_acc[pl.ds(s * 256, 256), :].astype(moe.dtype)
            d_normed[s] = d_acc[pl.ds(s * 256, 256), :].astype(d_normed.dtype)


def close_experts(seat, own, received, state, weights, before):
    whole = pl.BlockSpec((4, 256, HALF), lambda h, f: (0, 0, 0))
    line = pl.BlockSpec((1, 1, 1024), lambda h, f: (h, 0, 0))
    slot = pl.BlockSpec((1, CAP, HALF), lambda h, f: (h, 0, 0))
    slot_t = pl.BlockSpec((1, HALF, CAP), lambda h, f: (h, 0, 0))
    part = pl.BlockSpec((1, CAP, WIDE), lambda h, f: (h, 0, f))
    wide = pl.BlockSpec((1, HALF, WIDE), lambda h, f: (h, 0, f))
    full = jax.ShapeDtypeStruct((4, 256, HALF), jnp.bfloat16)

    def body(*refs):
        close_kernel(not before, *refs)

    return pl.pallas_call(
        body,
        grid=(2, CHUNKS),
        in_specs=[
            line,
            part,
            part,
            slot_t,
            slot_t,
            slot,
            slot_t,
            pl.BlockSpec((1, CAP, 1), lambda h, f: (h, 0, 0)),
            wide,
        ]
        + [whole] * len(before),
        out_specs=[whole, whole, wide, line],
        out_shape=[
            full,
            full,
            jax.ShapeDtypeStruct((2, HALF, 3 * FF), jnp.bfloat16),
            jax.ShapeDtypeStruct((2, 1, 1024), jnp.float32),
        ],
        scratch_shapes=[
            pltpu.VMEM((1024, HALF), jnp.float32),
            pltpu.VMEM((1024, HALF), jnp.float32),
            pltpu.VMEM((CAP, HALF), jnp.float32),
            pltpu.VMEM((CAP, HALF), jnp.float32),
        ],
        compiler_params=pltpu.CompilerParams(vmem_limit_bytes=VMEM_LIMIT),
        cost_estimate=pl.CostEstimate(
            flops=2 * 2 * CAP * 1024 * 8192, bytes_accessed=50 << 20, transcendentals=2 * CAP * FF
        ),
    )(seat, own, received, *state, weights, *before)


def on_device(
    tokens,
    cotangent,
    w_qkv,
    w_out,
    w_router,
    norm_attn,
    norm_moe,
    query_gain,
    key_gain,
    w_gate_up,
    w_down,
    routes,
    block_order,
):
    y, zh, c = lax.axis_index("y"), lax.axis_index("zh"), lax.axis_index("c")
    plane = ("zh", "zl", "x")
    own_first = c == 0

    low, high = split_halves(tokens[0])
    low, high, w_qkv = lax.optimization_barrier((low, high, w_qkv))
    x_blocks = jnp.concatenate(to_half(low, high, zh, c))
    x_blocks, block_order, w_gate_up, cotangent, routes = lax.optimization_barrier(
        (x_blocks, block_order, w_gate_up, cotangent, routes)
    )
    x_own = y_gather(x_blocks)
    x_par = [other_core(part) for part in x_own]
    place = jnp.full((8, 128), block_order[0, 0], jnp.int32).astype(jnp.float32)
    places = y_gather(jnp.stack(to_half(place, place, zh, c)))
    places = jnp.stack(places)[:, :, 0, 0].reshape(8)

    pieces = w_qkv.reshape(16, 3, 8, 256).transpose(2, 0, 1, 3).reshape(8, 16, 768)
    small = jnp.concatenate(
        [norm_attn[:, None], norm_moe[:, None], w_router, query_gain[:, None], key_gain[:, None]],
        axis=1,
    )
    small = jnp.pad(small, ((0, 0), (0, 108)))
    pieces = jnp.concatenate([pieces, jnp.broadcast_to(small, (8, 16, 128))], axis=2)
    pieces = trade(pieces, y, c).reshape(128, 896)
    out_low, out_high = split_halves(w_out)
    out_par = other_core(jnp.where(own_first, out_high, out_low))
    out_own = jnp.where(own_first, out_low, out_high)
    out_both = jnp.where(
        own_first, jnp.concatenate([out_own, out_par]), jnp.concatenate([out_par, out_own])
    )
    out_both = out_both.reshape(32, 4, 256).transpose(1, 0, 2).reshape(128, 256)
    dense = jnp.concatenate([pieces, out_both], axis=1)
    dense, w_gate_up = lax.optimization_barrier((dense, w_gate_up))
    dense = lax.all_gather(dense, plane, axis=0, tiled=True).reshape(2, 2, 4, 4, 2, 16, 1152)

    expert_w = [
        lax.all_gather(part, plane, axis=0, tiled=True).reshape(2, HALF, 3 * FF)
        for part in pack_experts(w_gate_up, w_down)
    ]

    cot_low, cot_high = split_halves(cotangent[0])
    cot_here = jnp.concatenate(to_half(cot_low, cot_high, zh, c))
    cot_sent, x_own = lax.optimization_barrier((cot_here, x_own))
    cot_parts = y_gather(cot_sent)
    route_t = routes[0].T
    route_t = jnp.where(c == zh, route_t, other_core(route_t))
    route_t = by_distance(route_t.reshape(4, 4, 256), y).reshape(4, 1024)

    def rolled(a):
        a = a.transpose(1, 3, 0, 2, 4, 5, 6).reshape(2, HALF, -1)
        return jnp.where(own_first, a, a[::-1])

    qkv_w = rolled(dense[..., :768]).reshape(D, 768)
    small_all = dense[..., 768:788]
    small_rolled = f32(rolled(small_all))
    gain_attn = small_rolled[:, :, 0]
    gain_moe = small_rolled[0, :, 1]
    router_w = bf16(small_rolled[0, :, 2:18])
    small_true = f32(small_all[..., 18:20].transpose(3, 0, 1, 2, 4, 5, 6).reshape(8, 256, 2))
    head_block = y * 2 + c
    mine = lax.dynamic_index_in_dim(small_true, head_block, 0, keepdims=False)
    gain_query, gain_key = mine[:, 0], mine[:, 1]
    out_w = dense.reshape(16, 128, 1152)[:, :, 896:].reshape(16, 4, 32, 256)
    out_w = out_w.transpose(0, 2, 1, 3).reshape(2, 256, HALF)
    out_w = jnp.where(own_first, out_w, out_w[::-1]).reshape(512, HALF)

    qkv, x_all, rstd_one, squares = project(x_own, x_par, gain_attn, qkv_w)
    squares = squares.reshape(2, 8, 1024)[:, 0]
    rstd = lax.rsqrt(ring_sum(squares, y) / D + epsilon)
    rstd_q, rstd_k = rstd[0][:, None], rstd[1][:, None]
    here = places[:, None, None] == jnp.arange(8, dtype=jnp.float32)[None, :, None]
    block_cos, block_sin, row_cos, row_sin = angle_tables()
    block_cos = jnp.sum(jnp.where(here, block_cos, 0.0), axis=1)[:, None]
    block_sin = jnp.sum(jnp.where(here, block_sin, 0.0), axis=1)[:, None]
    cosine = block_cos * row_cos - block_sin * row_sin
    sine = block_sin * row_cos + block_cos * row_sin
    cosine = jnp.concatenate([cosine, cosine], axis=2).reshape(1024, 128)
    sine = jnp.concatenate([-sine, sine], axis=2).reshape(1024, 128)
    qkv, out_w, cosine, sine = lax.optimization_barrier((qkv, out_w, cosine, sine))
    attended, *heads = attend(qkv, rstd_q, rstd_k, gain_query, gain_key, cosine, sine)
    attended, cot_parts = lax.optimization_barrier(
        (attended.reshape(1024, 256), cot_parts)
    )
    cot_all = jnp.concatenate(cot_parts)
    attended = jnp.concatenate([attended, other_core(attended)], axis=1)
    out_parts, out_here = output_product(attended, out_w)
    got = [from_chip(out_parts[step], 4 - step) for step in (1, 2, 3)]
    x_here = f32(x_all[:256, :HALF])
    after, square = residual(x_all, out_here, got)

    square = square.reshape(256)
    rstd_two = lax.rsqrt((square + other_core(square)) / D + epsilon)[:, None]
    after_hat = after * rstd_two
    normed_two = bf16(after_hat * gain_moe)
    normed_all = jnp.concatenate(y_gather(normed_two))
    router_t = router_w.T
    logits = logits_of(router_t, normed_all)
    logits = logits + other_core(logits)
    picked = route_t[:, None, :] == jnp.arange(16, dtype=jnp.int32)[None, :, None]
    routed = jnp.sum(jnp.where(picked, logits[None], 0.0), axis=1)
    routed = jnp.exp(routed - jnp.max(routed, axis=0, keepdims=True))
    gates = routed / (routed[0] + routed[1] + routed[2] + routed[3])

    before, d_gates, expert_grads = (), jnp.zeros((4, 1024), jnp.float32), []
    for m in range(2):
        chosen = route_t[None] == y * 4 + jnp.arange(2, dtype=jnp.int32)[:, None, None] * 2 + m
        hit = jnp.sum(chosen.astype(jnp.int32), axis=1)
        rank = jnp.cumsum(hit, axis=1) - hit
        seat = jnp.where(hit > 0, rank, CAP)[:, None]
        gate_token = jnp.sum(jnp.where(chosen, gates[None], 0.0), axis=1)[:, None]
        seat, before = lax.optimization_barrier((seat, before))
        part, *state = open_experts(seat, gate_token, normed_all, cot_all, expert_w[m])
        moe_sum, d_normed, grads, d_token = close_experts(
            seat, part, other_core(part), state, expert_w[m], before
        )
        before = (moe_sum, d_normed)
        d_gates = d_gates + jnp.sum(jnp.where(chosen, d_token, 0.0), axis=0)
        expert_grads.append(
            lax.psum_scatter(grads.reshape(D, 3 * FF), plane, scatter_dimension=0, tiled=True)
        )

    def ring_scatter(a):
        a = a.reshape(4, 256, HALF)
        return sum(f32(g) for g in y_scatter([a[s] for s in range(4)]))

    d_got = y_scatter([d_normed[step] for step in range(4)])
    d_gates = d_gates.reshape(4, 4, 256)
    d_gates = sum(y_scatter([d_gates[:, s] for s in range(4)]))
    d_gates = d_gates + other_core(d_gates)

    gates_here, picked_here = gates[:, :256], picked[:, :, :256]
    shared = gates_here * d_gates
    shared = shared[0] + shared[1] + shared[2] + shared[3]
    d_routed = gates_here * (d_gates - shared)
    d_logits = jnp.sum(jnp.where(picked_here, d_routed[:, None, :], 0.0), axis=0)
    grad_router, d_normed_here, grad_norm_moe, along = route_back(
        normed_two, d_logits, router_t, after, rstd_two, gain_moe[None], d_got
    )
    grad_router, grad_norm_moe = grad_router.T, grad_norm_moe.reshape(HALF)
    d_scaled = d_normed_here * gain_moe
    along = along.reshape(256)
    along = (along + other_core(along))[:, None] / D
    d_after = f32(cot_here) + rstd_two * (d_scaled - after_hat * along)

    d_attn = jnp.concatenate(y_gather(bf16(d_after)))
    moe_sum, d_attn = lax.optimization_barrier((moe_sum, d_attn))
    moe_here = ring_scatter(moe_sum)
    d_att, d_other = heads_product(d_attn, out_w)
    d_att = bf16(d_att + other_core(d_other))
    d_att, expert_grads[0] = lax.optimization_barrier((d_att, expert_grads[0]))
    d_query, d_key, d_value = attend_back(d_att, *heads, cosine, sine)
    d_query, d_attn = lax.optimization_barrier((d_query, d_attn))
    grad_out = out_grad(attended, d_attn)
    along, grad_query_gain, grad_key_gain = along_sums(
        d_query, d_key, qkv, rstd_q, rstd_k, gain_query, gain_key
    )
    grad_query_gain, grad_key_gain = grad_query_gain.reshape(256), grad_key_gain.reshape(256)
    along = ring_sum(along.reshape(2, 8, 1024)[:, 0], y)[:, :, None] / D
    along, moe_here = lax.optimization_barrier((along, moe_here))
    d_qkv, d_par, d_own, grad_norm_attn = spread(
        d_query, d_key, d_value, qkv, rstd_q, rstd_k, along[0], along[1],
        gain_query, gain_key, x_all, rstd_one, qkv_w,
    )
    grad_norm_attn = grad_norm_attn.reshape(D)
    received = other_core(d_par)
    received, d_qkv = lax.optimization_barrier((received, d_qkv))
    d_sent = bf16(d_own + f32(received))
    got = y_scatter([d_sent[s * 256 : s * 256 + 256] for s in range(4)])
    grad_qkv = outer(x_all, rstd_one, gain_attn.reshape(1, D), d_qkv)
    got, moe_here = lax.optimization_barrier((got, moe_here))
    layer_output = from_half(bf16(after + moe_here), zh, c)[None]
    hat_here = x_here * rstd_one[:256]
    d_normed_one, along = back_sums(x_all, rstd_one, gain_attn[:1], got)
    along = along.reshape(256)
    along = (along + other_core(along))[:, None] / D
    grad_tokens = bf16(d_after + rstd_one[:256] * (d_normed_one - hat_here * along))

    wide = jnp.concatenate([grad_norm_moe[:, None], grad_router], axis=1)
    wide = jnp.pad(wide, ((0, HALF), (0, 0)))
    extras = jnp.concatenate([grad_norm_attn[:, None], wide], axis=1).reshape(2, HALF, 18)
    extras = jnp.where(own_first, extras, extras[::-1]).reshape(2, 4, 2, 4, 2, 16, 18)
    gains = jnp.stack([grad_query_gain, grad_key_gain], axis=1)
    at_home = jnp.arange(8)[:, None, None] == head_block
    gains = jnp.where(at_home, gains[None], 0.0).reshape(4, 2, 2, 4, 2, 16, 2)
    extras = jnp.concatenate(
        [extras.transpose(2, 0, 3, 1, 4, 5, 6), gains.transpose(1, 2, 3, 0, 4, 5, 6)], axis=-1
    )
    coarse = bf16(extras)
    extras = jnp.concatenate([coarse, bf16(extras - f32(coarse))], axis=-1)
    extras = jnp.pad(extras, ((0, 0),) * 6 + ((0, 88),))
    both = grad_qkv.reshape(2, HALF, 768)
    both = jnp.where(own_first, both, both[::-1]).reshape(2, 4, 2, 4, 2, 16, 768)
    both = both.transpose(2, 0, 3, 1, 4, 5, 6)
    both = jnp.concatenate([both, extras], axis=-1).reshape(16, 128, 896)
    grad_out = grad_out.reshape(2, 256, HALF)
    grad_out = jnp.where(own_first, grad_out, grad_out[::-1]).reshape(16, 32, 4, 256)
    grad_out = grad_out.transpose(0, 2, 1, 3).reshape(16, 128, 256)
    both = jnp.concatenate([both, grad_out], axis=2).reshape(D, 1152)
    both, expert_grads, got = lax.optimization_barrier((both, expert_grads, got))
    both = lax.psum_scatter(both, plane, scatter_dimension=0, tiled=True)
    grad_out = both[:, 896:].reshape(4, 32, 256).transpose(1, 0, 2).reshape(32, HALF)
    both = f32(trade(both[:, :896].reshape(8, 16, 896), y, c))
    grad_w_qkv = both[:, :, :768].reshape(8, 16, 3, 256).transpose(1, 2, 0, 3).reshape(16, 3 * D)
    smalls = jnp.sum(both[:, :, 768:788] + both[:, :, 788:808], axis=0)

    out_own = jnp.where(own_first, grad_out[:16], grad_out[16:])
    out_par = other_core(jnp.where(own_first, grad_out[16:], grad_out[:16]))
    grad_w_out = jnp.where(own_first, join_halves(out_own, out_par), join_halves(out_par, out_own))
    grad_w_out = f32(grad_w_out)

    grad_gate_up, grad_down = unpack_experts(*expert_grads)
    return (
        layer_output,
        from_half(grad_tokens, zh, c)[None],
        grad_w_qkv,
        grad_w_out,
        smalls[:, 2:18],
        smalls[:, 0],
        smalls[:, 1],
        smalls[:, 18],
        smalls[:, 19],
        grad_gate_up,
        grad_down,
    )


def solution(mesh):
    fine = Mesh(mesh.devices.reshape(4, 2, 2, 4, 2), ("y", "zh", "zl", "x", "c"))
    ctx, fsdp = ("y", "zh"), ("zl", "x", "c")
    rows, blocks, line = P(ctx + fsdp, None), P(fsdp, ctx, None), P(ctx + fsdp)
    gate_up, down = P(ctx, fsdp, None), P(ctx, None, fsdp)
    return jax.shard_map(
        on_device,
        mesh=fine,
        in_specs=(blocks, blocks, rows, rows, rows, line, line, line, line, gate_up, down)
        + (P(fsdp, None, None), P(fsdp, ctx)),
        out_specs=(blocks, blocks, rows, rows, rows, line, line, line, line, gate_up, down),
        check_vma=False,
    )
```

```python
import jax
import jax.numpy as jnp
import numpy as np
from jax import lax
from jax.experimental import pallas as pl
from jax.experimental.pallas import tpu as pltpu
from jax.sharding import Mesh, PartitionSpec as P

D = 2048
HALF = 1024
HEAD_DIM = 128
FF = 1024
CAP = 384
ROWS = 128
SCALE = HEAD_DIM**-0.5

epsilon = 1e-06
rope_base = 10000.0


def f32(a):
    return a.astype(jnp.float32)


def bf16(a):
    return a.astype(jnp.bfloat16)


def dot(a, b):
    return jnp.dot(a, b, preferred_element_type=jnp.float32)


def dot_t(a, b):
    return lax.dot_general(a, b, (((1,), (1,)), ((), ())), preferred_element_type=jnp.float32)


def t_dot(a, b):
    return lax.dot_general(a, b, (((0,), (0,)), ((), ())), preferred_element_type=jnp.float32)


def other_core(a):
    return lax.ppermute(a, "c", [(0, 1), (1, 0)])


def from_chip(a, step):
    return lax.ppermute(a, "y", [(i, (i + step) % 4) for i in range(4)])


def y_gather(a):
    return [a] + [from_chip(a, step) for step in (1, 2, 3)]


def y_scatter(parts):
    return [parts[0]] + [from_chip(parts[step], 4 - step) for step in (1, 2, 3)]


def by_distance(a, y):
    place = (y - jnp.arange(4)) % 4
    hit = place[:, None] == jnp.arange(4)[None, :]
    return jnp.sum(jnp.where(hit[None, :, :, None], a[:, None], jnp.zeros((), a.dtype)), axis=2)


def chosen(a, place):
    hit = place[:, None] == jnp.arange(4)[None, :]
    hit = hit.reshape(4, 4, *[1] * (a.ndim - 1))
    return jnp.sum(jnp.where(hit, a[None], jnp.zeros((), a.dtype)), axis=1)


def trade(pieces, y, c):
    pairs = pieces.reshape(4, 2, *pieces.shape[1:])
    mine = jnp.where(c == 0, pairs[:, 0], pairs[:, 1])
    theirs = jnp.where(c == 0, pairs[:, 1], pairs[:, 0])
    got = other_core(theirs)
    both = jnp.where(c == 0, jnp.stack([mine, got], 1), jnp.stack([got, mine], 1))
    both = chosen(both, (y + jnp.arange(4)) % 4)
    got = jnp.stack([both[0]] + [from_chip(both[step], step) for step in (1, 2, 3)])
    return chosen(got, (y - jnp.arange(4)) % 4).reshape(pieces.shape)


def ring_sum(a, y):
    n = a.shape[0]
    a = a + other_core(a)
    a = by_distance(a.reshape(n, 4, 256), y)
    a = a + from_chip(a, 1) + from_chip(a, 2) + from_chip(a, 3)
    return by_distance(a, y).reshape(n, 1024)


def angle_tables():
    frequency = rope_base ** (-2.0 * np.arange(64) / HEAD_DIM)
    blocks = np.arange(8)[:, None] * ROWS * frequency[None]
    rows = np.arange(ROWS)[:, None] * frequency[None]
    tables = (np.cos(blocks), np.sin(blocks), np.cos(rows), np.sin(rows))
    return [jnp.asarray(table, jnp.float32) for table in tables]


def plane_sum(a, z, x):
    def summed(b, dim, axes, me):
        parts = []
        for step in range(4):
            part = lax.dynamic_index_in_dim(b, (me + step) % 4, dim, keepdims=False)
            if step:
                part = lax.ppermute(part, axes, [(i, (i + step) % 4) for i in range(4)])
            parts.append(f32(part))
        return bf16(((parts[0] + parts[1]) + parts[2]) + parts[3])

    depth = ("zh", "zl")
    low, high = summed(a[:, :, :64], 1, "x", x), summed(a[:, :, 64:], 0, depth, z)
    low, high = summed(low, 0, depth, z), summed(high, 0, "x", x)
    return jnp.concatenate([low, high])


def split_halves(a):
    blocks = [a[..., k * 128 : k * 128 + 128] for k in range(a.shape[-1] // 128)]
    return jnp.concatenate(blocks[0::2], axis=-1), jnp.concatenate(blocks[1::2], axis=-1)


def join_halves(low, high):
    blocks = []
    for k in range(low.shape[-1] // 128):
        blocks += [low[..., k * 128 : k * 128 + 128], high[..., k * 128 : k * 128 + 128]]
    return jnp.concatenate(blocks, axis=-1)


def other_layer(a):
    return lax.ppermute(a, "zh", [(0, 1), (1, 0)])


def to_half(low, high, zh, c):
    mine = jnp.where(c == 0, low, high)
    got = other_core(jnp.where(c == 0, high, low))
    keep = jnp.where(zh == c, mine, got)
    got = other_layer(jnp.where(zh == c, got, mine))
    return jnp.where(zh == 0, keep, got), jnp.where(zh == 0, got, keep)


def from_half(a, zh, c):
    first, second = a[:ROWS], a[ROWS:]
    mine = jnp.where(zh == 0, first, second)
    got = other_layer(jnp.where(zh == 0, second, first))
    keep = jnp.where(zh == c, mine, got)
    got = other_core(jnp.where(zh == c, got, mine))
    return join_halves(jnp.where(c == 0, keep, got), jnp.where(c == 0, got, keep))


def roped(values, cosine, sine):
    return values * cosine + pltpu.roll(values, 64, 1) * sine


def project_kernel(*refs):
    own, par = refs[:4], refs[4:8]
    gain, weights, qkv, tokens, rstd, squares = refs[8:]
    for s in range(4):

        @pl.when(pl.program_id(0) == s)
        def _():
            first, second = own[s][...].astype(jnp.float32), par[s][...].astype(jnp.float32)
            tokens[:, pl.ds(0, HALF)] = own[s][...]
            tokens[:, pl.ds(HALF, HALF)] = par[s][...]
            total = jnp.sum(first * first, axis=1, keepdims=True)
            total = total + jnp.sum(second * second, axis=1, keepdims=True)
            scale = lax.rsqrt(total * (1.0 / D) + epsilon)
            rstd[...] = scale
            first = (first * scale * gain[pl.ds(0, 1), :]).astype(jnp.bfloat16)
            second = (second * scale * gain[pl.ds(1, 1), :]).astype(jnp.bfloat16)
            out = dot(first, weights[pl.ds(0, HALF), :])
            out = out + dot(second, weights[pl.ds(HALF, HALF), :])
            qkv[...] = out
            ones = jnp.ones((8, 256), jnp.bfloat16)
            for k in range(2):
                part = out[:, k * 256 : k * 256 + 256]
                part = part * part
                coarse = part.astype(jnp.bfloat16)
                fine = (part - coarse.astype(jnp.float32)).astype(jnp.bfloat16)
                squares[pl.ds(k * 8, 8), :] = dot_t(ones, coarse) + dot_t(ones, fine)


def project(own, par, gain, weights):
    whole = pl.BlockSpec((256, HALF), lambda s: (0, 0))
    rows = lambda n: pl.BlockSpec((256, n), lambda s: (s, 0))
    return pl.pallas_call(
        project_kernel,
        grid=(4,),
        in_specs=[whole] * 8
        + [pl.BlockSpec((2, HALF), lambda s: (0, 0)), pl.BlockSpec((D, 768), lambda s: (0, 0))],
        out_specs=[
            rows(768),
            rows(D),
            rows(1),
            pl.BlockSpec((16, 256), lambda s: (0, s)),
        ],
        out_shape=[
            jax.ShapeDtypeStruct((1024, 768), jnp.float32),
            jax.ShapeDtypeStruct((1024, D), jnp.bfloat16),
            jax.ShapeDtypeStruct((1024, 1), jnp.float32),
            jax.ShapeDtypeStruct((16, 1024), jnp.float32),
        ],
        compiler_params=pltpu.CompilerParams(vmem_limit_bytes=VMEM_LIMIT),
        cost_estimate=pl.CostEstimate(
            flops=2 * 1024 * D * 768, bytes_accessed=20 << 20, transcendentals=0
        ),
    )(*own, *par, gain, weights)


def spread_kernel(
    d_q, d_k, d_v, q_pre, k_pre, rstd_q, rstd_k, along_q, along_k, gain_q, gain_k, tokens, rstd,
    weights, d_qkv, d_par, d_own, d_gain,
):
    @pl.when(pl.program_id(0) == 0)
    def _():
        d_gain[...] = jnp.zeros_like(d_gain)

    sides = (
        (d_q, q_pre, rstd_q, along_q, gain_q),
        (d_k, k_pre, rstd_k, along_k, gain_k),
    )
    for k, (grad, pre, scale, along, gain) in enumerate(sides):
        hat = pre[...] * scale[...]
        part = scale[...] * (grad[...] * gain[...] - hat * along[...])
        d_qkv[:, pl.ds(k * 256, 256)] = part.astype(jnp.bfloat16)
    d_qkv[:, pl.ds(512, 256)] = d_v[0]
    low = d_qkv[...]
    for k, out in ((1, d_par), (0, d_own)):
        at = pl.ds(k * HALF, HALF)
        part = dot_t(low, weights[at, :])
        out[...] = part.astype(out.dtype)
        hat = tokens[:, at].astype(jnp.float32) * rstd[...]
        d_gain[:, at] += jnp.sum(part * hat, axis=0, keepdims=True)


def spread(d_q, d_k, d_v, qkv, rstd_q, rstd_k, along_q, along_k, gain_q, gain_k, tokens, rstd, w):
    rows = lambda n, k=0: pl.BlockSpec((256, n), lambda s: (s, k))
    line = pl.BlockSpec((1, 256), lambda s: (0, 0))
    return pl.pallas_call(
        spread_kernel,
        grid=(4,),
        in_specs=[
            rows(256),
            rows(256),
            pl.BlockSpec((1, 256, 256), lambda s: (s, 0, 0)),
            rows(256),
            rows(256, 1),
            rows(1),
            rows(1),
            rows(1),
            rows(1),
            line,
            line,
            rows(D),
            rows(1),
            pl.BlockSpec((D, 768), lambda s: (0, 0)),
        ],
        out_specs=[rows(768), rows(HALF), rows(HALF), pl.BlockSpec((1, D), lambda s: (0, 0))],
        out_shape=[
            jax.ShapeDtypeStruct((1024, 768), jnp.bfloat16),
            jax.ShapeDtypeStruct((1024, HALF), jnp.bfloat16),
            jax.ShapeDtypeStruct((1024, HALF), jnp.float32),
            jax.ShapeDtypeStruct((1, D), jnp.float32),
        ],
        compiler_params=pltpu.CompilerParams(vmem_limit_bytes=VMEM_LIMIT),
        cost_estimate=pl.CostEstimate(
            flops=2 * 1024 * D * 768, bytes_accessed=20 << 20, transcendentals=0
        ),
    )(
        d_q, d_k, d_v, qkv, qkv, rstd_q, rstd_k, along_q, along_k,
        gain_q[None], gain_k[None], tokens, rstd, w,
    )


def whole_spec(*shape):
    return pl.BlockSpec(shape, lambda *_: (0,) * len(shape))


def params(flops, data):
    return dict(
        compiler_params=pltpu.CompilerParams(vmem_limit_bytes=VMEM_LIMIT),
        cost_estimate=pl.CostEstimate(flops=flops, bytes_accessed=data, transcendentals=0),
    )


def output_kernel(attended, weights, parts, own):
    out = dot(attended[...], weights[...])
    parts[0] = out.astype(jnp.bfloat16)

    @pl.when(pl.program_id(0) == 0)
    def _():
        own[...] = out


def output_product(attended, weights):
    return pl.pallas_call(
        output_kernel,
        grid=(4,),
        in_specs=[pl.BlockSpec((256, 512), lambda s: (s, 0)), whole_spec(512, HALF)],
        out_specs=[pl.BlockSpec((1, 256, HALF), lambda s: (s, 0, 0)), whole_spec(256, HALF)],
        out_shape=[
            jax.ShapeDtypeStruct((4, 256, HALF), jnp.bfloat16),
            jax.ShapeDtypeStruct((256, HALF), jnp.float32),
        ],
        **params(1 << 30, 5 << 20),
    )(attended, weights)


def residual_kernel(tokens, own, first, second, third, after, square):
    total = tokens[...].astype(jnp.float32) + own[...]
    for part in (first, second, third):
        total = total + part[...].astype(jnp.float32)
    after[...] = total
    square[...] = jnp.sum(total * total, axis=1, keepdims=True)


def residual(tokens, own, got):
    rows = whole_spec(256, HALF)
    return pl.pallas_call(
        residual_kernel,
        grid=(1,),
        in_specs=[rows] * 5,
        out_specs=[rows, whole_spec(256, 1)],
        out_shape=[
            jax.ShapeDtypeStruct((256, HALF), jnp.float32),
            jax.ShapeDtypeStruct((256, 1), jnp.float32),
        ],
        **params(1 << 20, 5 << 20),
    )(tokens, own, *got)


def logits_kernel(router_t, normed, out):
    out[...] = dot_t(router_t[...], normed[...])


def logits_of(router_t, normed):
    return pl.pallas_call(
        logits_kernel,
        grid=(1,),
        in_specs=[whole_spec(16, HALF), whole_spec(1024, HALF)],
        out_specs=whole_spec(16, 1024),
        out_shape=jax.ShapeDtypeStruct((16, 1024), jnp.float32),
        **params(1 << 25, 2 << 20),
    )(router_t, normed)


def route_back_kernel(
    normed, d_logits, router_t, after, rstd, gain, *refs
):
    got, (grad, d_normed, d_gain, along) = refs[:4], refs[4:]
    coarse = d_logits[...].astype(jnp.bfloat16)
    fine = (d_logits[...] - coarse.astype(jnp.float32)).astype(jnp.bfloat16)
    grad[...] = dot(coarse, normed[...]) + dot(fine, normed[...])
    total = got[0][...].astype(jnp.float32)
    for part in got[1:]:
        total = total + part[...].astype(jnp.float32)
    total = total + (t_dot(coarse, router_t[...]) + t_dot(fine, router_t[...]))
    d_normed[...] = total
    hat = after[...] * rstd[...]
    d_gain[...] = jnp.sum(total * hat, axis=0, keepdims=True)
    along[...] = jnp.sum(total * gain[...] * hat, axis=1, keepdims=True)


def route_back(normed, d_logits, router_t, after, rstd, gain, got):
    rows = whole_spec(256, HALF)
    return pl.pallas_call(
        route_back_kernel,
        grid=(1,),
        in_specs=[
            rows,
            whole_spec(16, 256),
            whole_spec(16, HALF),
            rows,
            whole_spec(256, 1),
            whole_spec(1, HALF),
            rows,
            rows,
            rows,
            rows,
        ],
        out_specs=[whole_spec(16, HALF), rows, whole_spec(1, HALF), whole_spec(256, 1)],
        out_shape=[
            jax.ShapeDtypeStruct((16, HALF), jnp.float32),
            jax.ShapeDtypeStruct((256, HALF), jnp.float32),
            jax.ShapeDtypeStruct((1, HALF), jnp.float32),
            jax.ShapeDtypeStruct((256, 1), jnp.float32),
        ],
        **params(1 << 25, 6 << 20),
    )(normed, d_logits, router_t, after, rstd, gain, *got)


def back_kernel(tokens, rstd, gain, first, second, third, fourth, d_normed, along):
    total = first[...].astype(jnp.float32)
    for part in (second, third, fourth):
        total = total + part[...].astype(jnp.float32)
    total = total * gain[...]
    d_normed[...] = total
    hat = tokens[...].astype(jnp.float32) * rstd[...]
    along[...] = jnp.sum(total * hat, axis=1, keepdims=True)


def back_sums(tokens, rstd, gain, got):
    rows = whole_spec(256, HALF)
    return pl.pallas_call(
        back_kernel,
        grid=(1,),
        in_specs=[rows, whole_spec(256, 1), whole_spec(1, HALF)] + [rows] * 4,
        out_specs=[rows, whole_spec(256, 1)],
        out_shape=[
            jax.ShapeDtypeStruct((256, HALF), jnp.float32),
            jax.ShapeDtypeStruct((256, 1), jnp.float32),
        ],
        **params(1 << 20, 5 << 20),
    )(tokens, rstd, gain, *got)


def out_grad_kernel(attended, d_attn, out, total):
    @pl.when(pl.program_id(0) == 0)
    def _():
        total[...] = jnp.zeros_like(total)

    total[...] += t_dot(attended[...], d_attn[...])

    @pl.when(pl.program_id(0) == 3)
    def _():
        out[...] = total[...].astype(jnp.bfloat16)


def out_grad(attended, d_attn):
    rows = lambda n: pl.BlockSpec((256, n), lambda s: (s, 0))
    return pl.pallas_call(
        out_grad_kernel,
        grid=(4,),
        in_specs=[rows(512), rows(HALF)],
        out_specs=whole_spec(512, HALF),
        out_shape=jax.ShapeDtypeStruct((512, HALF), jnp.bfloat16),
        scratch_shapes=[pltpu.VMEM((512, HALF), jnp.float32)],
        **params(1 << 30, 5 << 20),
    )(attended, d_attn)


def heads_kernel(d_attn, weights, own, par):
    own[...] = dot_t(d_attn[...], weights[pl.ds(0, 256), :])
    par[...] = dot_t(d_attn[...], weights[pl.ds(256, 256), :])


def heads_product(d_attn, weights):
    rows = lambda n: pl.BlockSpec((256, n), lambda s: (s, 0))
    return pl.pallas_call(
        heads_kernel,
        grid=(4,),
        in_specs=[rows(HALF), whole_spec(512, HALF)],
        out_specs=[rows(256), rows(256)],
        out_shape=[jax.ShapeDtypeStruct((1024, 256), jnp.float32)] * 2,
        **params(1 << 30, 5 << 20),
    )(d_attn, weights)


def along_kernel(
    d_q, d_k, q_pre, k_pre, rstd_q, rstd_k, gain_q, gain_k, along, d_gain_q, d_gain_k
):
    @pl.when(pl.program_id(0) == 0)
    def _():
        d_gain_q[...] = jnp.zeros_like(d_gain_q)
        d_gain_k[...] = jnp.zeros_like(d_gain_k)

    ones = jnp.ones((8, 256), jnp.bfloat16)
    sides = ((d_q, q_pre, rstd_q, gain_q, d_gain_q), (d_k, k_pre, rstd_k, gain_k, d_gain_k))
    for k, (grad, pre, scale, gain, d_gain) in enumerate(sides):
        part = grad[...] * (pre[...] * scale[...])
        d_gain[...] += jnp.sum(part, axis=0, keepdims=True)
        part = part * gain[...]
        coarse = part.astype(jnp.bfloat16)
        part = part - coarse.astype(jnp.float32)
        fine = part.astype(jnp.bfloat16)
        along[pl.ds(k * 8, 8), :] = dot_t(ones, coarse) + dot_t(ones, fine)


def along_sums(d_q, d_k, qkv, rstd_q, rstd_k, gain_q, gain_k):
    rows = lambda n, k=0: pl.BlockSpec((256, n), lambda s: (s, k))
    line = whole_spec(1, 256)
    return pl.pallas_call(
        along_kernel,
        grid=(4,),
        in_specs=[rows(256), rows(256), rows(256), rows(256, 1), rows(1), rows(1), line, line],
        out_specs=[pl.BlockSpec((16, 256), lambda s: (0, s)), line, line],
        out_shape=[
            jax.ShapeDtypeStruct((16, 1024), jnp.float32),
            jax.ShapeDtypeStruct((1, 256), jnp.float32),
            jax.ShapeDtypeStruct((1, 256), jnp.float32),
        ],
        **params(1 << 22, 5 << 20),
    )(d_q, d_k, qkv, qkv, rstd_q, rstd_k, gain_q[None], gain_k[None])


def outer_kernel(tokens, rstd, gain, d_qkv, out, total):
    @pl.when(pl.program_id(0) == 0)
    def _():
        total[...] = jnp.zeros_like(total)

    low = d_qkv[...]
    for k in range(4):
        at = pl.ds(k * 512, 512)
        normed = tokens[:, at].astype(jnp.float32) * rstd[...] * gain[:, at]
        total[at, :] += dot(jnp.transpose(normed).astype(jnp.bfloat16), low)

    @pl.when(pl.program_id(0) == 3)
    def _():
        out[...] = total[...].astype(jnp.bfloat16)


def outer(tokens, rstd, gain, d_qkv):
    rows = lambda n: pl.BlockSpec((256, n), lambda s: (s, 0))
    return pl.pallas_call(
        outer_kernel,
        grid=(4,),
        in_specs=[rows(D), rows(1), pl.BlockSpec((1, D), lambda s: (0, 0)), rows(768)],
        out_specs=pl.BlockSpec((D, 768), lambda s: (0, 0)),
        out_shape=jax.ShapeDtypeStruct((D, 768), jnp.bfloat16),
        scratch_shapes=[pltpu.VMEM((D, 768), jnp.float32)],
        compiler_params=pltpu.CompilerParams(vmem_limit_bytes=VMEM_LIMIT),
        cost_estimate=pl.CostEstimate(
            flops=2 * 1024 * D * 768, bytes_accessed=16 << 20, transcendentals=0
        ),
    )(tokens, rstd, gain, d_qkv)


def attend_kernel(
    q_pre, k_pre, v_pre, rstd_q, rstd_k, gain_q, gain_k, cosine, sine,
    attended, q_out, k_out, v_out, total, v_t,
):
    i = pl.program_id(1)

    @pl.when(i == 0)
    def _():
        cos, sin = cosine[...], sine[...]
        q_out[0] = roped(q_pre[...] * rstd_q[...] * gain_q[0], cos, sin).astype(jnp.bfloat16)
        k_out[0] = roped(k_pre[...] * rstd_k[...] * gain_k[0], cos, sin).astype(jnp.bfloat16)
        v_out[0] = v_pre[...].astype(jnp.bfloat16)
        v_t[...] = jnp.transpose(v_pre[...]).astype(jnp.bfloat16)

    query = q_out[0, pl.ds(pl.multiple_of(i * SPAN, SPAN), SPAN), :]
    scores = dot_t(k_out[0], query) * SCALE
    most = jnp.max(scores, axis=0, keepdims=True)
    weights = jnp.exp(scores - most)
    mass = jnp.sum(weights, axis=0, keepdims=True)
    total[0] = most + jnp.log(mass)
    probs = (weights / mass).astype(jnp.bfloat16)
    attended[0] = jnp.transpose(dot(v_t[...], probs)).astype(jnp.bfloat16)


SPAN = 256


def attend(qkv, rstd_q, rstd_k, gain_q, gain_k, cosine, sine):
    column = pl.BlockSpec((1024, 1), lambda h, i: (0, 0))
    gain = pl.BlockSpec((1, 1, 128), lambda h, i: (h, 0, 0))
    table = pl.BlockSpec((1024, 128), lambda h, i: (0, 0))
    head = pl.BlockSpec((1, 1024, 128), lambda h, i: (h, 0, 0))
    head_shape = jax.ShapeDtypeStruct((2, 1024, 128), jnp.bfloat16)
    return pl.pallas_call(
        attend_kernel,
        grid=(2, 1024 // SPAN),
        in_specs=[
            pl.BlockSpec((1024, 128), lambda h, i: (0, h)),
            pl.BlockSpec((1024, 128), lambda h, i: (0, 2 + h)),
            pl.BlockSpec((1024, 128), lambda h, i: (0, 4 + h)),
            column,
            column,
            gain,
            gain,
            table,
            table,
        ],
        out_specs=[
            pl.BlockSpec((1, SPAN, 128), lambda h, i: (i, 0, h)),
            head,
            head,
            head,
            pl.BlockSpec((1, 1, SPAN), lambda h, i: (h, 0, i)),
        ],
        out_shape=[
            jax.ShapeDtypeStruct((1024 // SPAN, SPAN, 256), jnp.bfloat16),
            head_shape,
            head_shape,
            head_shape,
            jax.ShapeDtypeStruct((2, 1, 1024), jnp.float32),
        ],
        scratch_shapes=[pltpu.VMEM((128, 1024), jnp.bfloat16)],
        compiler_params=pltpu.CompilerParams(vmem_limit_bytes=VMEM_LIMIT),
        cost_estimate=pl.CostEstimate(
            flops=2 * 4 * 1024 * 1024 * 128, bytes_accessed=8 << 20, transcendentals=2 << 20
        ),
    )(
        qkv,
        qkv,
        qkv,
        rstd_q,
        rstd_k,
        gain_q.reshape(2, 1, 128),
        gain_k.reshape(2, 1, 128),
        cosine,
        sine,
    )


def attend_back_kernel(
    d_att, q, k, v, total, cosine, sine, d_q, d_k, d_v, k_t, k_acc, v_acc
):
    i = pl.program_id(1)

    @pl.when(i == 0)
    def _():
        k_t[...] = jnp.transpose(k[0].astype(jnp.float32)).astype(jnp.bfloat16)
        k_acc[...] = jnp.zeros_like(k_acc)
        v_acc[...] = jnp.zeros_like(v_acc)

    at = pl.ds(pl.multiple_of(i * SPAN, SPAN), SPAN)
    query = q[0, at, :]
    probs = jnp.exp(dot_t(k[0], query) * SCALE - total[0])
    d_probs = dot_t(v[0], d_att[...])
    spread = jnp.sum(probs * d_probs, axis=0, keepdims=True)
    d_scores = (probs * (d_probs - spread)).astype(jnp.bfloat16)
    v_acc[...] += dot(probs.astype(jnp.bfloat16), d_att[...])
    k_acc[...] += dot(d_scores, query)
    d_query = jnp.transpose(dot(k_t[...], d_scores)) * SCALE
    d_q[...] = roped(d_query, cosine[at, :], -sine[at, :])

    @pl.when(i == pl.num_programs(1) - 1)
    def _():
        d_k[...] = roped(k_acc[...] * SCALE, cosine[...], -sine[...])
        d_v[...] = v_acc[...].reshape(4, 256, 128).astype(jnp.bfloat16)


def attend_back(d_att, q, k, v, total, cosine, sine):
    table = pl.BlockSpec((1024, 128), lambda h, i: (0, 0))
    head = pl.BlockSpec((1, 1024, 128), lambda h, i: (h, 0, 0))
    columns = pl.BlockSpec((1024, 128), lambda h, i: (0, h))
    tile = pl.BlockSpec((SPAN, 128), lambda h, i: (i, h))
    return pl.pallas_call(
        attend_back_kernel,
        grid=(2, 1024 // SPAN),
        in_specs=[
            tile,
            head,
            head,
            head,
            pl.BlockSpec((1, 1, SPAN), lambda h, i: (h, 0, i)),
            table,
            table,
        ],
        out_specs=[tile, columns, pl.BlockSpec((4, 256, 128), lambda h, i: (0, 0, h))],
        out_shape=[
            jax.ShapeDtypeStruct((1024, 256), jnp.float32),
            jax.ShapeDtypeStruct((1024, 256), jnp.float32),
            jax.ShapeDtypeStruct((4, 256, 256), jnp.bfloat16),
        ],
        scratch_shapes=[
            pltpu.VMEM((128, 1024), jnp.bfloat16),
            pltpu.VMEM((1024, 128), jnp.float32),
            pltpu.VMEM((1024, 128), jnp.float32),
        ],
        compiler_params=pltpu.CompilerParams(vmem_limit_bytes=VMEM_LIMIT),
        cost_estimate=pl.CostEstimate(
            flops=2 * 10 * 1024 * 1024 * 128, bytes_accessed=8 << 20, transcendentals=2 << 20
        ),
    )(d_att, q, k, v, total, cosine, sine)


CHUNKS = 2
PART = FF // CHUNKS
WIDE = 3 * PART
VMEM_LIMIT = 58 * 1024 * 1024


def pack_kernel(gate_up, down, out):
    down_t = jnp.transpose(down[0].astype(jnp.float32)).astype(jnp.bfloat16)
    for f in range(CHUNKS):
        out[0, :, pl.ds(f * WIDE, PART)] = gate_up[0, :, pl.ds(f * PART, PART)]
        out[0, :, pl.ds(f * WIDE + PART, PART)] = gate_up[0, :, pl.ds(FF + f * PART, PART)]
        out[0, :, pl.ds(f * WIDE + 2 * PART, PART)] = down_t[:, f * PART : (f + 1) * PART]


def pack_experts(gate_up, down):
    return pl.pallas_call(
        pack_kernel,
        grid=(2,),
        in_specs=[
            pl.BlockSpec((1, 128, 2 * FF), lambda m: (m, 0, 0)),
            pl.BlockSpec((1, FF, 128), lambda m: (m, 0, 0)),
        ],
        out_specs=pl.BlockSpec((1, 128, 3 * FF), lambda m: (m, 0, 0)),
        out_shape=jax.ShapeDtypeStruct((2, 128, 3 * FF), jnp.bfloat16),
        compiler_params=pltpu.CompilerParams(vmem_limit_bytes=VMEM_LIMIT),
        cost_estimate=pl.CostEstimate(flops=0, bytes_accessed=4 << 20, transcendentals=0),
    )(gate_up, down)


def unpack_kernel(first, second, gate_up, down):
    for m, part in enumerate((first, second)):

        @pl.when(pl.program_id(0) == m)
        def _():
            for f in range(CHUNKS):
                at = f * WIDE
                gate_up[0, :, pl.ds(f * PART, PART)] = part[:, pl.ds(at, PART)].astype(jnp.float32)
                up = part[:, pl.ds(at + PART, PART)].astype(jnp.float32)
                gate_up[0, :, pl.ds(FF + f * PART, PART)] = up
                down_t = part[:, pl.ds(at + 2 * PART, PART)].astype(jnp.float32)
                down[0, pl.ds(f * PART, PART), :] = jnp.transpose(down_t)


def unpack_experts(first, second):
    whole = pl.BlockSpec((128, 3 * FF), lambda m: (0, 0))
    return pl.pallas_call(
        unpack_kernel,
        grid=(2,),
        in_specs=[whole, whole],
        out_specs=[
            pl.BlockSpec((1, 128, 2 * FF), lambda m: (m, 0, 0)),
            pl.BlockSpec((1, FF, 128), lambda m: (m, 0, 0)),
        ],
        out_shape=[
            jax.ShapeDtypeStruct((2, 128, 2 * FF), jnp.float32),
            jax.ShapeDtypeStruct((2, FF, 128), jnp.float32),
        ],
        compiler_params=pltpu.CompilerParams(vmem_limit_bytes=VMEM_LIMIT),
        cost_estimate=pl.CostEstimate(flops=0, bytes_accessed=4 << 20, transcendentals=0),
    )(first, second)


def turned(a):
    return jnp.transpose(a.astype(jnp.float32)).astype(jnp.bfloat16)


def open_kernel(
    seat, gate, normed, cot, weights,
    part, rows_t, d_out_t, cot_rows, pick_t, weight, rows, d_out,
):
    @pl.when(pl.program_id(1) == 0)
    def _():
        taken = lax.broadcasted_iota(jnp.int32, (CAP, 1024), 0) == seat[0]
        slot_weight = jnp.sum(jnp.where(taken, gate[0], 0.0), axis=1, keepdims=True)
        weight[0] = slot_weight
        pick = jnp.where(taken, 1.0, 0.0)
        pick_t[0] = turned(pick)
        pick = pick.astype(jnp.bfloat16)
        for at in range(0, HALF, 512):
            spot = pl.ds(at, 512)
            found = dot(pick, normed[:, spot])
            rows[:, spot] = found.astype(jnp.bfloat16)
            rows_t[0, spot, :] = turned(found)
            picked = dot(pick, cot[:, spot])
            cot_rows[0, :, spot] = picked.astype(jnp.bfloat16)
            picked = picked * slot_weight
            d_out[:, spot] = picked.astype(jnp.bfloat16)
            d_out_t[0, spot, :] = turned(picked)

    for k, left in enumerate((rows, rows, d_out)):
        at = pl.ds(k * PART, PART)
        part[0, :, at] = dot(left[...], weights[0, :, at]).astype(jnp.bfloat16)


def open_experts(seat, gate, normed, cot, weights):
    whole = pl.BlockSpec((1024, HALF), lambda h, f: (0, 0))
    line = pl.BlockSpec((1, 1, 1024), lambda h, f: (h, 0, 0))
    slot = pl.BlockSpec((1, CAP, HALF), lambda h, f: (h, 0, 0))
    slot_t = pl.BlockSpec((1, HALF, CAP), lambda h, f: (h, 0, 0))
    shape_t = jax.ShapeDtypeStruct((2, HALF, CAP), jnp.bfloat16)
    return pl.pallas_call(
        open_kernel,
        grid=(2, CHUNKS),
        in_specs=[
            line,
            line,
            whole,
            whole,
            pl.BlockSpec((1, HALF, WIDE), lambda h, f: (h, 0, f)),
        ],
        out_specs=[
            pl.BlockSpec((1, CAP, WIDE), lambda h, f: (h, 0, f)),
            slot_t,
            slot_t,
            slot,
            slot_t,
            pl.BlockSpec((1, CAP, 1), lambda h, f: (h, 0, 0)),
        ],
        out_shape=[
            jax.ShapeDtypeStruct((2, CAP, 3 * FF), jnp.bfloat16),
            shape_t,
            shape_t,
            jax.ShapeDtypeStruct((2, CAP, HALF), jnp.bfloat16),
            shape_t,
            jax.ShapeDtypeStruct((2, CAP, 1), jnp.float32),
        ],
        scratch_shapes=[pltpu.VMEM((CAP, HALF), jnp.bfloat16)] * 2,
        compiler_params=pltpu.CompilerParams(vmem_limit_bytes=VMEM_LIMIT),
        cost_estimate=pl.CostEstimate(
            flops=2 * 2 * CAP * 1024 * 5120, bytes_accessed=30 << 20, transcendentals=0
        ),
    )(seat, gate, normed, cot, weights)


def close_kernel(
    first, seat, own, received, rows_t, d_out_t, cot_rows, pick_t, weight, weights, *refs
):
    if first:
        moe, d_normed, grads, d_token, moe_acc, d_acc, out_acc, row_acc = refs
    else:
        moe_in, d_in, moe, d_normed, grads, d_token, moe_acc, d_acc, out_acc, row_acc = refs
    h, f = pl.program_id(0), pl.program_id(1)

    @pl.when((h == 0) & (f == 0))
    def _():
        if first:
            moe_acc[...] = jnp.zeros_like(moe_acc)
            d_acc[...] = jnp.zeros_like(d_acc)
        else:
            for s in range(4):
                moe_acc[pl.ds(s * 256, 256), :] = moe_in[s].astype(jnp.float32)
                d_acc[pl.ds(s * 256, 256), :] = d_in[s].astype(jnp.float32)

    @pl.when(f == 0)
    def _():
        out_acc[...] = jnp.zeros_like(out_acc)
        row_acc[...] = jnp.zeros_like(row_acc)

    def both(k):
        at = pl.ds(k * PART, PART)
        return own[0, :, at].astype(jnp.float32) + received[0, :, at].astype(jnp.float32)

    gate, up, d_hidden = both(0), both(1), both(2)
    sig = jax.nn.sigmoid(gate)
    scaled = gate * sig
    hidden = (scaled * up).astype(jnp.bfloat16)
    d_gate = (d_hidden * up * sig * (1.0 + gate * (1.0 - sig))).astype(jnp.bfloat16)
    d_up = (d_hidden * scaled).astype(jnp.bfloat16)
    out_acc[...] += dot_t(hidden, weights[0, :, pl.ds(2 * PART, PART)])
    row_acc[...] += dot_t(d_gate, weights[0, :, pl.ds(0, PART)])
    row_acc[...] += dot_t(d_up, weights[0, :, pl.ds(PART, PART)])
    grads[0, :, pl.ds(0, PART)] = dot(rows_t[0], d_gate).astype(jnp.bfloat16)
    grads[0, :, pl.ds(PART, PART)] = dot(rows_t[0], d_up).astype(jnp.bfloat16)
    grads[0, :, pl.ds(2 * PART, PART)] = dot(d_out_t[0], hidden).astype(jnp.bfloat16)

    @pl.when(f == CHUNKS - 1)
    def _():
        d_weight = jnp.sum(out_acc[...] * cot_rows[0].astype(jnp.float32), axis=1, keepdims=True)
        taken = lax.broadcasted_iota(jnp.int32, (CAP, 1024), 0) == seat[0]
        d_token[0] = jnp.sum(jnp.where(taken, d_weight, 0.0), axis=0, keepdims=True)
        weighted = (weight[0] * out_acc[...]).astype(jnp.bfloat16)
        d_rows = row_acc[...].astype(jnp.bfloat16)
        for at in range(0, HALF, 512):
            spot = pl.ds(at, 512)
            moe_acc[:, spot] += dot(pick_t[0], weighted[:, at : at + 512])
            d_acc[:, spot] += dot(pick_t[0], d_rows[:, at : at + 512])

    @pl.when((h == 1) & (f == CHUNKS - 1))
    def _():
        for s in range(4):
            moe[s] = moe_acc[pl.ds(s * 256, 256), :].astype(moe.dtype)
            d_normed[s] = d_acc[pl.ds(s * 256, 256), :].astype(d_normed.dtype)


def close_experts(seat, own, received, state, weights, before):
    whole = pl.BlockSpec((4, 256, HALF), lambda h, f: (0, 0, 0))
    line = pl.BlockSpec((1, 1, 1024), lambda h, f: (h, 0, 0))
    slot = pl.BlockSpec((1, CAP, HALF), lambda h, f: (h, 0, 0))
    slot_t = pl.BlockSpec((1, HALF, CAP), lambda h, f: (h, 0, 0))
    part = pl.BlockSpec((1, CAP, WIDE), lambda h, f: (h, 0, f))
    wide = pl.BlockSpec((1, HALF, WIDE), lambda h, f: (h, 0, f))
    full = jax.ShapeDtypeStruct((4, 256, HALF), jnp.bfloat16)

    def body(*refs):
        close_kernel(not before, *refs)

    return pl.pallas_call(
        body,
        grid=(2, CHUNKS),
        in_specs=[
            line,
            part,
            part,
            slot_t,
            slot_t,
            slot,
            slot_t,
            pl.BlockSpec((1, CAP, 1), lambda h, f: (h, 0, 0)),
            wide,
        ]
        + [whole] * len(before),
        out_specs=[whole, whole, wide, line],
        out_shape=[
            full,
            full,
            jax.ShapeDtypeStruct((2, HALF, 3 * FF), jnp.bfloat16),
            jax.ShapeDtypeStruct((2, 1, 1024), jnp.float32),
        ],
        scratch_shapes=[
            pltpu.VMEM((1024, HALF), jnp.float32),
            pltpu.VMEM((1024, HALF), jnp.float32),
            pltpu.VMEM((CAP, HALF), jnp.float32),
            pltpu.VMEM((CAP, HALF), jnp.float32),
        ],
        compiler_params=pltpu.CompilerParams(vmem_limit_bytes=VMEM_LIMIT),
        cost_estimate=pl.CostEstimate(
            flops=2 * 2 * CAP * 1024 * 8192, bytes_accessed=50 << 20, transcendentals=2 * CAP * FF
        ),
    )(seat, own, received, *state, weights, *before)


def on_device(
    tokens,
    cotangent,
    w_qkv,
    w_out,
    w_router,
    norm_attn,
    norm_moe,
    query_gain,
    key_gain,
    w_gate_up,
    w_down,
    routes,
    block_order,
):
    y, zh, c = lax.axis_index("y"), lax.axis_index("zh"), lax.axis_index("c")
    plane = ("zh", "zl", "x")
    own_first = c == 0

    low, high = split_halves(tokens[0])
    low, high, w_qkv = lax.optimization_barrier((low, high, w_qkv))
    x_blocks = jnp.concatenate(to_half(low, high, zh, c))
    x_blocks, block_order, w_gate_up, cotangent, routes = lax.optimization_barrier(
        (x_blocks, block_order, w_gate_up, cotangent, routes)
    )
    x_own = y_gather(x_blocks)
    x_par = [other_core(part) for part in x_own]
    place = jnp.full((8, 128), block_order[0, 0], jnp.int32).astype(jnp.float32)
    places = y_gather(jnp.stack(to_half(place, place, zh, c)))
    places = jnp.stack(places)[:, :, 0, 0].reshape(8)

    pieces = w_qkv.reshape(16, 3, 8, 256).transpose(2, 0, 1, 3).reshape(8, 16, 768)
    small = jnp.concatenate(
        [norm_attn[:, None], norm_moe[:, None], w_router, query_gain[:, None], key_gain[:, None]],
        axis=1,
    )
    small = jnp.pad(small, ((0, 0), (0, 108)))
    pieces = jnp.concatenate([pieces, jnp.broadcast_to(small, (8, 16, 128))], axis=2)
    pieces = trade(pieces, y, c).reshape(128, 896)
    out_low, out_high = split_halves(w_out)
    out_par = other_core(jnp.where(own_first, out_high, out_low))
    out_own = jnp.where(own_first, out_low, out_high)
    out_both = jnp.where(
        own_first, jnp.concatenate([out_own, out_par]), jnp.concatenate([out_par, out_own])
    )
    out_both = out_both.reshape(32, 4, 256).transpose(1, 0, 2).reshape(128, 256)
    dense = jnp.concatenate([pieces, out_both], axis=1)
    dense, w_gate_up = lax.optimization_barrier((dense, w_gate_up))
    dense = lax.all_gather(dense, plane, axis=0, tiled=True).reshape(2, 2, 4, 4, 2, 16, 1152)

    expert_w = [
        lax.all_gather(part, plane, axis=0, tiled=True).reshape(2, HALF, 3 * FF)
        for part in pack_experts(w_gate_up, w_down)
    ]

    cot_low, cot_high = split_halves(cotangent[0])
    cot_here = jnp.concatenate(to_half(cot_low, cot_high, zh, c))
    cot_sent, x_own = lax.optimization_barrier((cot_here, x_own))
    cot_parts = y_gather(cot_sent)
    route_t = routes[0].T
    route_t = jnp.where(c == zh, route_t, other_core(route_t))
    route_t = by_distance(route_t.reshape(4, 4, 256), y).reshape(4, 1024)

    def rolled(a):
        a = a.transpose(1, 3, 0, 2, 4, 5, 6).reshape(2, HALF, -1)
        return jnp.where(own_first, a, a[::-1])

    qkv_w = rolled(dense[..., :768]).reshape(D, 768)
    small_all = dense[..., 768:788]
    small_rolled = f32(rolled(small_all))
    gain_attn = small_rolled[:, :, 0]
    gain_moe = small_rolled[0, :, 1]
    router_w = bf16(small_rolled[0, :, 2:18])
    small_true = f32(small_all[..., 18:20].transpose(3, 0, 1, 2, 4, 5, 6).reshape(8, 256, 2))
    head_block = y * 2 + c
    mine = lax.dynamic_index_in_dim(small_true, head_block, 0, keepdims=False)
    gain_query, gain_key = mine[:, 0], mine[:, 1]
    out_w = dense.reshape(16, 128, 1152)[:, :, 896:].reshape(16, 4, 32, 256)
    out_w = out_w.transpose(0, 2, 1, 3).reshape(2, 256, HALF)
    out_w = jnp.where(own_first, out_w, out_w[::-1]).reshape(512, HALF)

    qkv, x_all, rstd_one, squares = project(x_own, x_par, gain_attn, qkv_w)
    squares = squares.reshape(2, 8, 1024)[:, 0]
    rstd = lax.rsqrt(ring_sum(squares, y) / D + epsilon)
    rstd_q, rstd_k = rstd[0][:, None], rstd[1][:, None]
    here = places[:, None, None] == jnp.arange(8, dtype=jnp.float32)[None, :, None]
    block_cos, block_sin, row_cos, row_sin = angle_tables()
    block_cos = jnp.sum(jnp.where(here, block_cos, 0.0), axis=1)[:, None]
    block_sin = jnp.sum(jnp.where(here, block_sin, 0.0), axis=1)[:, None]
    cosine = block_cos * row_cos - block_sin * row_sin
    sine = block_sin * row_cos + block_cos * row_sin
    cosine = jnp.concatenate([cosine, cosine], axis=2).reshape(1024, 128)
    sine = jnp.concatenate([-sine, sine], axis=2).reshape(1024, 128)
    qkv, out_w, cosine, sine = lax.optimization_barrier((qkv, out_w, cosine, sine))
    attended, *heads = attend(qkv, rstd_q, rstd_k, gain_query, gain_key, cosine, sine)
    attended, cot_parts = lax.optimization_barrier(
        (attended.reshape(1024, 256), cot_parts)
    )
    cot_all = jnp.concatenate(cot_parts)
    attended = jnp.concatenate([attended, other_core(attended)], axis=1)
    out_parts, out_here = output_product(attended, out_w)
    got = [from_chip(out_parts[step], 4 - step) for step in (1, 2, 3)]
    x_here = f32(x_all[:256, :HALF])
    after, square = residual(x_all, out_here, got)

    square = square.reshape(256)
    rstd_two = lax.rsqrt((square + other_core(square)) / D + epsilon)[:, None]
    after_hat = after * rstd_two
    normed_two = bf16(after_hat * gain_moe)
    normed_all = jnp.concatenate(y_gather(normed_two))
    router_t = router_w.T
    logits = logits_of(router_t, normed_all)
    logits = logits + other_core(logits)
    picked = route_t[:, None, :] == jnp.arange(16, dtype=jnp.int32)[None, :, None]
    routed = jnp.sum(jnp.where(picked, logits[None], 0.0), axis=1)
    routed = jnp.exp(routed - jnp.max(routed, axis=0, keepdims=True))
    gates = routed / (routed[0] + routed[1] + routed[2] + routed[3])

    before, d_gates, expert_grads = (), jnp.zeros((4, 1024), jnp.float32), []
    for m in range(2):
        chosen = route_t[None] == y * 4 + jnp.arange(2, dtype=jnp.int32)[:, None, None] * 2 + m
        hit = jnp.sum(chosen.astype(jnp.int32), axis=1)
        rank = jnp.cumsum(hit, axis=1) - hit
        seat = jnp.where(hit > 0, rank, CAP)[:, None]
        gate_token = jnp.sum(jnp.where(chosen, gates[None], 0.0), axis=1)[:, None]
        seat, before = lax.optimization_barrier((seat, before))
        part, *state = open_experts(seat, gate_token, normed_all, cot_all, expert_w[m])
        moe_sum, d_normed, grads, d_token = close_experts(
            seat, part, other_core(part), state, expert_w[m], before
        )
        before = (moe_sum, d_normed)
        d_gates = d_gates + jnp.sum(jnp.where(chosen, d_token, 0.0), axis=0)
        expert_grads.append(
            lax.psum_scatter(grads.reshape(D, 3 * FF), plane, scatter_dimension=0, tiled=True)
        )

    def ring_scatter(a):
        a = a.reshape(4, 256, HALF)
        return sum(f32(g) for g in y_scatter([a[s] for s in range(4)]))

    d_got = y_scatter([d_normed[step] for step in range(4)])
    d_gates = d_gates.reshape(4, 4, 256)
    d_gates = sum(y_scatter([d_gates[:, s] for s in range(4)]))
    d_gates = d_gates + other_core(d_gates)

    gates_here, picked_here = gates[:, :256], picked[:, :, :256]
    shared = gates_here * d_gates
    shared = shared[0] + shared[1] + shared[2] + shared[3]
    d_routed = gates_here * (d_gates - shared)
    d_logits = jnp.sum(jnp.where(picked_here, d_routed[:, None, :], 0.0), axis=0)
    grad_router, d_normed_here, grad_norm_moe, along = route_back(
        normed_two, d_logits, router_t, after, rstd_two, gain_moe[None], d_got
    )
    grad_router, grad_norm_moe = grad_router.T, grad_norm_moe.reshape(HALF)
    d_scaled = d_normed_here * gain_moe
    along = along.reshape(256)
    along = (along + other_core(along))[:, None] / D
    d_after = f32(cot_here) + rstd_two * (d_scaled - after_hat * along)

    d_attn = jnp.concatenate(y_gather(bf16(d_after)))
    moe_sum, d_attn = lax.optimization_barrier((moe_sum, d_attn))
    moe_here = ring_scatter(moe_sum)
    d_att, d_other = heads_product(d_attn, out_w)
    d_att = bf16(d_att + other_core(d_other))
    d_att, expert_grads[0] = lax.optimization_barrier((d_att, expert_grads[0]))
    d_query, d_key, d_value = attend_back(d_att, *heads, cosine, sine)
    d_query, d_attn = lax.optimization_barrier((d_query, d_attn))
    grad_out = out_grad(attended, d_attn)
    along, grad_query_gain, grad_key_gain = along_sums(
        d_query, d_key, qkv, rstd_q, rstd_k, gain_query, gain_key
    )
    grad_query_gain, grad_key_gain = grad_query_gain.reshape(256), grad_key_gain.reshape(256)
    along = ring_sum(along.reshape(2, 8, 1024)[:, 0], y)[:, :, None] / D
    along, moe_here = lax.optimization_barrier((along, moe_here))
    d_qkv, d_par, d_own, grad_norm_attn = spread(
        d_query, d_key, d_value, qkv, rstd_q, rstd_k, along[0], along[1],
        gain_query, gain_key, x_all, rstd_one, qkv_w,
    )
    grad_norm_attn = grad_norm_attn.reshape(D)
    received = other_core(d_par)
    received, d_qkv = lax.optimization_barrier((received, d_qkv))
    d_sent = bf16(d_own + f32(received))
    got = y_scatter([d_sent[s * 256 : s * 256 + 256] for s in range(4)])
    grad_qkv = outer(x_all, rstd_one, gain_attn.reshape(1, D), d_qkv)
    got, moe_here, expert_grads[1] = lax.optimization_barrier((got, moe_here, expert_grads[1]))
    layer_output = from_half(bf16(after + moe_here), zh, c)[None]
    hat_here = x_here * rstd_one[:256]
    d_normed_one, along = back_sums(x_all, rstd_one, gain_attn[:1], got)
    along = along.reshape(256)
    along = (along + other_core(along))[:, None] / D
    grad_tokens = bf16(d_after + rstd_one[:256] * (d_normed_one - hat_here * along))

    wide = jnp.concatenate([grad_norm_moe[:, None], grad_router], axis=1)
    wide = jnp.pad(wide, ((0, HALF), (0, 0)))
    extras = jnp.concatenate([grad_norm_attn[:, None], wide], axis=1).reshape(2, HALF, 18)
    extras = jnp.where(own_first, extras, extras[::-1]).reshape(2, 4, 2, 4, 2, 16, 18)
    gains = jnp.stack([grad_query_gain, grad_key_gain], axis=1)
    at_home = jnp.arange(8)[:, None, None] == head_block
    gains = jnp.where(at_home, gains[None], 0.0).reshape(4, 2, 2, 4, 2, 16, 2)
    extras = jnp.concatenate(
        [extras.transpose(2, 0, 3, 1, 4, 5, 6), gains.transpose(1, 2, 3, 0, 4, 5, 6)], axis=-1
    )
    coarse = bf16(extras)
    extras = jnp.concatenate([coarse, bf16(extras - f32(coarse))], axis=-1)
    extras = jnp.pad(extras, ((0, 0),) * 6 + ((0, 88),))
    both = grad_qkv.reshape(2, HALF, 768)
    both = jnp.where(own_first, both, both[::-1]).reshape(2, 4, 2, 4, 2, 16, 768)
    both = both.transpose(2, 0, 3, 1, 4, 5, 6)
    both = jnp.concatenate([both, extras], axis=-1).reshape(16, 128, 896)
    grad_out = grad_out.reshape(2, 256, HALF)
    grad_out = jnp.where(own_first, grad_out, grad_out[::-1]).reshape(16, 32, 4, 256)
    grad_out = grad_out.transpose(0, 2, 1, 3).reshape(16, 128, 256)
    both = jnp.concatenate([both, grad_out], axis=2).reshape(D, 1152)
    both = plane_sum(both.reshape(4, 4, 128, 1152), zh * 2 + lax.axis_index("zl"), lax.axis_index("x"))
    grad_out = both[:, 896:].reshape(4, 32, 256).transpose(1, 0, 2).reshape(32, HALF)
    both = f32(trade(both[:, :896].reshape(8, 16, 896), y, c))
    grad_w_qkv = both[:, :, :768].reshape(8, 16, 3, 256).transpose(1, 2, 0, 3).reshape(16, 3 * D)
    smalls = jnp.sum(both[:, :, 768:788] + both[:, :, 788:808], axis=0)

    out_own = jnp.where(own_first, grad_out[:16], grad_out[16:])
    out_par = other_core(jnp.where(own_first, grad_out[16:], grad_out[:16]))
    grad_w_out = jnp.where(own_first, join_halves(out_own, out_par), join_halves(out_par, out_own))
    grad_w_out = f32(grad_w_out)

    grad_gate_up, grad_down = unpack_experts(*expert_grads)
    return (
        layer_output,
        from_half(grad_tokens, zh, c)[None],
        grad_w_qkv,
        grad_w_out,
        smalls[:, 2:18],
        smalls[:, 0],
        smalls[:, 1],
        smalls[:, 18],
        smalls[:, 19],
        grad_gate_up,
        grad_down,
    )


def solution(mesh):
    fine = Mesh(mesh.devices.reshape(4, 2, 2, 4, 2), ("y", "zh", "zl", "x", "c"))
    ctx, fsdp = ("y", "zh"), ("zl", "x", "c")
    rows, blocks, line = P(ctx + fsdp, None), P(fsdp, ctx, None), P(ctx + fsdp)
    gate_up, down = P(ctx, fsdp, None), P(ctx, None, fsdp)
    return jax.shard_map(
        on_device,
        mesh=fine,
        in_specs=(blocks, blocks, rows, rows, rows, line, line, line, line, gate_up, down)
        + (P(fsdp, None, None), P(fsdp, ctx)),
        out_specs=(blocks, blocks, rows, rows, rows, line, line, line, line, gate_up, down),
        check_vma=False,
    )
```

```python
import jax
import jax.numpy as jnp
import numpy as np
from jax import lax
from jax.experimental import pallas as pl
from jax.experimental.pallas import tpu as pltpu
from jax.sharding import Mesh, PartitionSpec as P

D = 2048
HALF = 1024
HEAD_DIM = 128
FF = 1024
CAP = 384
ROWS = 128
SCALE = HEAD_DIM**-0.5

epsilon = 1e-06
rope_base = 10000.0


def f32(a):
    return a.astype(jnp.float32)


def bf16(a):
    return a.astype(jnp.bfloat16)


def dot(a, b):
    return jnp.dot(a, b, preferred_element_type=jnp.float32)


def dot_t(a, b):
    return lax.dot_general(a, b, (((1,), (1,)), ((), ())), preferred_element_type=jnp.float32)


def t_dot(a, b):
    return lax.dot_general(a, b, (((0,), (0,)), ((), ())), preferred_element_type=jnp.float32)


def other_core(a):
    return lax.ppermute(a, "c", [(0, 1), (1, 0)])


def from_chip(a, step):
    return lax.ppermute(a, "y", [(i, (i + step) % 4) for i in range(4)])


def y_gather(a):
    return [a] + [from_chip(a, step) for step in (1, 2, 3)]


def y_scatter(parts):
    return [parts[0]] + [from_chip(parts[step], 4 - step) for step in (1, 2, 3)]


def by_distance(a, y):
    place = (y - jnp.arange(4)) % 4
    hit = place[:, None] == jnp.arange(4)[None, :]
    return jnp.sum(jnp.where(hit[None, :, :, None], a[:, None], jnp.zeros((), a.dtype)), axis=2)


def chosen(a, place):
    hit = place[:, None] == jnp.arange(4)[None, :]
    hit = hit.reshape(4, 4, *[1] * (a.ndim - 1))
    return jnp.sum(jnp.where(hit, a[None], jnp.zeros((), a.dtype)), axis=1)


def trade(pieces, y, c):
    pairs = pieces.reshape(4, 2, *pieces.shape[1:])
    mine = jnp.where(c == 0, pairs[:, 0], pairs[:, 1])
    theirs = jnp.where(c == 0, pairs[:, 1], pairs[:, 0])
    got = other_core(theirs)
    both = jnp.where(c == 0, jnp.stack([mine, got], 1), jnp.stack([got, mine], 1))
    both = chosen(both, (y + jnp.arange(4)) % 4)
    got = jnp.stack([both[0]] + [from_chip(both[step], step) for step in (1, 2, 3)])
    return chosen(got, (y - jnp.arange(4)) % 4).reshape(pieces.shape)


def ring_sum(a, y):
    n = a.shape[0]
    a = a + other_core(a)
    a = by_distance(a.reshape(n, 4, 256), y)
    a = a + from_chip(a, 1) + from_chip(a, 2) + from_chip(a, 3)
    return by_distance(a, y).reshape(n, 1024)


def angle_tables():
    frequency = rope_base ** (-2.0 * np.arange(64) / HEAD_DIM)
    blocks = np.arange(8)[:, None] * ROWS * frequency[None]
    rows = np.arange(ROWS)[:, None] * frequency[None]
    tables = (np.cos(blocks), np.sin(blocks), np.cos(rows), np.sin(rows))
    return [jnp.asarray(table, jnp.float32) for table in tables]


def plane_and_ring_sum(a, ring, z, x):
    depth = ("zh", "zl")

    def pieces(b, dim, me):
        return [
            lax.dynamic_index_in_dim(b, (me + step) % 4, dim, keepdims=False) for step in range(4)
        ]

    def moved(parts, axes):
        return [parts[0]] + [
            lax.ppermute(parts[step], axes, [(i, (i + step) % 4) for i in range(4)])
            for step in (1, 2, 3)
        ]

    def summed(parts):
        first, second, third, fourth = [f32(part) for part in parts]
        return bf16(((first + second) + third) + fourth)

    low, high = pieces(a[:, :, :64], 1, x), pieces(a[:, :, 64:], 0, z)
    low, high, ring = lax.optimization_barrier((low, high, ring))
    ring = y_scatter(ring)
    low, high = moved(low, "x"), moved(high, depth)
    low, high, ring = lax.optimization_barrier((low, high, ring))
    low, high = pieces(summed(low), 0, z), pieces(summed(high), 0, x)
    low, high = lax.optimization_barrier((low, high))
    return jnp.concatenate([summed(moved(low, depth)), summed(moved(high, "x"))]), ring


def split_halves(a):
    lead = a.shape[:-1]
    pairs = a.reshape(*lead, a.shape[-1] // 256, 2, 128)
    return pairs[..., 0, :].reshape(*lead, -1), pairs[..., 1, :].reshape(*lead, -1)


def join_halves(low, high):
    lead = low.shape[:-1]
    pairs = jnp.stack([low.reshape(*lead, -1, 128), high.reshape(*lead, -1, 128)], axis=-2)
    return pairs.reshape(*lead, -1)


def other_layer(a):
    return lax.ppermute(a, "zh", [(0, 1), (1, 0)])


def to_half(low, high, zh, c):
    mine = jnp.where(c == 0, low, high)
    got = other_core(jnp.where(c == 0, high, low))
    keep = jnp.where(zh == c, mine, got)
    got = other_layer(jnp.where(zh == c, got, mine))
    return jnp.where(zh == 0, keep, got), jnp.where(zh == 0, got, keep)


def from_half(a, zh, c):
    first, second = a[:ROWS], a[ROWS:]
    mine = jnp.where(zh == 0, first, second)
    got = other_layer(jnp.where(zh == 0, second, first))
    keep = jnp.where(zh == c, mine, got)
    got = other_core(jnp.where(zh == c, got, mine))
    return join_halves(jnp.where(c == 0, keep, got), jnp.where(c == 0, got, keep))


def roped(values, cosine, sine):
    return values * cosine + pltpu.roll(values, 64, 1) * sine


def project_kernel(*refs):
    own, par = refs[:4], refs[4:8]
    gain, weights, qkv, tokens, rstd, squares = refs[8:]
    for s in range(4):

        @pl.when(pl.program_id(0) == s)
        def _():
            first, second = own[s][...].astype(jnp.float32), par[s][...].astype(jnp.float32)
            tokens[:, pl.ds(0, HALF)] = own[s][...]
            tokens[:, pl.ds(HALF, HALF)] = par[s][...]
            total = jnp.sum(first * first, axis=1, keepdims=True)
            total = total + jnp.sum(second * second, axis=1, keepdims=True)
            scale = lax.rsqrt(total * (1.0 / D) + epsilon)
            rstd[...] = scale
            first = (first * scale * gain[pl.ds(0, 1), :]).astype(jnp.bfloat16)
            second = (second * scale * gain[pl.ds(1, 1), :]).astype(jnp.bfloat16)
            out = dot(first, weights[pl.ds(0, HALF), :])
            out = out + dot(second, weights[pl.ds(HALF, HALF), :])
            qkv[...] = out
            ones = jnp.ones((8, 256), jnp.bfloat16)
            for k in range(2):
                part = out[:, k * 256 : k * 256 + 256]
                part = part * part
                coarse = part.astype(jnp.bfloat16)
                fine = (part - coarse.astype(jnp.float32)).astype(jnp.bfloat16)
                squares[pl.ds(k * 8, 8), :] = dot_t(ones, coarse) + dot_t(ones, fine)


def project(own, par, gain, weights):
    whole = pl.BlockSpec((256, HALF), lambda s: (0, 0))
    rows = lambda n: pl.BlockSpec((256, n), lambda s: (s, 0))
    return pl.pallas_call(
        project_kernel,
        grid=(4,),
        in_specs=[whole] * 8
        + [pl.BlockSpec((2, HALF), lambda s: (0, 0)), pl.BlockSpec((D, 768), lambda s: (0, 0))],
        out_specs=[
            rows(768),
            rows(D),
            rows(1),
            pl.BlockSpec((16, 256), lambda s: (0, s)),
        ],
        out_shape=[
            jax.ShapeDtypeStruct((1024, 768), jnp.float32),
            jax.ShapeDtypeStruct((1024, D), jnp.bfloat16),
            jax.ShapeDtypeStruct((1024, 1), jnp.float32),
            jax.ShapeDtypeStruct((16, 1024), jnp.float32),
        ],
        compiler_params=pltpu.CompilerParams(vmem_limit_bytes=VMEM_LIMIT),
        cost_estimate=pl.CostEstimate(
            flops=2 * 1024 * D * 768, bytes_accessed=20 << 20, transcendentals=0
        ),
    )(*own, *par, gain, weights)


def spread_kernel(
    d_q, d_k, d_v, q_pre, k_pre, rstd_q, rstd_k, along_q, along_k, gain_q, gain_k, tokens, rstd,
    weights, d_qkv, d_par, d_own, d_gain,
):
    @pl.when(pl.program_id(0) == 0)
    def _():
        d_gain[...] = jnp.zeros_like(d_gain)

    sides = (
        (d_q, q_pre, rstd_q, along_q, gain_q),
        (d_k, k_pre, rstd_k, along_k, gain_k),
    )
    for k, (grad, pre, scale, along, gain) in enumerate(sides):
        hat = pre[...] * scale[...]
        part = scale[...] * (grad[...] * gain[...] - hat * along[...])
        d_qkv[:, pl.ds(k * 256, 256)] = part.astype(jnp.bfloat16)
    d_qkv[:, pl.ds(512, 256)] = d_v[0]
    low = d_qkv[...]
    for k, out in ((1, d_par), (0, d_own)):
        at = pl.ds(k * HALF, HALF)
        part = dot_t(low, weights[at, :])
        out[...] = part.astype(out.dtype)
        hat = tokens[:, at].astype(jnp.float32) * rstd[...]
        d_gain[:, at] += jnp.sum(part * hat, axis=0, keepdims=True)


def spread(d_q, d_k, d_v, qkv, rstd_q, rstd_k, along_q, along_k, gain_q, gain_k, tokens, rstd, w):
    rows = lambda n, k=0: pl.BlockSpec((256, n), lambda s: (s, k))
    line = pl.BlockSpec((1, 256), lambda s: (0, 0))
    return pl.pallas_call(
        spread_kernel,
        grid=(4,),
        in_specs=[
            rows(256),
            rows(256),
            pl.BlockSpec((1, 256, 256), lambda s: (s, 0, 0)),
            rows(256),
            rows(256, 1),
            rows(1),
            rows(1),
            rows(1),
            rows(1),
            line,
            line,
            rows(D),
            rows(1),
            pl.BlockSpec((D, 768), lambda s: (0, 0)),
        ],
        out_specs=[rows(768), rows(HALF), rows(HALF), pl.BlockSpec((1, D), lambda s: (0, 0))],
        out_shape=[
            jax.ShapeDtypeStruct((1024, 768), jnp.bfloat16),
            jax.ShapeDtypeStruct((1024, HALF), jnp.bfloat16),
            jax.ShapeDtypeStruct((1024, HALF), jnp.float32),
            jax.ShapeDtypeStruct((1, D), jnp.float32),
        ],
        compiler_params=pltpu.CompilerParams(vmem_limit_bytes=VMEM_LIMIT),
        cost_estimate=pl.CostEstimate(
            flops=2 * 1024 * D * 768, bytes_accessed=20 << 20, transcendentals=0
        ),
    )(
        d_q, d_k, d_v, qkv, qkv, rstd_q, rstd_k, along_q, along_k,
        gain_q[None], gain_k[None], tokens, rstd, w,
    )


def whole_spec(*shape):
    return pl.BlockSpec(shape, lambda *_: (0,) * len(shape))


def params(flops, data):
    return dict(
        compiler_params=pltpu.CompilerParams(vmem_limit_bytes=VMEM_LIMIT),
        cost_estimate=pl.CostEstimate(flops=flops, bytes_accessed=data, transcendentals=0),
    )


def output_kernel(attended, weights, parts, own):
    out = dot(attended[...], weights[...])
    parts[0] = out.astype(jnp.bfloat16)

    @pl.when(pl.program_id(0) == 0)
    def _():
        own[...] = out


def output_product(attended, weights):
    return pl.pallas_call(
        output_kernel,
        grid=(4,),
        in_specs=[pl.BlockSpec((256, 512), lambda s: (s, 0)), whole_spec(512, HALF)],
        out_specs=[pl.BlockSpec((1, 256, HALF), lambda s: (s, 0, 0)), whole_spec(256, HALF)],
        out_shape=[
            jax.ShapeDtypeStruct((4, 256, HALF), jnp.bfloat16),
            jax.ShapeDtypeStruct((256, HALF), jnp.float32),
        ],
        **params(1 << 30, 5 << 20),
    )(attended, weights)


def residual_kernel(tokens, own, first, second, third, after, square):
    total = tokens[...].astype(jnp.float32) + own[...]
    for part in (first, second, third):
        total = total + part[...].astype(jnp.float32)
    after[...] = total
    square[...] = jnp.sum(total * total, axis=1, keepdims=True)


def residual(tokens, own, got):
    rows = whole_spec(256, HALF)
    return pl.pallas_call(
        residual_kernel,
        grid=(1,),
        in_specs=[rows] * 5,
        out_specs=[rows, whole_spec(256, 1)],
        out_shape=[
            jax.ShapeDtypeStruct((256, HALF), jnp.float32),
            jax.ShapeDtypeStruct((256, 1), jnp.float32),
        ],
        **params(1 << 20, 5 << 20),
    )(tokens, own, *got)


def logits_kernel(router_t, normed, out):
    out[...] = dot_t(router_t[...], normed[...])


def logits_of(router_t, normed):
    return pl.pallas_call(
        logits_kernel,
        grid=(1,),
        in_specs=[whole_spec(16, HALF), whole_spec(1024, HALF)],
        out_specs=whole_spec(16, 1024),
        out_shape=jax.ShapeDtypeStruct((16, 1024), jnp.float32),
        **params(1 << 25, 2 << 20),
    )(router_t, normed)


def route_back_kernel(
    normed, d_logits, router_t, after, rstd, gain, *refs
):
    got, (grad, d_normed, d_gain, along) = refs[:4], refs[4:]
    coarse = d_logits[...].astype(jnp.bfloat16)
    fine = (d_logits[...] - coarse.astype(jnp.float32)).astype(jnp.bfloat16)
    grad[...] = dot(coarse, normed[...]) + dot(fine, normed[...])
    total = got[0][...].astype(jnp.float32)
    for part in got[1:]:
        total = total + part[...].astype(jnp.float32)
    total = total + (t_dot(coarse, router_t[...]) + t_dot(fine, router_t[...]))
    d_normed[...] = total
    hat = after[...] * rstd[...]
    d_gain[...] = jnp.sum(total * hat, axis=0, keepdims=True)
    along[...] = jnp.sum(total * gain[...] * hat, axis=1, keepdims=True)


def route_back(normed, d_logits, router_t, after, rstd, gain, got):
    rows = whole_spec(256, HALF)
    return pl.pallas_call(
        route_back_kernel,
        grid=(1,),
        in_specs=[
            rows,
            whole_spec(16, 256),
            whole_spec(16, HALF),
            rows,
            whole_spec(256, 1),
            whole_spec(1, HALF),
            rows,
            rows,
            rows,
            rows,
        ],
        out_specs=[whole_spec(16, HALF), rows, whole_spec(1, HALF), whole_spec(256, 1)],
        out_shape=[
            jax.ShapeDtypeStruct((16, HALF), jnp.float32),
            jax.ShapeDtypeStruct((256, HALF), jnp.float32),
            jax.ShapeDtypeStruct((1, HALF), jnp.float32),
            jax.ShapeDtypeStruct((256, 1), jnp.float32),
        ],
        **params(1 << 25, 6 << 20),
    )(normed, d_logits, router_t, after, rstd, gain, *got)


def back_kernel(tokens, rstd, gain, first, second, third, fourth, d_normed, along):
    total = first[...].astype(jnp.float32)
    for part in (second, third, fourth):
        total = total + part[...].astype(jnp.float32)
    total = total * gain[...]
    d_normed[...] = total
    hat = tokens[...].astype(jnp.float32) * rstd[...]
    along[...] = jnp.sum(total * hat, axis=1, keepdims=True)


def back_sums(tokens, rstd, gain, got):
    rows = whole_spec(256, HALF)
    return pl.pallas_call(
        back_kernel,
        grid=(1,),
        in_specs=[rows, whole_spec(256, 1), whole_spec(1, HALF)] + [rows] * 4,
        out_specs=[rows, whole_spec(256, 1)],
        out_shape=[
            jax.ShapeDtypeStruct((256, HALF), jnp.float32),
            jax.ShapeDtypeStruct((256, 1), jnp.float32),
        ],
        **params(1 << 20, 5 << 20),
    )(tokens, rstd, gain, *got)


def out_grad_kernel(attended, d_attn, out, total):
    @pl.when(pl.program_id(0) == 0)
    def _():
        total[...] = jnp.zeros_like(total)

    total[...] += t_dot(attended[...], d_attn[...])

    @pl.when(pl.program_id(0) == 3)
    def _():
        out[...] = total[...].astype(jnp.bfloat16)


def out_grad(attended, d_attn):
    rows = lambda n: pl.BlockSpec((256, n), lambda s: (s, 0))
    return pl.pallas_call(
        out_grad_kernel,
        grid=(4,),
        in_specs=[rows(512), rows(HALF)],
        out_specs=whole_spec(512, HALF),
        out_shape=jax.ShapeDtypeStruct((512, HALF), jnp.bfloat16),
        scratch_shapes=[pltpu.VMEM((512, HALF), jnp.float32)],
        **params(1 << 30, 5 << 20),
    )(attended, d_attn)


def heads_kernel(d_attn, weights, own, par):
    own[...] = dot_t(d_attn[...], weights[pl.ds(0, 256), :])
    par[...] = dot_t(d_attn[...], weights[pl.ds(256, 256), :])


def heads_product(d_attn, weights):
    rows = lambda n: pl.BlockSpec((256, n), lambda s: (s, 0))
    return pl.pallas_call(
        heads_kernel,
        grid=(4,),
        in_specs=[rows(HALF), whole_spec(512, HALF)],
        out_specs=[rows(256), rows(256)],
        out_shape=[jax.ShapeDtypeStruct((1024, 256), jnp.float32)] * 2,
        **params(1 << 30, 5 << 20),
    )(d_attn, weights)


def along_kernel(
    d_q, d_k, q_pre, k_pre, rstd_q, rstd_k, gain_q, gain_k, along, d_gain_q, d_gain_k
):
    @pl.when(pl.program_id(0) == 0)
    def _():
        d_gain_q[...] = jnp.zeros_like(d_gain_q)
        d_gain_k[...] = jnp.zeros_like(d_gain_k)

    ones = jnp.ones((8, 256), jnp.bfloat16)
    sides = ((d_q, q_pre, rstd_q, gain_q, d_gain_q), (d_k, k_pre, rstd_k, gain_k, d_gain_k))
    for k, (grad, pre, scale, gain, d_gain) in enumerate(sides):
        part = grad[...] * (pre[...] * scale[...])
        d_gain[...] += jnp.sum(part, axis=0, keepdims=True)
        part = part * gain[...]
        coarse = part.astype(jnp.bfloat16)
        part = part - coarse.astype(jnp.float32)
        fine = part.astype(jnp.bfloat16)
        along[pl.ds(k * 8, 8), :] = dot_t(ones, coarse) + dot_t(ones, fine)


def along_sums(d_q, d_k, qkv, rstd_q, rstd_k, gain_q, gain_k):
    rows = lambda n, k=0: pl.BlockSpec((256, n), lambda s: (s, k))
    line = whole_spec(1, 256)
    return pl.pallas_call(
        along_kernel,
        grid=(4,),
        in_specs=[rows(256), rows(256), rows(256), rows(256, 1), rows(1), rows(1), line, line],
        out_specs=[pl.BlockSpec((16, 256), lambda s: (0, s)), line, line],
        out_shape=[
            jax.ShapeDtypeStruct((16, 1024), jnp.float32),
            jax.ShapeDtypeStruct((1, 256), jnp.float32),
            jax.ShapeDtypeStruct((1, 256), jnp.float32),
        ],
        **params(1 << 22, 5 << 20),
    )(d_q, d_k, qkv, qkv, rstd_q, rstd_k, gain_q[None], gain_k[None])


def outer_kernel(tokens, rstd, gain, d_qkv, out, total):
    @pl.when(pl.program_id(0) == 0)
    def _():
        total[...] = jnp.zeros_like(total)

    low = d_qkv[...]
    for k in range(4):
        at = pl.ds(k * 512, 512)
        normed = tokens[:, at].astype(jnp.float32) * rstd[...] * gain[:, at]
        total[at, :] += dot(jnp.transpose(normed).astype(jnp.bfloat16), low)

    @pl.when(pl.program_id(0) == 3)
    def _():
        out[...] = total[...].astype(jnp.bfloat16)


def outer(tokens, rstd, gain, d_qkv):
    rows = lambda n: pl.BlockSpec((256, n), lambda s: (s, 0))
    return pl.pallas_call(
        outer_kernel,
        grid=(4,),
        in_specs=[rows(D), rows(1), pl.BlockSpec((1, D), lambda s: (0, 0)), rows(768)],
        out_specs=pl.BlockSpec((D, 768), lambda s: (0, 0)),
        out_shape=jax.ShapeDtypeStruct((D, 768), jnp.bfloat16),
        scratch_shapes=[pltpu.VMEM((D, 768), jnp.float32)],
        compiler_params=pltpu.CompilerParams(vmem_limit_bytes=VMEM_LIMIT),
        cost_estimate=pl.CostEstimate(
            flops=2 * 1024 * D * 768, bytes_accessed=16 << 20, transcendentals=0
        ),
    )(tokens, rstd, gain, d_qkv)


def attend_kernel(
    q_pre, k_pre, v_pre, rstd_q, rstd_k, gain_q, gain_k, cosine, sine,
    attended, q_out, k_out, v_out, total, v_t,
):
    i = pl.program_id(1)

    @pl.when(i == 0)
    def _():
        cos, sin = cosine[...], sine[...]
        q_out[0] = roped(q_pre[...] * rstd_q[...] * gain_q[0], cos, sin).astype(jnp.bfloat16)
        k_out[0] = roped(k_pre[...] * rstd_k[...] * gain_k[0], cos, sin).astype(jnp.bfloat16)
        v_out[0] = v_pre[...].astype(jnp.bfloat16)
        v_t[...] = jnp.transpose(v_pre[...]).astype(jnp.bfloat16)

    query = q_out[0, pl.ds(pl.multiple_of(i * SPAN, SPAN), SPAN), :]
    scores = dot_t(k_out[0], query) * SCALE
    most = jnp.max(scores, axis=0, keepdims=True)
    weights = jnp.exp(scores - most)
    mass = jnp.sum(weights, axis=0, keepdims=True)
    total[0] = most + jnp.log(mass)
    probs = (weights / mass).astype(jnp.bfloat16)
    attended[0] = jnp.transpose(dot(v_t[...], probs)).astype(jnp.bfloat16)


SPAN = 256


def attend(qkv, rstd_q, rstd_k, gain_q, gain_k, cosine, sine):
    column = pl.BlockSpec((1024, 1), lambda h, i: (0, 0))
    gain = pl.BlockSpec((1, 1, 128), lambda h, i: (h, 0, 0))
    table = pl.BlockSpec((1024, 128), lambda h, i: (0, 0))
    head = pl.BlockSpec((1, 1024, 128), lambda h, i: (h, 0, 0))
    head_shape = jax.ShapeDtypeStruct((2, 1024, 128), jnp.bfloat16)
    return pl.pallas_call(
        attend_kernel,
        grid=(2, 1024 // SPAN),
        in_specs=[
            pl.BlockSpec((1024, 128), lambda h, i: (0, h)),
            pl.BlockSpec((1024, 128), lambda h, i: (0, 2 + h)),
            pl.BlockSpec((1024, 128), lambda h, i: (0, 4 + h)),
            column,
            column,
            gain,
            gain,
            table,
            table,
        ],
        out_specs=[
            pl.BlockSpec((1, SPAN, 128), lambda h, i: (i, 0, h)),
            head,
            head,
            head,
            pl.BlockSpec((1, 1, SPAN), lambda h, i: (h, 0, i)),
        ],
        out_shape=[
            jax.ShapeDtypeStruct((1024 // SPAN, SPAN, 256), jnp.bfloat16),
            head_shape,
            head_shape,
            head_shape,
            jax.ShapeDtypeStruct((2, 1, 1024), jnp.float32),
        ],
        scratch_shapes=[pltpu.VMEM((128, 1024), jnp.bfloat16)],
        compiler_params=pltpu.CompilerParams(vmem_limit_bytes=VMEM_LIMIT),
        cost_estimate=pl.CostEstimate(
            flops=2 * 4 * 1024 * 1024 * 128, bytes_accessed=8 << 20, transcendentals=2 << 20
        ),
    )(
        qkv,
        qkv,
        qkv,
        rstd_q,
        rstd_k,
        gain_q.reshape(2, 1, 128),
        gain_k.reshape(2, 1, 128),
        cosine,
        sine,
    )


def attend_back_kernel(
    d_att, q, k, v, total, cosine, sine, d_q, d_k, d_v, k_t, k_acc, v_acc
):
    i = pl.program_id(1)

    @pl.when(i == 0)
    def _():
        k_t[...] = jnp.transpose(k[0].astype(jnp.float32)).astype(jnp.bfloat16)
        k_acc[...] = jnp.zeros_like(k_acc)
        v_acc[...] = jnp.zeros_like(v_acc)

    at = pl.ds(pl.multiple_of(i * SPAN, SPAN), SPAN)
    query = q[0, at, :]
    probs = jnp.exp(dot_t(k[0], query) * SCALE - total[0])
    d_probs = dot_t(v[0], d_att[...])
    spread = jnp.sum(probs * d_probs, axis=0, keepdims=True)
    d_scores = (probs * (d_probs - spread)).astype(jnp.bfloat16)
    v_acc[...] += dot(probs.astype(jnp.bfloat16), d_att[...])
    k_acc[...] += dot(d_scores, query)
    d_query = jnp.transpose(dot(k_t[...], d_scores)) * SCALE
    d_q[...] = roped(d_query, cosine[at, :], -sine[at, :])

    @pl.when(i == pl.num_programs(1) - 1)
    def _():
        d_k[...] = roped(k_acc[...] * SCALE, cosine[...], -sine[...])
        d_v[...] = v_acc[...].reshape(4, 256, 128).astype(jnp.bfloat16)


def attend_back(d_att, q, k, v, total, cosine, sine):
    table = pl.BlockSpec((1024, 128), lambda h, i: (0, 0))
    head = pl.BlockSpec((1, 1024, 128), lambda h, i: (h, 0, 0))
    columns = pl.BlockSpec((1024, 128), lambda h, i: (0, h))
    tile = pl.BlockSpec((SPAN, 128), lambda h, i: (i, h))
    return pl.pallas_call(
        attend_back_kernel,
        grid=(2, 1024 // SPAN),
        in_specs=[
            tile,
            head,
            head,
            head,
            pl.BlockSpec((1, 1, SPAN), lambda h, i: (h, 0, i)),
            table,
            table,
        ],
        out_specs=[tile, columns, pl.BlockSpec((4, 256, 128), lambda h, i: (0, 0, h))],
        out_shape=[
            jax.ShapeDtypeStruct((1024, 256), jnp.float32),
            jax.ShapeDtypeStruct((1024, 256), jnp.float32),
            jax.ShapeDtypeStruct((4, 256, 256), jnp.bfloat16),
        ],
        scratch_shapes=[
            pltpu.VMEM((128, 1024), jnp.bfloat16),
            pltpu.VMEM((1024, 128), jnp.float32),
            pltpu.VMEM((1024, 128), jnp.float32),
        ],
        compiler_params=pltpu.CompilerParams(vmem_limit_bytes=VMEM_LIMIT),
        cost_estimate=pl.CostEstimate(
            flops=2 * 10 * 1024 * 1024 * 128, bytes_accessed=8 << 20, transcendentals=2 << 20
        ),
    )(d_att, q, k, v, total, cosine, sine)


CHUNKS = 2
PART = FF // CHUNKS
WIDE = 3 * PART
VMEM_LIMIT = 58 * 1024 * 1024


def pack_kernel(gate_up, down, out):
    down_t = jnp.transpose(down[0].astype(jnp.float32)).astype(jnp.bfloat16)
    for f in range(CHUNKS):
        out[0, :, pl.ds(f * WIDE, PART)] = gate_up[0, :, pl.ds(f * PART, PART)]
        out[0, :, pl.ds(f * WIDE + PART, PART)] = gate_up[0, :, pl.ds(FF + f * PART, PART)]
        out[0, :, pl.ds(f * WIDE + 2 * PART, PART)] = down_t[:, f * PART : (f + 1) * PART]


def pack_experts(gate_up, down):
    return pl.pallas_call(
        pack_kernel,
        grid=(2,),
        in_specs=[
            pl.BlockSpec((1, 128, 2 * FF), lambda m: (m, 0, 0)),
            pl.BlockSpec((1, FF, 128), lambda m: (m, 0, 0)),
        ],
        out_specs=pl.BlockSpec((1, 128, 3 * FF), lambda m: (m, 0, 0)),
        out_shape=jax.ShapeDtypeStruct((2, 128, 3 * FF), jnp.bfloat16),
        compiler_params=pltpu.CompilerParams(vmem_limit_bytes=VMEM_LIMIT),
        cost_estimate=pl.CostEstimate(flops=0, bytes_accessed=4 << 20, transcendentals=0),
    )(gate_up, down)


def unpack_kernel(first, second, gate_up, down):
    for m, part in enumerate((first, second)):

        @pl.when(pl.program_id(0) == m)
        def _():
            for f in range(CHUNKS):
                at = f * WIDE
                gate_up[0, :, pl.ds(f * PART, PART)] = part[:, pl.ds(at, PART)].astype(jnp.float32)
                up = part[:, pl.ds(at + PART, PART)].astype(jnp.float32)
                gate_up[0, :, pl.ds(FF + f * PART, PART)] = up
                down_t = part[:, pl.ds(at + 2 * PART, PART)].astype(jnp.float32)
                down[0, pl.ds(f * PART, PART), :] = jnp.transpose(down_t)


def unpack_experts(first, second):
    whole = pl.BlockSpec((128, 3 * FF), lambda m: (0, 0))
    return pl.pallas_call(
        unpack_kernel,
        grid=(2,),
        in_specs=[whole, whole],
        out_specs=[
            pl.BlockSpec((1, 128, 2 * FF), lambda m: (m, 0, 0)),
            pl.BlockSpec((1, FF, 128), lambda m: (m, 0, 0)),
        ],
        out_shape=[
            jax.ShapeDtypeStruct((2, 128, 2 * FF), jnp.float32),
            jax.ShapeDtypeStruct((2, FF, 128), jnp.float32),
        ],
        compiler_params=pltpu.CompilerParams(vmem_limit_bytes=VMEM_LIMIT),
        cost_estimate=pl.CostEstimate(flops=0, bytes_accessed=4 << 20, transcendentals=0),
    )(first, second)


def turned(a):
    return jnp.transpose(a.astype(jnp.float32)).astype(jnp.bfloat16)


def open_kernel(
    seat, gate, normed, cot, weights,
    part, rows_t, d_out_t, cot_rows, pick_t, weight, rows, d_out,
):
    @pl.when(pl.program_id(1) == 0)
    def _():
        taken = lax.broadcasted_iota(jnp.int32, (CAP, 1024), 0) == seat[0]
        slot_weight = jnp.sum(jnp.where(taken, gate[0], 0.0), axis=1, keepdims=True)
        weight[0] = slot_weight
        pick = jnp.where(taken, 1.0, 0.0)
        pick_t[0] = turned(pick)
        pick = pick.astype(jnp.bfloat16)
        for at in range(0, HALF, 512):
            spot = pl.ds(at, 512)
            found = dot(pick, normed[:, spot])
            rows[:, spot] = found.astype(jnp.bfloat16)
            rows_t[0, spot, :] = turned(found)
            picked = dot(pick, cot[:, spot])
            cot_rows[0, :, spot] = picked.astype(jnp.bfloat16)
            picked = picked * slot_weight
            d_out[:, spot] = picked.astype(jnp.bfloat16)
            d_out_t[0, spot, :] = turned(picked)

    for k, left in enumerate((rows, rows, d_out)):
        at = pl.ds(k * PART, PART)
        part[0, :, at] = dot(left[...], weights[0, :, at]).astype(jnp.bfloat16)


def open_experts(seat, gate, normed, cot, weights):
    whole = pl.BlockSpec((1024, HALF), lambda h, f: (0, 0))
    line = pl.BlockSpec((1, 1, 1024), lambda h, f: (h, 0, 0))
    slot = pl.BlockSpec((1, CAP, HALF), lambda h, f: (h, 0, 0))
    slot_t = pl.BlockSpec((1, HALF, CAP), lambda h, f: (h, 0, 0))
    shape_t = jax.ShapeDtypeStruct((2, HALF, CAP), jnp.bfloat16)
    return pl.pallas_call(
        open_kernel,
        grid=(2, CHUNKS),
        in_specs=[
            line,
            line,
            whole,
            whole,
            pl.BlockSpec((1, HALF, WIDE), lambda h, f: (h, 0, f)),
        ],
        out_specs=[
            pl.BlockSpec((1, CAP, WIDE), lambda h, f: (h, 0, f)),
            slot_t,
            slot_t,
            slot,
            slot_t,
            pl.BlockSpec((1, CAP, 1), lambda h, f: (h, 0, 0)),
        ],
        out_shape=[
            jax.ShapeDtypeStruct((2, CAP, 3 * FF), jnp.bfloat16),
            shape_t,
            shape_t,
            jax.ShapeDtypeStruct((2, CAP, HALF), jnp.bfloat16),
            shape_t,
            jax.ShapeDtypeStruct((2, CAP, 1), jnp.float32),
        ],
        scratch_shapes=[pltpu.VMEM((CAP, HALF), jnp.bfloat16)] * 2,
        compiler_params=pltpu.CompilerParams(vmem_limit_bytes=VMEM_LIMIT),
        cost_estimate=pl.CostEstimate(
            flops=2 * 2 * CAP * 1024 * 5120, bytes_accessed=30 << 20, transcendentals=0
        ),
    )(seat, gate, normed, cot, weights)


def close_kernel(
    first, seat, own, received, rows_t, d_out_t, cot_rows, pick_t, weight, weights, *refs
):
    if first:
        moe, d_normed, grads, d_token, moe_acc, d_acc, out_acc, row_acc = refs
    else:
        moe_in, d_in, moe, d_normed, grads, d_token, moe_acc, d_acc, out_acc, row_acc = refs
    h, f = pl.program_id(0), pl.program_id(1)

    @pl.when((h == 0) & (f == 0))
    def _():
        if first:
            moe_acc[...] = jnp.zeros_like(moe_acc)
            d_acc[...] = jnp.zeros_like(d_acc)
        else:
            for s in range(4):
                moe_acc[pl.ds(s * 256, 256), :] = moe_in[s].astype(jnp.float32)
                d_acc[pl.ds(s * 256, 256), :] = d_in[s].astype(jnp.float32)

    @pl.when(f == 0)
    def _():
        out_acc[...] = jnp.zeros_like(out_acc)
        row_acc[...] = jnp.zeros_like(row_acc)

    def both(k):
        at = pl.ds(k * PART, PART)
        return own[0, :, at].astype(jnp.float32) + received[0, :, at].astype(jnp.float32)

    gate, up, d_hidden = both(0), both(1), both(2)
    sig = jax.nn.sigmoid(gate)
    scaled = gate * sig
    hidden = (scaled * up).astype(jnp.bfloat16)
    d_gate = (d_hidden * up * sig * (1.0 + gate * (1.0 - sig))).astype(jnp.bfloat16)
    d_up = (d_hidden * scaled).astype(jnp.bfloat16)
    out_acc[...] += dot_t(hidden, weights[0, :, pl.ds(2 * PART, PART)])
    row_acc[...] += dot_t(d_gate, weights[0, :, pl.ds(0, PART)])
    row_acc[...] += dot_t(d_up, weights[0, :, pl.ds(PART, PART)])
    grads[0, :, pl.ds(0, PART)] = dot(rows_t[0], d_gate).astype(jnp.bfloat16)
    grads[0, :, pl.ds(PART, PART)] = dot(rows_t[0], d_up).astype(jnp.bfloat16)
    grads[0, :, pl.ds(2 * PART, PART)] = dot(d_out_t[0], hidden).astype(jnp.bfloat16)

    @pl.when(f == CHUNKS - 1)
    def _():
        d_weight = jnp.sum(out_acc[...] * cot_rows[0].astype(jnp.float32), axis=1, keepdims=True)
        taken = lax.broadcasted_iota(jnp.int32, (CAP, 1024), 0) == seat[0]
        d_token[0] = jnp.sum(jnp.where(taken, d_weight, 0.0), axis=0, keepdims=True)
        weighted = (weight[0] * out_acc[...]).astype(jnp.bfloat16)
        d_rows = row_acc[...].astype(jnp.bfloat16)
        for at in range(0, HALF, 512):
            spot = pl.ds(at, 512)
            moe_acc[:, spot] += dot(pick_t[0], weighted[:, at : at + 512])
            d_acc[:, spot] += dot(pick_t[0], d_rows[:, at : at + 512])

    @pl.when((h == 1) & (f == CHUNKS - 1))
    def _():
        for s in range(4):
            moe[s] = moe_acc[pl.ds(s * 256, 256), :].astype(moe.dtype)
            d_normed[s] = d_acc[pl.ds(s * 256, 256), :].astype(d_normed.dtype)


def close_experts(seat, own, received, state, weights, before):
    whole = pl.BlockSpec((4, 256, HALF), lambda h, f: (0, 0, 0))
    line = pl.BlockSpec((1, 1, 1024), lambda h, f: (h, 0, 0))
    slot = pl.BlockSpec((1, CAP, HALF), lambda h, f: (h, 0, 0))
    slot_t = pl.BlockSpec((1, HALF, CAP), lambda h, f: (h, 0, 0))
    part = pl.BlockSpec((1, CAP, WIDE), lambda h, f: (h, 0, f))
    wide = pl.BlockSpec((1, HALF, WIDE), lambda h, f: (h, 0, f))
    full = jax.ShapeDtypeStruct((4, 256, HALF), jnp.bfloat16)

    def body(*refs):
        close_kernel(not before, *refs)

    return pl.pallas_call(
        body,
        grid=(2, CHUNKS),
        in_specs=[
            line,
            part,
            part,
            slot_t,
            slot_t,
            slot,
            slot_t,
            pl.BlockSpec((1, CAP, 1), lambda h, f: (h, 0, 0)),
            wide,
        ]
        + [whole] * len(before),
        out_specs=[whole, whole, wide, line],
        out_shape=[
            full,
            full,
            jax.ShapeDtypeStruct((2, HALF, 3 * FF), jnp.bfloat16),
            jax.ShapeDtypeStruct((2, 1, 1024), jnp.float32),
        ],
        scratch_shapes=[
            pltpu.VMEM((1024, HALF), jnp.float32),
            pltpu.VMEM((1024, HALF), jnp.float32),
            pltpu.VMEM((CAP, HALF), jnp.float32),
            pltpu.VMEM((CAP, HALF), jnp.float32),
        ],
        compiler_params=pltpu.CompilerParams(vmem_limit_bytes=VMEM_LIMIT),
        cost_estimate=pl.CostEstimate(
            flops=2 * 2 * CAP * 1024 * 8192, bytes_accessed=50 << 20, transcendentals=2 * CAP * FF
        ),
    )(seat, own, received, *state, weights, *before)


def on_device(
    tokens,
    cotangent,
    w_qkv,
    w_out,
    w_router,
    norm_attn,
    norm_moe,
    query_gain,
    key_gain,
    w_gate_up,
    w_down,
    routes,
    block_order,
):
    y, zh, c = lax.axis_index("y"), lax.axis_index("zh"), lax.axis_index("c")
    plane = ("zh", "zl", "x")
    own_first = c == 0

    low, high = split_halves(tokens[0])
    low, high, w_qkv = lax.optimization_barrier((low, high, w_qkv))
    x_blocks = jnp.concatenate(to_half(low, high, zh, c))
    x_blocks, block_order, w_gate_up, cotangent, routes = lax.optimization_barrier(
        (x_blocks, block_order, w_gate_up, cotangent, routes)
    )
    x_own = y_gather(x_blocks)
    x_par = [other_core(part) for part in x_own]
    place = jnp.full((8, 128), block_order[0, 0], jnp.int32).astype(jnp.float32)
    places = y_gather(jnp.stack(to_half(place, place, zh, c)))
    places = jnp.stack(places)[:, :, 0, 0].reshape(8)

    pieces = w_qkv.reshape(16, 3, 8, 256).transpose(2, 0, 1, 3).reshape(8, 16, 768)
    small = jnp.concatenate(
        [norm_attn[:, None], norm_moe[:, None], w_router, query_gain[:, None], key_gain[:, None]],
        axis=1,
    )
    small = jnp.pad(small, ((0, 0), (0, 108)))
    pieces = jnp.concatenate([pieces, jnp.broadcast_to(small, (8, 16, 128))], axis=2)
    pieces = trade(pieces, y, c).reshape(128, 896)
    out_low, out_high = split_halves(w_out)
    out_par = other_core(jnp.where(own_first, out_high, out_low))
    out_own = jnp.where(own_first, out_low, out_high)
    out_both = jnp.where(
        own_first, jnp.concatenate([out_own, out_par]), jnp.concatenate([out_par, out_own])
    )
    out_both = out_both.reshape(32, 4, 256).transpose(1, 0, 2).reshape(128, 256)
    dense = jnp.concatenate([pieces, out_both], axis=1)
    dense, w_gate_up = lax.optimization_barrier((dense, w_gate_up))
    dense = lax.all_gather(dense, plane, axis=0, tiled=True).reshape(2, 2, 4, 4, 2, 16, 1152)

    expert_w = [
        lax.all_gather(part, plane, axis=0, tiled=True).reshape(2, HALF, 3 * FF)
        for part in pack_experts(w_gate_up, w_down)
    ]

    cot_low, cot_high = split_halves(cotangent[0])
    cot_here = jnp.concatenate(to_half(cot_low, cot_high, zh, c))
    cot_sent, x_own = lax.optimization_barrier((cot_here, x_own))
    cot_parts = y_gather(cot_sent)
    route_t = routes[0].T
    route_t = jnp.where(c == zh, route_t, other_core(route_t))
    route_t = by_distance(route_t.reshape(4, 4, 256), y).reshape(4, 1024)

    def rolled(a):
        a = a.transpose(1, 3, 0, 2, 4, 5, 6).reshape(2, HALF, -1)
        return jnp.where(own_first, a, a[::-1])

    qkv_w = rolled(dense[..., :768]).reshape(D, 768)
    small_all = dense[..., 768:788]
    small_rolled = f32(rolled(small_all))
    gain_attn = small_rolled[:, :, 0]
    gain_moe = small_rolled[0, :, 1]
    router_w = bf16(small_rolled[0, :, 2:18])
    small_true = f32(small_all[..., 18:20].transpose(3, 0, 1, 2, 4, 5, 6).reshape(8, 256, 2))
    head_block = y * 2 + c
    mine = lax.dynamic_index_in_dim(small_true, head_block, 0, keepdims=False)
    gain_query, gain_key = mine[:, 0], mine[:, 1]
    out_w = dense.reshape(16, 128, 1152)[:, :, 896:].reshape(16, 4, 32, 256)
    out_w = out_w.transpose(0, 2, 1, 3).reshape(2, 256, HALF)
    out_w = jnp.where(own_first, out_w, out_w[::-1]).reshape(512, HALF)

    qkv, x_all, rstd_one, squares = project(x_own, x_par, gain_attn, qkv_w)
    squares = squares.reshape(2, 8, 1024)[:, 0]
    rstd = lax.rsqrt(ring_sum(squares, y) / D + epsilon)
    rstd_q, rstd_k = rstd[0][:, None], rstd[1][:, None]
    here = places[:, None, None] == jnp.arange(8, dtype=jnp.float32)[None, :, None]
    block_cos, block_sin, row_cos, row_sin = angle_tables()
    block_cos = jnp.sum(jnp.where(here, block_cos, 0.0), axis=1)[:, None]
    block_sin = jnp.sum(jnp.where(here, block_sin, 0.0), axis=1)[:, None]
    cosine = block_cos * row_cos - block_sin * row_sin
    sine = block_sin * row_cos + block_cos * row_sin
    cosine = jnp.concatenate([cosine, cosine], axis=2).reshape(1024, 128)
    sine = jnp.concatenate([-sine, sine], axis=2).reshape(1024, 128)
    qkv, out_w, cosine, sine = lax.optimization_barrier((qkv, out_w, cosine, sine))
    attended, *heads = attend(qkv, rstd_q, rstd_k, gain_query, gain_key, cosine, sine)
    attended, cot_parts = lax.optimization_barrier(
        (attended.reshape(1024, 256), cot_parts)
    )
    cot_all = jnp.concatenate(cot_parts)
    attended = jnp.concatenate([attended, other_core(attended)], axis=1)
    out_parts, out_here = output_product(attended, out_w)
    got = [from_chip(out_parts[step], 4 - step) for step in (1, 2, 3)]
    x_here = f32(x_all[:256, :HALF])
    after, square = residual(x_all, out_here, got)

    square = square.reshape(256)
    rstd_two = lax.rsqrt((square + other_core(square)) / D + epsilon)[:, None]
    after_hat = after * rstd_two
    normed_two = bf16(after_hat * gain_moe)
    normed_all = jnp.concatenate(y_gather(normed_two))
    router_t = router_w.T
    logits = logits_of(router_t, normed_all)
    logits = logits + other_core(logits)
    picked = route_t[:, None, :] == jnp.arange(16, dtype=jnp.int32)[None, :, None]
    routed = jnp.sum(jnp.where(picked, logits[None], 0.0), axis=1)
    routed = jnp.exp(routed - jnp.max(routed, axis=0, keepdims=True))
    gates = routed / (routed[0] + routed[1] + routed[2] + routed[3])

    before, d_gates, expert_grads = (), jnp.zeros((4, 1024), jnp.float32), []
    for m in range(2):
        chosen = route_t[None] == y * 4 + jnp.arange(2, dtype=jnp.int32)[:, None, None] * 2 + m
        hit = jnp.sum(chosen.astype(jnp.int32), axis=1)
        rank = jnp.cumsum(hit, axis=1) - hit
        seat = jnp.where(hit > 0, rank, CAP)[:, None]
        gate_token = jnp.sum(jnp.where(chosen, gates[None], 0.0), axis=1)[:, None]
        seat, before = lax.optimization_barrier((seat, before))
        part, *state = open_experts(seat, gate_token, normed_all, cot_all, expert_w[m])
        moe_sum, d_normed, grads, d_token = close_experts(
            seat, part, other_core(part), state, expert_w[m], before
        )
        before = (moe_sum, d_normed)
        d_gates = d_gates + jnp.sum(jnp.where(chosen, d_token, 0.0), axis=0)
        expert_grads.append(
            lax.psum_scatter(grads.reshape(D, 3 * FF), plane, scatter_dimension=0, tiled=True)
        )

    def ring_scatter(a):
        a = a.reshape(4, 256, HALF)
        return sum(f32(g) for g in y_scatter([a[s] for s in range(4)]))

    d_got = y_scatter([d_normed[step] for step in range(4)])
    d_gates = d_gates.reshape(4, 4, 256)
    d_gates = sum(y_scatter([d_gates[:, s] for s in range(4)]))
    d_gates = d_gates + other_core(d_gates)

    gates_here, picked_here = gates[:, :256], picked[:, :, :256]
    shared = gates_here * d_gates
    shared = shared[0] + shared[1] + shared[2] + shared[3]
    d_routed = gates_here * (d_gates - shared)
    d_logits = jnp.sum(jnp.where(picked_here, d_routed[:, None, :], 0.0), axis=0)
    grad_router, d_normed_here, grad_norm_moe, along = route_back(
        normed_two, d_logits, router_t, after, rstd_two, gain_moe[None], d_got
    )
    grad_router, grad_norm_moe = grad_router.T, grad_norm_moe.reshape(HALF)
    d_scaled = d_normed_here * gain_moe
    along = along.reshape(256)
    along = (along + other_core(along))[:, None] / D
    d_after = f32(cot_here) + rstd_two * (d_scaled - after_hat * along)

    d_attn = jnp.concatenate(y_gather(bf16(d_after)))
    moe_sum, d_attn = lax.optimization_barrier((moe_sum, d_attn))
    moe_here = ring_scatter(moe_sum)
    d_att, d_other = heads_product(d_attn, out_w)
    d_att = bf16(d_att + other_core(d_other))
    d_att, expert_grads[0] = lax.optimization_barrier((d_att, expert_grads[0]))
    d_query, d_key, d_value = attend_back(d_att, *heads, cosine, sine)
    d_query, d_attn = lax.optimization_barrier((d_query, d_attn))
    grad_out = out_grad(attended, d_attn)
    along, grad_query_gain, grad_key_gain = along_sums(
        d_query, d_key, qkv, rstd_q, rstd_k, gain_query, gain_key
    )
    grad_query_gain, grad_key_gain = grad_query_gain.reshape(256), grad_key_gain.reshape(256)
    along = ring_sum(along.reshape(2, 8, 1024)[:, 0], y)[:, :, None] / D
    along, moe_here = lax.optimization_barrier((along, moe_here))
    d_qkv, d_par, d_own, grad_norm_attn = spread(
        d_query, d_key, d_value, qkv, rstd_q, rstd_k, along[0], along[1],
        gain_query, gain_key, x_all, rstd_one, qkv_w,
    )
    grad_norm_attn = grad_norm_attn.reshape(D)
    received = other_core(d_par)
    received, d_qkv, expert_grads[1] = lax.optimization_barrier(
        (received, d_qkv, expert_grads[1])
    )
    d_sent = bf16(d_own + f32(received))
    grad_qkv = outer(x_all, rstd_one, gain_attn.reshape(1, D), d_qkv)
    wide = jnp.concatenate([grad_norm_moe[:, None], grad_router], axis=1)
    wide = jnp.pad(wide, ((0, HALF), (0, 0)))
    extras = jnp.concatenate([grad_norm_attn[:, None], wide], axis=1).reshape(2, HALF, 18)
    extras = jnp.where(own_first, extras, extras[::-1]).reshape(2, 4, 2, 4, 2, 16, 18)
    gains = jnp.stack([grad_query_gain, grad_key_gain], axis=1)
    at_home = jnp.arange(8)[:, None, None] == head_block
    gains = jnp.where(at_home, gains[None], 0.0).reshape(4, 2, 2, 4, 2, 16, 2)
    extras = jnp.concatenate(
        [extras.transpose(2, 0, 3, 1, 4, 5, 6), gains.transpose(1, 2, 3, 0, 4, 5, 6)], axis=-1
    )
    coarse = bf16(extras)
    extras = jnp.concatenate([coarse, bf16(extras - f32(coarse))], axis=-1)
    extras = jnp.pad(extras, ((0, 0),) * 6 + ((0, 88),))
    both = grad_qkv.reshape(2, HALF, 768)
    both = jnp.where(own_first, both, both[::-1]).reshape(2, 4, 2, 4, 2, 16, 768)
    both = both.transpose(2, 0, 3, 1, 4, 5, 6)
    both = jnp.concatenate([both, extras], axis=-1).reshape(16, 128, 896)
    grad_out = grad_out.reshape(2, 256, HALF)
    grad_out = jnp.where(own_first, grad_out, grad_out[::-1]).reshape(16, 32, 4, 256)
    grad_out = grad_out.transpose(0, 2, 1, 3).reshape(16, 128, 256)
    both = jnp.concatenate([both, grad_out], axis=2).reshape(D, 1152)
    both, got = plane_and_ring_sum(
        both.reshape(4, 4, 128, 1152),
        [d_sent[s * 256 : s * 256 + 256] for s in range(4)],
        zh * 2 + lax.axis_index("zl"),
        lax.axis_index("x"),
    )
    got, moe_here = lax.optimization_barrier((got, moe_here))
    layer_output = from_half(bf16(after + moe_here), zh, c)[None]
    hat_here = x_here * rstd_one[:256]
    d_normed_one, along = back_sums(x_all, rstd_one, gain_attn[:1], got)
    along = along.reshape(256)
    along = (along + other_core(along))[:, None] / D
    grad_tokens = bf16(d_after + rstd_one[:256] * (d_normed_one - hat_here * along))

    grad_out = both[:, 896:].reshape(4, 32, 256).transpose(1, 0, 2).reshape(32, HALF)
    both = f32(trade(both[:, :896].reshape(8, 16, 896), y, c))
    grad_w_qkv = both[:, :, :768].reshape(8, 16, 3, 256).transpose(1, 2, 0, 3).reshape(16, 3 * D)
    smalls = jnp.sum(both[:, :, 768:788] + both[:, :, 788:808], axis=0)

    out_own = jnp.where(own_first, grad_out[:16], grad_out[16:])
    out_par = other_core(jnp.where(own_first, grad_out[16:], grad_out[:16]))
    grad_w_out = jnp.where(own_first, join_halves(out_own, out_par), join_halves(out_par, out_own))
    grad_w_out = f32(grad_w_out)

    grad_gate_up, grad_down = unpack_experts(*expert_grads)
    return (
        layer_output,
        from_half(grad_tokens, zh, c)[None],
        grad_w_qkv,
        grad_w_out,
        smalls[:, 2:18],
        smalls[:, 0],
        smalls[:, 1],
        smalls[:, 18],
        smalls[:, 19],
        grad_gate_up,
        grad_down,
    )


def solution(mesh):
    fine = Mesh(mesh.devices.reshape(4, 2, 2, 4, 2), ("y", "zh", "zl", "x", "c"))
    ctx, fsdp = ("y", "zh"), ("zl", "x", "c")
    rows, blocks, line = P(ctx + fsdp, None), P(fsdp, ctx, None), P(ctx + fsdp)
    gate_up, down = P(ctx, fsdp, None), P(ctx, None, fsdp)
    return jax.shard_map(
        on_device,
        mesh=fine,
        in_specs=(blocks, blocks, rows, rows, rows, line, line, line, line, gate_up, down)
        + (P(fsdp, None, None), P(fsdp, ctx)),
        out_specs=(blocks, blocks, rows, rows, rows, line, line, line, line, gate_up, down),
        check_vma=False,
    )
```
